32 devices in a mesh: dp: 16 (over z, y, x), mp: 2 (over core).
Axes of the slice: x: 2, y: 2, z: 4, core: 2. Of those that a mesh axis runs over, the one named last changes fastest.
Arguments:
- features: bfloat16 [8, 512, 512], P(None, 'dp'), may hold values from -6 to 6
- token_ids: int32 [8, 512], P(None, 'dp'), may hold values from 0 to 80
- mel_target: bfloat16 [8, 512, 80], P(None, 'dp'), may hold values from -6 to 6
- token_target: int32 [8, 512], P(None, 'dp'), may hold values from 0 to 80
- segments: int32 [16, 512], replicated, may hold values from 0 to 511, as said below
- row_device: int32 [16], replicated, may hold values from 0 to 15, as said below
- offset_bucket: int32 [1023], replicated, may hold values from 0 to 319
- speech_weight: bfloat16 [512, 768], replicated, may hold values from -0.25 to 0.25
- speech_bias: float32 [768], replicated, may hold values from -3 to 3
- token_table: bfloat16 [81, 768], replicated, may hold values from -6 to 6
- first_gain: float32 [768], replicated, may hold values from 0.1 to 1.9
- first_shift: float32 [768], replicated, may hold values from -3 to 3
- query_weight: bfloat16 [768, 768], P(None, 'mp'), may hold values from -0.21875 to 0.21875
- key_weight: bfloat16 [768, 768], P(None, 'mp'), may hold values from -0.21875 to 0.21875
- value_weight: bfloat16 [768, 768], P(None, 'mp'), may hold values from -0.21875 to 0.21875
- bias_table: float32 [320, 12], P(None, 'mp'), may hold values from -4 to 4
- out_weight: bfloat16 [768, 768], P('mp'), may hold values from -0.875 to 0.875
- second_gain: float32 [768], replicated, may hold values from 0.1 to 1.9
- second_shift: float32 [768], replicated, may hold values from -3 to 3
- up_weight: bfloat16 [768, 3072], P(None, 'mp'), may hold values from -0.21875 to 0.21875
- up_bias: float32 [3072], P('mp'), may hold values from -3 to 3
- down_weight: bfloat16 [3072, 768], P('mp'), may hold values from -0.109375 to 0.109375
- down_bias: float32 [768], replicated, may hold values from -3 to 3
- mel_weight: bfloat16 [768, 80], replicated, may hold values from -0.21875 to 0.21875
- mel_bias: float32 [80], replicated, may hold values from -3 to 3
- vocab_weight: bfloat16 [768, 81], replicated, may hold values from -0.4375 to 0.4375
- vocab_bias: float32 [81], replicated, may hold values from -4 to 4
Outputs:
- mean_loss: float32 [], replicated
- feature_grad: bfloat16 [8, 512, 512], P(None, 'dp')
- speech_weight_grad: float32 [512, 768], replicated
- speech_bias_grad: float32 [768], replicated
- token_table_grad: float32 [81, 768], replicated
- first_gain_grad: float32 [768], replicated
- first_shift_grad: float32 [768], replicated
- query_weight_grad: float32 [768, 768], P(None, 'mp')
- key_weight_grad: float32 [768, 768], P(None, 'mp')
- value_weight_grad: float32 [768, 768], P(None, 'mp')
- bias_table_grad: float32 [320, 12], P(None, 'mp')
- out_weight_grad: float32 [768, 768], P('mp')
- second_gain_grad: float32 [768], replicated
- second_shift_grad: float32 [768], replicated
- up_weight_grad: float32 [768, 3072], P(None, 'mp')
- up_bias_grad: float32 [3072], P('mp')
- down_weight_grad: float32 [3072, 768], P('mp')
- down_bias_grad: float32 [768], replicated
- mel_weight_grad: float32 [768, 80], replicated
- mel_bias_grad: float32 [80], replicated
- vocab_weight_grad: float32 [768, 81], replicated
- vocab_bias_grad: float32 [81], replicated
The draws below stay inside these ranges and needn't reach their ends.
Inputs may be any that keep to these rules, and one draw needn't show every extreme that they name: `segments`: along each row the ids start at 0 and never fall; a position attends to the positions of its row with its id. In every draw one speech row and one text row, chosen from the seed, hold one id over all 512 positions, and one other speech row starts a new id at every position. row_device[r] is the backbone index of row r. Rows below 8 are speech rows and go to indices below 8; text rows go to the others. No index receives more than 2 rows; in every draw some receive exactly 2 and some none.
All inputs are finite; a program needn't handle non-finite values.
Results may differ from the reference program's by a relative error of at most 0.015.
The reference program's roundings to bfloat16 on the way count: a program that leaves them out, or rounds other values in their place, can miss the bound.
Values may be sent and summed in bfloat16 or wider, within the bound.
No kernel may reach another device: no remote copies, remote signals or barrier semaphores. Data moves between devices by JAX's collectives and lax.ppermute only.
A program may use at most 192 MiB of HBM per device.

```python
import math
import jax
import jax.numpy as jnp
import numpy as np
from jax import lax

D = 768
H = 12
HD = 64
FF = 3072
FEAT = 512
MEL = 80
VOCAB = 81
NB = 320
LEN = 512
ROWS_DEV = 1
ROWS_S = 8
ROWS_T = 8
ROWS = 16


def draw_segments(key, part):
    key = jax.random.fold_in(key, 11)
    starts = jax.random.randint(jax.random.fold_in(key, 1), (ROWS, LEN), 0, LEN // 4) == 0
    columns = jnp.arange(LEN)
    whole_speech = jax.random.randint(jax.random.fold_in(key, 2), (), 0, ROWS_S)
    whole_text = ROWS_S + jax.random.randint(jax.random.fold_in(key, 3), (), 0, ROWS_T)
    every_row = (whole_speech + 1) % ROWS_S
    row_order = jnp.arange(ROWS)
    kept_rows = (row_order != whole_speech) & (row_order != whole_text)
    starts = (starts | (row_order == every_row)[:, None]) & kept_rows[:, None] & (columns[None, :] > 0)
    return jnp.cumsum(starts.astype(jnp.int32), axis=1).astype(jnp.int32)


def draw_row_device(key, part):
    key = jax.random.fold_in(key, 23)
    half_devices = ROWS_S // ROWS_DEV
    pattern = jnp.tile(jnp.array([2, 1, 0, 1], jnp.int32), half_devices // 4) * ROWS_DEV
    halves = []
    for modality in range(2):
        device_loads = pattern[jax.random.permutation(jax.random.fold_in(key, 2 * modality), half_devices)]
        first_loaded = jnp.argmax(device_loads > 0).astype(jnp.int32)
        device_loads = jnp.roll(device_loads, modality * (half_devices - 1) - first_loaded)
        load_ends = jnp.cumsum(device_loads)
        places = jnp.arange(ROWS_S)
        owners = jnp.sum((load_ends[None, :] <= places[:, None]).astype(jnp.int32), axis=1)
        shuffled = jax.random.permutation(jax.random.fold_in(key, 2 * modality + 1), ROWS_S)
        halves.append(owners[shuffled] + modality * half_devices)
    return jnp.concatenate(halves).astype(jnp.int32)


def plant(values, own_key, low, top_value):
    longest = values.shape.index(max(values.shape))
    spots = []
    for shift in (0, 1):
        where = [jax.random.randint(jax.random.fold_in(own_key, axis), (), 0, length) for axis, length in enumerate(values.shape)]
        where[longest] = (where[longest] + shift) % values.shape[longest]
        spots.append(tuple(where))
    return values.at[spots[0]].set(low).at[spots[1]].set(top_value)


def shard_levels(stream_key, dims, shards, low, high):
    gain = 1.0
    for dim, blocks in shards:
        heights = jax.random.uniform(jax.random.fold_in(jax.random.fold_in(stream_key, 6), dim), (blocks,), jnp.float32, low / len(shards), high / len(shards))
        gain = gain * jnp.repeat(jnp.exp(heights), dims[dim] // blocks).reshape((-1,) + (1,) * (len(dims) - 1 - dim))
    return gain


def cumulative_ranks(number_of, slope):
    weights = [(1 << 20) // math.isqrt(rank ** slope) + 1 for rank in range(1, number_of + 1)]
    width = 1 + sum(weights) // (1 << 30)
    return np.cumsum(np.array([max(1, weight // width) for weight in weights]))


def skewed_ids(own_key, dims, number_of, skew):
    table = cumulative_ranks(number_of, skew)
    pick = jax.random.randint(jax.random.fold_in(own_key, 1), dims, 0, int(table[number_of - 1]))
    grade = jnp.searchsorted(jnp.asarray(table, jnp.int32), pick, side="right")
    return jax.random.permutation(jax.random.fold_in(own_key, 2), number_of)[grade].astype(jnp.int32)


def noise(rng, extent, width, reach, split=(), held_as=jnp.bfloat16):
    result = jax.random.normal(rng, extent, jnp.float32) * width
    if len(split) > 0:
        result = shard_levels(rng, extent, split, -0.22, 0.18) * result
    return jnp.clip(result, min=-reach, max=reach).astype(held_as)


def setup_inputs(seed: int = 0) -> dict:
    splits = jax.random.split(jax.random.key(seed), 28)
    features = noise(splits[0], (ROWS_S, LEN, FEAT), 1.0, 6.0, ((1, 16),))
    token_ids = plant(skewed_ids(splits[1], (ROWS_T, LEN), VOCAB, 2), jax.random.fold_in(splits[1], 3), 0, VOCAB - 1).astype(jnp.int32)
    mel_target = noise(splits[2], (ROWS_S, LEN, MEL), 1.0, 6.0, ((1, 16),))
    token_target = plant(jax.random.randint(splits[3], (ROWS_T, LEN), 0, VOCAB), jax.random.fold_in(splits[3], 1), 0, VOCAB - 1).astype(jnp.int32)
    segments = draw_segments(jax.random.fold_in(splits[27], 71), 0)
    row_device = draw_row_device(jax.random.fold_in(splits[27], 71), 0)
    offset_bucket = plant(jax.random.randint(splits[6], (2 * LEN - 1,), 0, NB), jax.random.fold_in(splits[6], 1), 0, NB - 1).astype(jnp.int32)
    speech_weight = noise(splits[7], (FEAT, D), FEAT ** -0.5, 0.25)
    speech_bias = noise(splits[8], (D,), 0.5, 3.0, (), jnp.float32)
    token_table = noise(splits[9], (VOCAB, D), 1.0, 6.0)
    first_gain = jnp.clip(1.0 + 0.18 * jax.random.normal(splits[10], (D,), jnp.float32), 0.1, 1.9)
    first_shift = noise(splits[11], (D,), 0.5, 3.0, (), jnp.float32)
    query_weight = noise(splits[12], (D, D), D ** -0.5, 0.21875, ((1, 2),))
    key_weight = noise(splits[13], (D, D), D ** -0.5, 0.21875, ((1, 2),))
    value_weight = noise(splits[14], (D, D), D ** -0.5, 0.21875, ((1, 2),))
    bias_table = noise(splits[15], (NB, H), 1.0, 4.0, ((1, 2),), jnp.float32)
    out_weight = noise(splits[16], (D, D), (D // 16) ** -0.5, 0.875, ((0, 2),))
    second_gain = jnp.clip(1.0 + 0.18 * jax.random.normal(splits[17], (D,), jnp.float32), 0.1, 1.9)
    second_shift = noise(splits[18], (D,), 0.5, 3.0, (), jnp.float32)
    up_weight = noise(splits[19], (D, FF), D ** -0.5, 0.21875, ((1, 2),))
    up_bias = noise(splits[20], (FF,), 0.5, 3.0, ((0, 2),), jnp.float32)
    down_weight = noise(splits[21], (FF, D), FF ** -0.5, 0.109375, ((0, 2),))
    down_bias = noise(splits[22], (D,), 0.5, 3.0, (), jnp.float32)
    mel_weight = noise(splits[23], (D, MEL), D ** -0.5, 0.21875)
    mel_bias = noise(splits[24], (MEL,), 0.5, 3.0, (), jnp.float32)
    vocab_weight = noise(splits[25], (D, VOCAB), (D // 4) ** -0.5, 0.4375)
    vocab_bias = noise(splits[26], (VOCAB,), 1.0, 4.0, (), jnp.float32)
    return {"features": features, "token_ids": token_ids, "mel_target": mel_target, "token_target": token_target, "segments": segments, "row_device": row_device, "offset_bucket": offset_bucket, "speech_weight": speech_weight, "speech_bias": speech_bias, "token_table": token_table, "first_gain": first_gain, "first_shift": first_shift, "query_weight": query_weight, "key_weight": key_weight, "value_weight": value_weight, "bias_table": bias_table, "out_weight": out_weight, "second_gain": second_gain, "second_shift": second_shift, "up_weight": up_weight, "up_bias": up_bias, "down_weight": down_weight, "down_bias": down_bias, "mel_weight": mel_weight, "mel_bias": mel_bias, "vocab_weight": vocab_weight, "vocab_bias": vocab_bias}


@jax.custom_vjp
def low(v):
    return lax.optimization_barrier(v.astype(jnp.bfloat16)).astype(jnp.float32)

@jax.custom_vjp
def low_back(v):
    return v

def low_keep(v):
    return (low(v), None)

def low_pass(kept, grad):
    return (grad,)

def back_keep(v):
    return (v, None)

def back_low(kept, grad):
    return (low(grad),)
low.defvjp(low_keep, low_pass)
low_back.defvjp(back_keep, back_low)
EPSILON = 1e-05
NEGATIVE = -1e+30
HIGHEST = lax.Precision.HIGHEST

def norm_rows(row_data, norm_gain, norm_shift):
    center = row_data - lax.optimization_barrier(jnp.mean(row_data, axis=-1, keepdims=True))
    spread = lax.optimization_barrier(jnp.mean(center * center, axis=-1, keepdims=True))
    return center * lax.rsqrt(spread + EPSILON) * norm_gain + norm_shift

def total_loss(features, speech_weight, speech_bias, token_table, first_gain, first_shift, query_weight, key_weight, value_weight, bias_table, out_weight, second_gain, second_shift, up_weight, up_bias, down_weight, down_bias, mel_weight, mel_bias, vocab_weight, vocab_bias, token_ids, mel_target, token_target, segments, offset_bucket):
    speech_rows = jnp.einsum('rlf,fd->rld', features, speech_weight, precision=HIGHEST) + speech_bias
    text_rows = jnp.take(token_table, token_ids, axis=0)
    embedded = low_back(low(jnp.concatenate([speech_rows, text_rows], axis=0)))
    places = jnp.arange(LEN, dtype=jnp.int32)
    pair_bucket = offset_bucket[places[:, None] - places[None, :] + LEN - 1]
    pair_bias = jnp.transpose(jnp.take(bias_table, pair_bucket, axis=0), (2, 0, 1))
    group_rows = math.gcd(ROWS, 8)
    scaling = HD ** (-0.5)

    def encoder_layer(packed):
        row_block, row_segments = packed
        heads_shape = (group_rows, LEN, H, HD)
        normed = low(norm_rows(row_block, first_gain, first_shift))
        queries = low_back(low(jnp.einsum('gld,de->gle', normed, query_weight, precision=HIGHEST))).reshape(heads_shape)
        key_rows = low_back(low(jnp.einsum('gld,de->gle', normed, key_weight, precision=HIGHEST))).reshape(heads_shape)
        value_rows = low_back(low(jnp.einsum('gld,de->gle', normed, value_weight, precision=HIGHEST))).reshape(heads_shape)
        raw_scores = low_back(jnp.einsum('gqhd,gkhd->ghqk', queries, key_rows, precision=HIGHEST) * scaling)
        same_segment = row_segments[:, :, None] == row_segments[:, None, :]
        scores = jnp.where(same_segment[:, None], raw_scores + pair_bias[None], NEGATIVE)
        weights = low(jax.nn.softmax(scores, axis=-1))
        heads_out = low_back(low(jnp.einsum('ghqk,gkhd->gqhd', weights, value_rows, precision=HIGHEST))).reshape(group_rows, LEN, D)
        mixed_rows = row_block + low_back(jnp.einsum('gle,ed->gld', heads_out, out_weight, precision=HIGHEST))
        normed_two = low(norm_rows(mixed_rows, second_gain, second_shift))
        hidden = low_back(jnp.einsum('gld,df->glf', normed_two, up_weight, precision=HIGHEST) + up_bias)
        active = low(jax.nn.gelu(hidden, approximate=True))
        return mixed_rows + jnp.einsum('glf,fd->gld', active, down_weight, precision=HIGHEST) + down_bias
    stacked = (embedded.reshape(ROWS // group_rows, group_rows, LEN, D), segments.reshape(ROWS // group_rows, group_rows, LEN))
    final_rows = low_back(low(lax.map(jax.checkpoint(encoder_layer), stacked).reshape(ROWS, LEN, D)))
    speech_final = final_rows[:ROWS_S]
    text_final = final_rows[ROWS_S:]
    predicted = low_back(jnp.einsum('rld,dm->rlm', speech_final, mel_weight, precision=HIGHEST) + mel_bias)
    mel_error = predicted - mel_target
    mel_part = jnp.sum(jnp.sqrt(mel_error * mel_error + 1.0) - 1.0) / (MEL * LEN)
    logits = low_back(jnp.einsum('rld,dv->rlv', text_final, vocab_weight, precision=HIGHEST) + vocab_bias)
    picked = lax.optimization_barrier(jnp.sum(logits * jax.nn.one_hot(token_target, VOCAB, dtype=logits.dtype), axis=-1))
    text_part = jnp.sum(jax.nn.logsumexp(logits, axis=-1) - picked) / LEN
    return mel_part + text_part

def reference(features, token_ids, mel_target, token_target, segments, row_device, offset_bucket, speech_weight, speech_bias, token_table, first_gain, first_shift, query_weight, key_weight, value_weight, bias_table, out_weight, second_gain, second_shift, up_weight, up_bias, down_weight, down_bias, mel_weight, mel_bias, vocab_weight, vocab_bias):
    floats = tuple((array_in.astype(jnp.float32) for array_in in (features, speech_weight, speech_bias, token_table, first_gain, first_shift, query_weight, key_weight, value_weight, bias_table, out_weight, second_gain, second_shift, up_weight, up_bias, down_weight, down_bias, mel_weight, mel_bias, vocab_weight, vocab_bias)))
    target_float = mel_target.astype(jnp.float32)

    def loss_of(*params):
        return total_loss(*params, token_ids, target_float, token_target, segments, offset_bucket)
    summed, pullback = jax.vjp(loss_of, *floats)
    gradients = pullback(jnp.ones_like(summed))
    return (summed / ROWS, gradients[0].astype(jnp.bfloat16), gradients[1], gradients[2], gradients[3], gradients[4], gradients[5], gradients[6], gradients[7], gradients[8], gradients[9], gradients[10], gradients[11], gradients[12], gradients[13], gradients[14], gradients[15], gradients[16], gradients[17], gradients[18], gradients[19], gradients[20])
```

```python
import jax
import jax.numpy as jnp
from jax import lax
from jax.experimental import pallas as pl
from jax.experimental.pallas import tpu as pltpu
from jax.sharding import PartitionSpec as P

EPSILON = 1e-05
NEGATIVE = -1e30
HIGHEST = lax.Precision.HIGHEST
BF16 = jnp.bfloat16
F32 = jnp.float32
LANES = 128


def contract_rows(left_side, right_side):
    return lax.dot_general(
        left_side, right_side, (((0,), (0,)), ((), ())), preferred_element_type=F32
    )


def times_transposed(left_side, right_side):
    return lax.dot_general(
        left_side, right_side, (((1,), (1,)), ((), ())), preferred_element_type=F32
    )


def matmul(left_side, right_side):
    return jnp.dot(left_side, right_side, preferred_element_type=F32)


def layer_norm(row_data, norm_gain, norm_shift):
    center = row_data - jnp.mean(row_data, axis=-1, keepdims=True)
    inverse = lax.rsqrt(jnp.mean(center * center, axis=-1, keepdims=True) + EPSILON)
    normal = center * inverse
    return (normal * norm_gain + norm_shift, normal, inverse)


def norm_back(grad_out, normal, inverse, norm_gain):
    scaled = grad_out * norm_gain
    grad_rows = inverse * (
        scaled
        - jnp.mean(scaled, axis=-1, keepdims=True)
        - normal * jnp.mean(scaled * normal, axis=-1, keepdims=True)
    )
    return (grad_rows, jnp.sum(grad_out * normal, axis=0), jnp.sum(grad_out, axis=0))


def smooth_gelu(hidden):
    return jax.nn.gelu(hidden, approximate=True)


def window_kernel(offsets_ref, window_ref):
    heads, width = offsets_ref.shape
    for head in range(heads):
        spread = jnp.broadcast_to(offsets_ref[head : head + 1, :], (LANES, width))
        window_ref[head] = pltpu.roll(spread, width - LANES + 1, 1, stride=1, stride_axis=0)


def bias_window(offsets):
    heads, width = offsets.shape
    return pl.pallas_call(
        window_kernel,
        out_shape=jax.ShapeDtypeStruct((heads, LANES, width), F32),
        name="bias_window",
    )(offsets)


def block_probs(queries, keys, window_ref, slot, block, blocks, segment_column, segment_row):
    length = keys.shape[0]
    start = LANES * (blocks - 1 - block)
    scores = times_transposed(queries, keys) + window_ref[slot, :, start : start + length]
    scores = jnp.where(segment_column == segment_row, scores, NEGATIVE)
    powers = jnp.exp(scores - jnp.max(scores, axis=-1, keepdims=True))
    return powers * (1.0 / jnp.sum(powers, axis=-1, keepdims=True))


def attend_kernel(
    head_size, queries_ref, keys_ref, values_ref, column_ref, row_ref, window_ref, heads_ref
):
    length = queries_ref.shape[0]
    blocks = length // LANES
    scaling = head_size ** (-0.5)
    for slot in range(queries_ref.shape[1] // head_size):
        columns = slice(slot * head_size, (slot + 1) * head_size)
        keys = keys_ref[:, columns]
        values = values_ref[:, columns]
        for block in range(blocks):
            rows = slice(block * LANES, (block + 1) * LANES)
            queries = queries_ref[rows, columns] * jnp.asarray(scaling, BF16)
            probs = block_probs(
                queries, keys, window_ref, slot, block, blocks, column_ref[rows, :], row_ref[...]
            )
            heads_ref[rows, columns] = matmul(probs.astype(BF16), values).astype(BF16)


def attend(queries, keys, values, segment_column, segment_row, window, head_size):
    length, width = queries.shape
    per_step = LANES // head_size
    flat = pl.BlockSpec((length, LANES), lambda step: (0, step))
    return pl.pallas_call(
        lambda *refs: attend_kernel(head_size, *refs),
        grid=(width // LANES,),
        in_specs=[
            flat,
            flat,
            flat,
            pl.BlockSpec((length, 1), lambda step: (0, 0)),
            pl.BlockSpec((1, length), lambda step: (0, 0)),
            pl.BlockSpec((per_step, LANES, 2 * length), lambda step: (step, 0, 0)),
        ],
        out_specs=flat,
        out_shape=jax.ShapeDtypeStruct((length, width), BF16),
        name="attend",
    )(queries, keys, values, segment_column, segment_row, window)


def attend_back_kernel(
    head_size,
    queries_ref,
    keys_ref,
    values_ref,
    grads_ref,
    column_ref,
    row_ref,
    window_ref,
    grad_queries_ref,
    grad_keys_ref,
    grad_values_ref,
    grad_offsets_ref,
    probs_ref,
    scores_ref,
    window_sum_ref,
):
    length = queries_ref.shape[0]
    blocks = length // LANES
    scaling = head_size ** (-0.5)
    for slot in range(queries_ref.shape[1] // head_size):
        columns = slice(slot * head_size, (slot + 1) * head_size)
        keys = keys_ref[:, columns]
        values = values_ref[:, columns]
        window_sum_ref[...] = jnp.zeros_like(window_sum_ref)
        for block in range(blocks):
            rows = slice(block * LANES, (block + 1) * LANES)
            queries = queries_ref[rows, columns] * jnp.asarray(scaling, BF16)
            probs = block_probs(
                queries, keys, window_ref, slot, block, blocks, column_ref[rows, :], row_ref[...]
            )
            grad_probs = times_transposed(grads_ref[rows, columns], values)
            grad_scores = probs * (
                grad_probs - jnp.sum(probs * grad_probs, axis=-1, keepdims=True)
            )
            probs_ref[rows, :] = probs.astype(BF16)
            scores_ref[rows, :] = grad_scores.astype(BF16)
            start = LANES * (blocks - 1 - block)
            window_sum_ref[:, start : start + length] += grad_scores
        grad_queries_ref[:, columns] = (matmul(scores_ref[...], keys) * scaling).astype(BF16)
        grad_keys_ref[:, columns] = (
            contract_rows(scores_ref[...], queries_ref[:, columns]) * scaling
        ).astype(BF16)
        grad_values_ref[:, columns] = contract_rows(probs_ref[...], grads_ref[:, columns]).astype(
            BF16
        )
        diagonal = window_sum_ref[...]
        half = LANES // 2
        while half >= 1:
            diagonal = pltpu.roll(diagonal[:half], half, 1) + diagonal[half:]
            half //= 2
        grad_offsets_ref[0, slot : slot + 1, :] = diagonal


def attend_back(queries, keys, values, grads, segment_column, segment_row, window, head_size):
    length, width = queries.shape
    per_step = LANES // head_size
    steps = width // LANES
    flat = pl.BlockSpec((length, LANES), lambda step: (0, step))
    flat_shape = jax.ShapeDtypeStruct((length, width), BF16)
    grad_queries, grad_keys, grad_values, grad_offsets = pl.pallas_call(
        lambda *refs: attend_back_kernel(head_size, *refs),
        grid=(steps,),
        in_specs=[
            flat,
            flat,
            flat,
            flat,
            pl.BlockSpec((length, 1), lambda step: (0, 0)),
            pl.BlockSpec((1, length), lambda step: (0, 0)),
            pl.BlockSpec((per_step, LANES, 2 * length), lambda step: (step, 0, 0)),
        ],
        out_specs=[
            flat,
            flat,
            flat,
            pl.BlockSpec((1, per_step, 2 * length), lambda step: (step, 0, 0)),
        ],
        out_shape=[
            flat_shape,
            flat_shape,
            flat_shape,
            jax.ShapeDtypeStruct((steps, per_step, 2 * length), F32),
        ],
        scratch_shapes=[
            pltpu.VMEM((length, length), BF16),
            pltpu.VMEM((length, length), BF16),
            pltpu.VMEM((LANES, 2 * length), F32),
        ],
        name="attend_back",
    )(queries, keys, values, grads, segment_column, segment_row, window)
    return grad_queries, grad_keys, grad_values, grad_offsets.reshape(steps * per_step, 2 * length)


def swap_cores(array):
    return lax.ppermute(array, "mp", [(0, 1), (1, 0)])


def add_small(values, devices):
    sizes = [value.size for value in values]
    flat = jnp.concatenate([value.reshape(-1) for value in values])
    rows = -(-flat.size // (8 * LANES)) * 8
    flat = jnp.pad(flat, (0, rows * LANES - flat.size)).reshape(rows, LANES)
    step = 1
    while step < devices:
        flat = flat + lax.ppermute(flat, "dp", [(i, i ^ step) for i in range(devices)])
        step *= 2
    flat = flat.reshape(-1)
    summed = []
    start = 0
    for value, size in zip(values, sizes):
        summed.append(flat[start : start + size].reshape(value.shape))
        start += size
    return summed


def add_large(values):
    return [
        value.astype(F32) for value in lax.psum([value.astype(BF16) for value in values], "dp")
    ]


def per_device(
    features,
    token_ids,
    mel_target,
    token_target,
    segments,
    row_device,
    offset_bucket,
    speech_weight,
    speech_bias,
    token_table,
    first_gain,
    first_shift,
    query_weight,
    key_weight,
    value_weight,
    bias_table,
    out_weight,
    second_gain,
    second_shift,
    up_weight,
    up_bias,
    down_weight,
    down_bias,
    mel_weight,
    mel_bias,
    vocab_weight,
    vocab_bias,
):
    devices = lax.axis_size("dp")
    device_index = lax.axis_index("dp")
    rows_speech, part_len, feat_width = features.shape
    rows_text = token_ids.shape[0]
    rows_total, length = segments.shape
    vocab_size = token_table.shape[0]
    mel_width = mel_weight.shape[1]
    local_heads = bias_table.shape[1]
    head_size = query_weight.shape[1] // local_heads
    is_speech = device_index < rows_speech

    plain_width = feat_width + mel_width
    sent_width = -(-(plain_width + 2) // LANES) * LANES
    speech_part = jnp.concatenate(
        [features, mel_target, jnp.zeros((rows_speech, part_len, sent_width - plain_width), BF16)],
        axis=2,
    )
    text_part = jnp.concatenate(
        [
            jnp.zeros((rows_text, part_len, plain_width), BF16),
            token_ids[:, :, None].astype(BF16),
            token_target[:, :, None].astype(BF16),
            jnp.zeros((rows_text, part_len, sent_width - plain_width - 2), BF16),
        ],
        axis=2,
    )
    arrived = lax.all_to_all(
        jnp.concatenate([speech_part, text_part], axis=0),
        "dp",
        split_axis=0,
        concat_axis=0,
        tiled=True,
    ).reshape(length, sent_width)
    my_features = arrived[:, :feat_width]
    my_mel = arrived[:, feat_width:plain_width]
    my_ids = arrived[:, plain_width].astype(jnp.int32)
    my_labels = arrived[:, plain_width + 1].astype(jnp.int32)

    my_segments = lax.dynamic_slice_in_dim(segments, device_index, 1)
    segment_column = my_segments.reshape(length, 1)
    reversed_bucket = jnp.pad(offset_bucket[::-1], (0, 1), constant_values=-1)
    bucket_hot = (reversed_bucket[:, None] == jnp.arange(bias_table.shape[0])[None, :]).astype(F32)
    offsets = jnp.dot(bucket_hot, bias_table, precision=HIGHEST).T
    window = bias_window(offsets)

    hot_ids = ((my_ids[:, None] == jnp.arange(vocab_size)[None, :]) & ~is_speech).astype(BF16)
    embedded = (
        matmul(my_features, speech_weight)
        + matmul(hot_ids, token_table)
        + jnp.where(is_speech, speech_bias, 0.0)
    ).astype(BF16)
    flat_rows = embedded.astype(F32)
    norm_one, normal_one, inverse_one = layer_norm(flat_rows, first_gain, first_shift)
    norm_one_low = norm_one.astype(BF16)
    queries = matmul(norm_one_low, query_weight).astype(BF16)
    key_rows = matmul(norm_one_low, key_weight).astype(BF16)
    value_rows = matmul(norm_one_low, value_weight).astype(BF16)
    heads_flat = attend(
        queries, key_rows, value_rows, segment_column, my_segments, window, head_size
    )
    attended = matmul(heads_flat, out_weight)
    mixed_rows = flat_rows + (attended + swap_cores(attended))
    norm_two, normal_two, inverse_two = layer_norm(mixed_rows, second_gain, second_shift)
    norm_two_low = norm_two.astype(BF16)
    hidden = matmul(norm_two_low, up_weight) + up_bias
    active_low = smooth_gelu(hidden).astype(BF16)
    branch = matmul(active_low, down_weight)
    final_low = (mixed_rows + (branch + swap_cores(branch)) + down_bias).astype(BF16)

    predicted = matmul(final_low, mel_weight) + mel_bias
    mel_error = predicted - my_mel.astype(F32)
    smooth = jnp.sqrt(mel_error * mel_error + 1.0)
    mel_scale = jnp.where(is_speech, 1.0 / (mel_width * length), 0.0)
    mel_sum = jnp.sum((smooth - 1.0) * mel_scale)
    grad_predicted = (mel_error / smooth * mel_scale).astype(BF16)
    logits = matmul(final_low, vocab_weight) + vocab_bias
    shifted = logits - jnp.max(logits, axis=-1, keepdims=True)
    powers = jnp.exp(shifted)
    totals = jnp.sum(powers, axis=-1, keepdims=True)
    label_hot = (my_labels[:, None] == jnp.arange(vocab_size)[None, :]).astype(F32)
    text_scale = jnp.where(is_speech, 0.0, 1.0 / length)
    losses = jnp.log(totals) - jnp.sum(shifted * label_hot, axis=-1, keepdims=True)
    text_sum = jnp.sum(losses * text_scale)
    grad_logits = ((powers / totals - label_hot) * text_scale).astype(BF16)
    local_loss = mel_sum + text_sum
    grad_mel_weight = contract_rows(final_low, grad_predicted)
    grad_mel_bias = jnp.sum(grad_predicted.astype(F32), axis=0)
    grad_vocab_weight = contract_rows(final_low, grad_logits)
    grad_vocab_bias = jnp.sum(grad_logits.astype(F32), axis=0)
    grad_final = (
        times_transposed(grad_predicted, mel_weight) + times_transposed(grad_logits, vocab_weight)
    ).astype(BF16)

    grad_down = contract_rows(active_low, grad_final)
    grad_down_bias = jnp.sum(grad_final.astype(F32), axis=0)
    grad_active = times_transposed(grad_final, down_weight)
    gelu_back = jax.vjp(smooth_gelu, hidden)[1]
    grad_hidden_low = gelu_back(grad_active)[0].astype(BF16)
    grad_up = contract_rows(norm_two_low, grad_hidden_low)
    grad_up_bias = jnp.sum(grad_hidden_low.astype(F32), axis=0)
    grad_down, grad_up, grad_mel_weight, grad_vocab_weight = add_large(
        [grad_down, grad_up, grad_mel_weight, grad_vocab_weight]
    )
    grad_norm_two = times_transposed(grad_hidden_low, up_weight).astype(BF16)
    grad_norm_two = grad_norm_two.astype(F32) + swap_cores(grad_norm_two).astype(F32)
    grad_mixed_part, grad_second_gain, grad_second_shift = norm_back(
        grad_norm_two, normal_two, inverse_two, second_gain
    )
    grad_mixed = grad_final.astype(F32) + grad_mixed_part
    grad_mixed_low = grad_mixed.astype(BF16)
    grad_out = contract_rows(heads_flat, grad_mixed_low)
    grad_heads = times_transposed(grad_mixed_low, out_weight).astype(BF16)
    grad_queries, grad_keys, grad_values, grad_offsets = attend_back(
        queries, key_rows, value_rows, grad_heads, segment_column, my_segments, window, head_size
    )
    grad_table = jnp.dot(bucket_hot.T, grad_offsets.T, precision=HIGHEST)
    grad_query = contract_rows(norm_one_low, grad_queries)
    grad_key = contract_rows(norm_one_low, grad_keys)
    grad_value = contract_rows(norm_one_low, grad_values)
    grad_norm_one = (
        times_transposed(grad_queries, query_weight)
        + times_transposed(grad_keys, key_weight)
        + times_transposed(grad_values, value_weight)
    ).astype(BF16)
    grad_norm_one = grad_norm_one.astype(F32) + swap_cores(grad_norm_one).astype(F32)
    grad_in_part, grad_first_gain, grad_first_shift = norm_back(
        grad_norm_one, normal_one, inverse_one, first_gain
    )
    grad_embedded = (grad_mixed + grad_in_part).astype(BF16)
    grad_speech_weight = contract_rows(my_features, grad_embedded)
    grad_speech_bias = jnp.where(is_speech, jnp.sum(grad_embedded.astype(F32), axis=0), 0.0)
    grad_token_table = contract_rows(hot_ids, grad_embedded)
    feature_back = times_transposed(grad_embedded, speech_weight).astype(BF16)
    feature_grad = lax.all_to_all(
        feature_back.reshape(devices, part_len, feat_width),
        "dp",
        split_axis=0,
        concat_axis=0,
        tiled=True,
    )[:rows_speech]
    (grad_out, grad_query, grad_key, grad_value, grad_speech_weight, grad_token_table) = add_large(
        [grad_out, grad_query, grad_key, grad_value, grad_speech_weight, grad_token_table]
    )
    (
        loss_total,
        grad_down_bias,
        grad_up_bias,
        grad_second_gain,
        grad_second_shift,
        grad_mel_bias,
        grad_vocab_bias,
        grad_table,
        grad_first_gain,
        grad_first_shift,
        grad_speech_bias,
    ) = add_small(
        [
            local_loss,
            grad_down_bias,
            grad_up_bias,
            grad_second_gain,
            grad_second_shift,
            grad_mel_bias,
            grad_vocab_bias,
            grad_table,
            grad_first_gain,
            grad_first_shift,
            grad_speech_bias,
        ],
        devices,
    )
    return (
        loss_total / rows_total,
        feature_grad,
        grad_speech_weight,
        grad_speech_bias,
        grad_token_table,
        grad_first_gain,
        grad_first_shift,
        grad_query,
        grad_key,
        grad_value,
        grad_table,
        grad_out,
        grad_second_gain,
        grad_second_shift,
        grad_up,
        grad_up_bias,
        grad_down,
        grad_down_bias,
        grad_mel_weight,
        grad_mel_bias,
        grad_vocab_weight,
        grad_vocab_bias,
    )


def solution(mesh):
    placed = (
        P(None, "dp", None),
        P(None, "dp"),
        P(None, "dp", None),
        P(None, "dp"),
        P(),
        P(),
        P(),
        P(),
        P(),
        P(),
        P(),
        P(),
        P(None, "mp"),
        P(None, "mp"),
        P(None, "mp"),
        P(None, "mp"),
        P("mp", None),
        P(),
        P(),
        P(None, "mp"),
        P("mp"),
        P("mp", None),
        P(),
        P(),
        P(),
        P(),
        P(),
    )
    return jax.shard_map(
        per_device,
        mesh=mesh,
        in_specs=placed,
        out_specs=(
            P(),
            P(None, "dp", None),
            P(),
            P(),
            P(),
            P(),
            P(),
            P(None, "mp"),
            P(None, "mp"),
            P(None, "mp"),
            P(None, "mp"),
            P("mp", None),
            P(),
            P(),
            P(None, "mp"),
            P("mp"),
            P("mp", None),
            P(),
            P(),
            P(),
            P(),
            P(),
        ),
        check_vma=False,
    )
```

```python
import functools

import jax
import jax.numpy as jnp
from jax import lax
from jax.experimental import pallas as pl
from jax.experimental.pallas import tpu as pltpu
from jax.sharding import PartitionSpec as P

EPSILON = 1e-05
NEGATIVE = -1e30
HIGHEST = lax.Precision.HIGHEST
BF16 = jnp.bfloat16
F32 = jnp.float32
LANES = 128
SMALL_ROWS = 16


def contract_rows(left_side, right_side):
    return lax.dot_general(
        left_side, right_side, (((0,), (0,)), ((), ())), preferred_element_type=F32
    )


def times_transposed(left_side, right_side):
    return lax.dot_general(
        left_side, right_side, (((1,), (1,)), ((), ())), preferred_element_type=F32
    )


def matmul(left_side, right_side):
    return jnp.dot(left_side, right_side, preferred_element_type=F32)


def normalize(row_data):
    center = row_data - jnp.mean(row_data, axis=-1, keepdims=True)
    inverse = lax.rsqrt(jnp.mean(center * center, axis=-1, keepdims=True) + EPSILON)
    return center * inverse, inverse


def norm_back(grad_out, normal, inverse, norm_gain):
    scaled = grad_out * norm_gain
    return inverse * (
        scaled
        - jnp.mean(scaled, axis=-1, keepdims=True)
        - normal * jnp.mean(scaled * normal, axis=-1, keepdims=True)
    )


def column_sum(array):
    return jnp.sum(array, axis=0, keepdims=True)


def cost(microseconds):
    return pl.CostEstimate(
        flops=0, bytes_accessed=int(microseconds * 3.5e6), transcendentals=0
    )


def run_kernel(kernel, name, microseconds, flags, operands, outputs, scratch=()):
    in_place = pl.BlockSpec(memory_space=pltpu.VMEM)
    return pl.pallas_call(
        kernel,
        in_specs=[pl.BlockSpec(memory_space=pltpu.SMEM)] + [in_place] * len(operands),
        out_specs=[in_place] * len(outputs),
        out_shape=[jax.ShapeDtypeStruct(shape, kind) for shape, kind in outputs],
        scratch_shapes=list(scratch),
        compiler_params=pltpu.CompilerParams(vmem_limit_bytes=40 * 1024 * 1024),
        cost_estimate=cost(microseconds),
        name=name,
    )(flags, *operands)


def blocks_of(length, size):
    return [slice(start, start + size) for start in range(0, length, size)]


def window_kernel(offsets_ref, window_ref):
    heads, width = offsets_ref.shape
    for head in range(heads):
        spread = jnp.broadcast_to(offsets_ref[head : head + 1, :], (LANES, width))
        window_ref[head] = pltpu.roll(spread, width - LANES + 1, 1, stride=1, stride_axis=0)


def bias_window(offsets):
    heads, width = offsets.shape
    return pl.pallas_call(
        window_kernel,
        out_shape=jax.ShapeDtypeStruct((heads, LANES, width), F32),
        cost_estimate=cost(3),
        name="bias_window",
    )(offsets)


def key_probs(keys, queries, window_ref, head, mask_ref):
    length = keys.shape[0]
    blocks = length // LANES
    bias = jnp.concatenate(
        [
            window_ref[head, :, LANES * (blocks - 1 - b) : LANES * (blocks - 1 - b) + length]
            for b in range(blocks)
        ],
        axis=0,
    )
    scores = times_transposed(keys, queries) + bias + mask_ref[...]
    powers = jnp.exp(scores - jnp.max(scores, axis=0, keepdims=True))
    return powers * (1.0 / column_sum(powers))


def attend_kernel(
    head_size,
    plain_width,
    flags_ref,
    own_ref,
    other_ref,
    input_weight_ref,
    speech_bias_ref,
    gain_ref,
    shift_ref,
    query_weight_ref,
    key_weight_ref,
    value_weight_ref,
    out_weight_ref,
    window_ref,
    column_ref,
    row_ref,
    embedded_ref,
    normed_ref,
    queries_ref,
    keys_ref,
    values_ref,
    heads_ref,
    attended_ref,
    inputs_ref,
    extra_ref,
    mask_ref,
):
    length, half_width = own_ref.shape
    feat_width = inputs_ref.shape[1] - LANES
    first = flags_ref[0] == 0
    speech = flags_ref[1].astype(F32)
    scaling = jnp.asarray(head_size ** (-0.5), BF16)
    for rows in blocks_of(length, LANES):
        own, other = own_ref[rows, :], other_ref[rows, :]
        low = jnp.where(first, own, other)
        high = jnp.where(first, other, own)
        inputs_ref[rows, :half_width] = low
        inputs_ref[rows, half_width:feat_width] = high[:, : feat_width - half_width]
        extra = high[:, feat_width - half_width : feat_width - half_width + LANES]
        extra_ref[rows, :] = extra
        ids = extra[:, plain_width - feat_width : plain_width - feat_width + 1].astype(F32)
        places = lax.broadcasted_iota(jnp.int32, (LANES, LANES), 1).astype(F32)
        hot = jnp.where(ids == places, 1.0 - speech, 0.0)
        inputs_ref[rows, feat_width:] = hot.astype(BF16)
    for rows in blocks_of(length, 2 * LANES):
        embedded = matmul(inputs_ref[rows, :], input_weight_ref[...]) + speech_bias_ref[...] * speech
        embedded = embedded.astype(BF16)
        embedded_ref[rows, :] = embedded
        normal, _ = normalize(embedded.astype(F32))
        normed = (normal * gain_ref[...] + shift_ref[...]).astype(BF16)
        normed_ref[rows, :] = normed
        queries_ref[rows, :] = matmul(normed, query_weight_ref[...]).astype(BF16) * scaling
        keys_ref[rows, :] = matmul(normed, key_weight_ref[...]).astype(BF16)
        values_ref[rows, :] = matmul(normed, value_weight_ref[...]).astype(BF16)
    mask_ref[...] = jnp.where(column_ref[...] == row_ref[...], 0.0, NEGATIVE)
    for head, columns in enumerate(blocks_of(queries_ref.shape[1], head_size)):
        probs = key_probs(
            keys_ref[:, columns], queries_ref[:, columns], window_ref, head, mask_ref
        ).astype(BF16)
        heads_ref[:, columns] = contract_rows(probs, values_ref[:, columns]).astype(BF16)
    for rows in blocks_of(length, 2 * LANES):
        attended_ref[rows, :] = matmul(heads_ref[rows, :], out_weight_ref[...]).astype(BF16)


def forward_kernel(
    flags_ref,
    embedded_ref,
    own_ref,
    other_ref,
    gain_ref,
    shift_ref,
    up_weight_ref,
    up_bias_ref,
    down_weight_ref,
    mixed_ref,
    normed_ref,
    active_ref,
    slope_ref,
    branch_ref,
):
    for rows in blocks_of(embedded_ref.shape[0], 2 * LANES):
        mixed = embedded_ref[rows, :].astype(F32) + (
            own_ref[rows, :].astype(F32) + other_ref[rows, :].astype(F32)
        )
        mixed_ref[rows, :] = mixed
        normal, _ = normalize(mixed)
        normed = (normal * gain_ref[...] + shift_ref[...]).astype(BF16)
        normed_ref[rows, :] = normed
        hidden = matmul(normed, up_weight_ref[...]) + up_bias_ref[...]
        square = hidden * hidden
        inner = 0.7978845608028654 * hidden * (1.0 + 0.044715 * square)
        curve = jnp.tanh(inner)
        half = 0.5 * (1.0 + curve)
        active = (hidden * half).astype(BF16)
        active_ref[rows, :] = active
        slope_ref[rows, :] = half + 0.5 * hidden * (1.0 - curve * curve) * (
            0.7978845608028654 * (1.0 + 0.134145 * square)
        )
        branch_ref[rows, :] = matmul(active, down_weight_ref[...]).astype(BF16)


def loss_kernel(
    mel_width,
    vocab_size,
    flags_ref,
    mixed_ref,
    own_ref,
    other_ref,
    down_bias_ref,
    post_weight_ref,
    post_bias_ref,
    extra_ref,
    slope_ref,
    up_weight_ref,
    down_weight_ref,
    final_ref,
    grad_post_ref,
    grad_final_ref,
    grad_hidden_ref,
    grad_normed_ref,
    loss_ref,
    post_sum_ref,
    final_sum_ref,
    hidden_sum_ref,
):
    length = mixed_ref.shape[0]
    speech = flags_ref[1].astype(F32)
    mel_scale = speech * (1.0 / (mel_width * length))
    text_scale = (1.0 - speech) * (1.0 / length)
    totals = None
    for rows in blocks_of(length, 2 * LANES):
        final = mixed_ref[rows, :] + (
            own_ref[rows, :].astype(F32) + other_ref[rows, :].astype(F32)
        )
        final = (final + down_bias_ref[...]).astype(BF16)
        final_ref[rows, :] = final
        results = matmul(final, post_weight_ref[...]) + post_bias_ref[...]
        extra = extra_ref[rows, :].astype(F32)
        places = lax.broadcasted_iota(jnp.int32, extra.shape, 1)
        error = jnp.where(places < mel_width, results[:, :LANES] - extra, 0.0)
        smooth = jnp.sqrt(error * error + 1.0)
        grad_mel = error / smooth * mel_scale
        logits = jnp.where(places < vocab_size, results[:, LANES:], NEGATIVE)
        shifted = logits - jnp.max(logits, axis=-1, keepdims=True)
        powers = jnp.exp(shifted)
        power_sum = jnp.sum(powers, axis=-1, keepdims=True)
        label = extra[:, mel_width + 1 : mel_width + 2] == places.astype(F32)
        picked = jnp.sum(jnp.where(label, shifted, 0.0), axis=-1, keepdims=True)
        text_loss = column_sum(jnp.log(power_sum) - picked) * text_scale
        mel_loss = column_sum((smooth - 1.0) * mel_scale)
        loss = mel_loss + jnp.where(places[:1] == 0, text_loss, 0.0)
        grad_text = (powers / power_sum - jnp.where(label, 1.0, 0.0)) * text_scale
        grad_post = jnp.concatenate([grad_mel, grad_text], axis=1).astype(BF16)
        grad_post_ref[rows, :] = grad_post
        grad_final = times_transposed(grad_post, post_weight_ref[...]).astype(BF16)
        grad_final_ref[rows, :] = grad_final
        grad_active = times_transposed(grad_final, down_weight_ref[...])
        grad_hidden = (slope_ref[rows, :] * grad_active).astype(BF16)
        grad_hidden_ref[rows, :] = grad_hidden
        grad_normed_ref[rows, :] = times_transposed(grad_hidden, up_weight_ref[...]).astype(BF16)
        sums = (
            loss,
            column_sum(grad_post.astype(F32)),
            column_sum(grad_final.astype(F32)),
            column_sum(grad_hidden.astype(F32)),
        )
        totals = sums if totals is None else [a + b for a, b in zip(totals, sums)]
    loss_ref[...] = jnp.broadcast_to(jnp.sum(totals[0], axis=1, keepdims=True), loss_ref.shape)
    post_sum_ref[...] = totals[1]
    final_sum_ref[...] = totals[2]
    hidden_sum_ref[...] = totals[3]


def wide(ref, start, size):
    return ref[:, pl.ds(pl.multiple_of(start, LANES), size)]


def early_kernel(
    flags_ref,
    active_ref,
    normed_ref,
    grad_final_ref,
    grad_hidden_ref,
    grad_post_ref,
    final_ref,
    first_ref,
    second_ref,
    post_ref,
):
    width = final_ref.shape[1]
    units = active_ref.shape[1] // 2
    post_rows = LANES // 2
    cut = width // 3
    model_rows = cut // 2
    first_half, second_half = flags_ref[2], flags_ref[3]
    first_ref[:units, :] = contract_rows(
        wide(active_ref, first_half * units, units), grad_final_ref[...]
    ).astype(BF16)
    post_ref[...] = contract_rows(wide(grad_post_ref, flags_ref[0] * LANES, LANES), final_ref[...])
    first_ref[units : units + post_rows, :] = post_ref[
        pl.ds(pl.multiple_of(first_half * post_rows, post_rows), post_rows), :
    ].astype(BF16)
    grad_model = contract_rows(
        wide(normed_ref, first_half * model_rows, model_rows), grad_hidden_ref[...]
    ).astype(BF16)
    start = units + post_rows
    for columns in blocks_of(grad_model.shape[1], width):
        first_ref[start : start + model_rows, :] = grad_model[:, columns]
        start += model_rows
    rest = (width - cut) // 2
    second_ref[...] = contract_rows(
        wide(normed_ref, cut + second_half * rest, rest), grad_hidden_ref[...]
    ).astype(BF16)


def back_kernel(
    head_size,
    flags_ref,
    own_ref,
    other_ref,
    mixed_ref,
    grad_final_ref,
    gain_ref,
    out_weight_ref,
    queries_ref,
    keys_ref,
    values_ref,
    window_ref,
    column_ref,
    row_ref,
    query_weight_ref,
    key_weight_ref,
    value_weight_ref,
    grad_mixed_ref,
    grad_low_ref,
    grad_projected_ref,
    grad_normed_ref,
    grad_offsets_ref,
    gain_sum_ref,
    shift_sum_ref,
    grad_heads_ref,
    mask_ref,
    probs_ref,
    scores_ref,
    window_sum_ref,
):
    length, head_width = queries_ref.shape
    blocks = length // LANES
    gain_sum, shift_sum = 0.0, 0.0
    for rows in blocks_of(length, 2 * LANES):
        grad_normed = own_ref[rows, :].astype(F32) + other_ref[rows, :].astype(F32)
        normal, inverse = normalize(mixed_ref[rows, :])
        gain_sum += column_sum(grad_normed * normal)
        shift_sum += column_sum(grad_normed)
        grad_mixed = grad_final_ref[rows, :].astype(F32) + norm_back(
            grad_normed, normal, inverse, gain_ref[...]
        )
        grad_mixed_ref[rows, :] = grad_mixed
        grad_low = grad_mixed.astype(BF16)
        grad_low_ref[rows, :] = grad_low
        grad_heads_ref[rows, :] = times_transposed(grad_low, out_weight_ref[...]).astype(BF16)
    gain_sum_ref[...] = gain_sum
    shift_sum_ref[...] = shift_sum
    mask_ref[...] = jnp.where(column_ref[...] == row_ref[...], 0.0, NEGATIVE)
    scaling = head_size ** (-0.5)
    for head, columns in enumerate(blocks_of(head_width, head_size)):
        keys, queries = keys_ref[:, columns], queries_ref[:, columns]
        grads = grad_heads_ref[:, columns]
        probs = key_probs(keys, queries, window_ref, head, mask_ref)
        weighted = probs * times_transposed(values_ref[:, columns], grads)
        grad_scores = weighted - probs * column_sum(weighted)
        probs_ref[...] = probs.astype(BF16)
        scores_ref[...] = grad_scores.astype(BF16)
        window_sum_ref[...] = jnp.zeros_like(window_sum_ref)
        for block in range(blocks):
            start = LANES * (blocks - 1 - block)
            window_sum_ref[:, start : start + length] += grad_scores[
                LANES * block : LANES * (block + 1)
            ]
        start = head * head_size
        for kind, value in enumerate(
            (
                contract_rows(scores_ref[...], keys) * scaling,
                matmul(scores_ref[...], queries),
                matmul(probs_ref[...], grads),
            )
        ):
            grad_projected_ref[
                :, kind * head_width + start : kind * head_width + start + head_size
            ] = value.astype(BF16)
        diagonal = window_sum_ref[...]
        half = LANES // 2
        while half >= 1:
            diagonal = pltpu.roll(diagonal[:half], half, 1) + diagonal[half:]
            half //= 2
        grad_offsets_ref[head : head + 1, :] = diagonal
    for rows in blocks_of(length, 2 * LANES):
        total = 0.0
        for kind, weight_ref in enumerate((query_weight_ref, key_weight_ref, value_weight_ref)):
            total += times_transposed(
                grad_projected_ref[rows, kind * head_width : (kind + 1) * head_width],
                weight_ref[...],
            )
        grad_normed_ref[rows, :] = total.astype(BF16)


def late_kernel(flags_ref, normed_ref, grad_projected_ref, heads_ref, grad_low_ref, first_ref):
    width = normed_ref.shape[1]
    head_width = heads_ref.shape[1]
    half = width // 2
    first_ref[:half, :] = contract_rows(
        wide(normed_ref, flags_ref[2] * half, half), grad_projected_ref[:, : 2 * head_width]
    ).astype(BF16)
    grad_out = contract_rows(heads_ref[...], wide(grad_low_ref, flags_ref[2] * half, half))
    count = head_width // 2
    first_ref[half:, :half] = grad_out[:count].astype(BF16)
    first_ref[half:, half:] = grad_out[count:].astype(BF16)


def input_kernel(
    flags_ref,
    own_ref,
    other_ref,
    embedded_ref,
    grad_mixed_ref,
    gain_ref,
    speech_weight_ref,
    inputs_ref,
    normed_ref,
    grad_projected_ref,
    loss_ref,
    post_sum_ref,
    final_sum_ref,
    gain_two_ref,
    shift_two_ref,
    hidden_sum_ref,
    table_ref,
    sent_ref,
    kept_ref,
    feature_back_ref,
    terms_ref,
    grad_embedded_ref,
    hot_ref,
):
    length, width = embedded_ref.shape
    feat_width = speech_weight_ref.shape[0]
    core_width = feat_width // 2
    head_width = grad_projected_ref.shape[1] // 3
    speech = flags_ref[1].astype(F32)
    core = flags_ref[0]
    gain_sum, shift_sum, bias_sum = 0.0, 0.0, 0.0
    core_weight = speech_weight_ref[pl.ds(pl.multiple_of(core * core_width, core_width), core_width), :]
    for rows in blocks_of(length, 2 * LANES):
        grad_normed = own_ref[rows, :].astype(F32) + other_ref[rows, :].astype(F32)
        normal, inverse = normalize(embedded_ref[rows, :].astype(F32))
        gain_sum += column_sum(grad_normed * normal)
        shift_sum += column_sum(grad_normed)
        grad_embedded = (
            grad_mixed_ref[rows, :] + norm_back(grad_normed, normal, inverse, gain_ref[...])
        ).astype(BF16)
        grad_embedded_ref[rows, :] = grad_embedded
        bias_sum += column_sum(grad_embedded.astype(F32))
        feature_back_ref[rows, :] = times_transposed(grad_embedded, core_weight).astype(BF16)
    hot_ref[...] = contract_rows(inputs_ref[:, feat_width:], grad_embedded_ref[...])
    value_rows = width // 4
    feat_rows = core_width // 2
    hot_rows = LANES // 4
    for which_ref, half in ((sent_ref, flags_ref[3]), (kept_ref, 1 - flags_ref[3])):
        grad_value = contract_rows(
            wide(normed_ref, half * (width // 2), width // 2),
            grad_projected_ref[:, 2 * head_width :],
        ).astype(BF16)
        which_ref[:value_rows, :head_width] = grad_value[:value_rows]
        which_ref[:value_rows, head_width:] = grad_value[value_rows:]
        which_ref[value_rows : value_rows + feat_rows, :] = contract_rows(
            wide(inputs_ref, core * core_width + half * feat_rows, feat_rows), grad_embedded_ref[...]
        ).astype(BF16)
        start = value_rows + feat_rows
        which_ref[start : start + hot_rows, :] = hot_ref[
            pl.ds(pl.multiple_of(core * 2 * hot_rows + half * hot_rows, hot_rows), hot_rows), :
        ].astype(BF16)
    terms_ref[...] = jnp.zeros_like(terms_ref)
    terms_ref[:1, :LANES] = loss_ref[...]
    terms_ref[:1, LANES : 3 * LANES] = post_sum_ref[...]
    bias_rows = hidden_sum_ref.shape[1] // width
    rows = [final_sum_ref[...], gain_two_ref[...], shift_two_ref[...], gain_sum, shift_sum]
    rows += [bias_sum * speech]
    rows += [hidden_sum_ref[:, part * width : (part + 1) * width] for part in range(bias_rows)]
    for place, row in enumerate(rows):
        terms_ref[place + 1 : place + 2, :] = row
    start = len(rows) + 1
    terms_ref[start : start + table_ref.shape[0], : table_ref.shape[1]] = table_ref[...]
    terms = terms_ref[...]
    high = terms.astype(BF16)
    rest = (terms - high.astype(F32)).astype(BF16)
    terms_ref[...] = high.astype(F32) + rest.astype(F32)
    start = value_rows + feat_rows + hot_rows
    sent_ref[start : start + SMALL_ROWS, :] = high
    sent_ref[start + SMALL_ROWS :, :] = rest


def swap_cores(array):
    return lax.ppermute(array, "mp", [(0, 1), (1, 0)])


def half_of(rows, which):
    count = rows.shape[0] // 2
    return lax.dynamic_slice_in_dim(rows, which * count, count)


def add_low(left_side, right_side):
    return (left_side.astype(F32) + right_side.astype(F32)).astype(BF16)


def split_small(small):
    high = lax.reduce_precision(small, exponent_bits=8, mantissa_bits=7)
    rest = lax.reduce_precision(small - high, exponent_bits=8, mantissa_bits=7)
    return high, rest


def tie(*arrays):
    return lax.optimization_barrier(arrays)


ORDERS = (((0, 1, 2), (1, 2, 0)), ((2, 0, 1), (2, 0, 1)))


class Links:
    def __init__(self, devices, cores, index, core):
        self.devices, self.cores, self.index, self.core = devices, cores, index, core
        self.bits = devices.bit_length() - 1

    def exchange(self, array, bits):
        pairs = [
            (place * self.cores + core, (place ^ (1 << bits[core])) * self.cores + core)
            for place in range(self.devices)
            for core in range(self.cores)
        ]
        return lax.ppermute(array, ("dp", "mp"), pairs)

    def mine(self, bits):
        return (self.index >> jnp.where(self.core == 0, bits[0], bits[1])) & 1


def order_bits(slot, step):
    return tuple(order[step] for order in ORDERS[slot])


class Wave:
    def __init__(self, links, terms=None):
        self.links = links
        self.terms = terms
        self.sent = [None, None]
        self.kept = [None, None]

    def with_small(self, rows):
        if self.terms is None:
            return rows
        high, rest = split_small(self.small)
        self.terms = high + rest
        return jnp.concatenate([rows, high.astype(BF16), rest.astype(BF16)], axis=0)

    def take_small(self, came):
        if self.terms is None:
            return came
        extra = self.terms.shape[0]
        count = came.shape[0] - 2 * extra
        self.small = self.terms + (
            came[count : count + extra].astype(F32) + came[count + extra :].astype(F32)
        )
        return came[:count]

    def scatter(self, slot, step):
        packed = slot == 1 and step > 0
        rows = self.with_small(self.sent[slot]) if packed else self.sent[slot]
        return self.links.exchange(rows, order_bits(slot, step))

    def add(self, slot, step, came):
        if slot == 1:
            came = self.take_small(came)
        kept = self.kept[slot]
        if step == 2:
            self.kept[slot] = add_low(kept, came)
            return
        mine = self.links.mine(order_bits(slot, step + 1))
        sent = add_low(half_of(kept, 1 - mine), half_of(came, 1 - mine))
        kept, came, self.sent[slot] = tie(kept, came, sent)
        self.kept[slot] = add_low(half_of(kept, mine), half_of(came, mine))

    def join(self):
        self.shapes = [share.shape for share in self.kept]
        self.joint = min(share.shape[1] for share in self.kept)
        self.joined = jnp.concatenate(
            [share.reshape(-1, self.joint) for share in self.kept], axis=0
        )
        self.came_joined = self.joined
        for bit in range(3, self.links.bits):
            if bit > 3:
                self.add_joined()
            mine = self.links.mine((bit, bit))
            sent, self.joined = half_of(self.joined, 1 - mine), half_of(self.joined, mine)
            self.came_joined = self.links.exchange(self.with_small(sent), (bit, bit))

    def add_joined(self):
        self.joined = add_low(self.joined, self.take_small(self.came_joined))

    def both(self, rows, came, bits):
        first = self.links.mine(bits) == 0
        return jnp.where(first, rows, came), jnp.where(first, came, rows)

    def gather_joined(self):
        for bit in reversed(range(3, self.links.bits)):
            if bit < self.links.bits - 1:
                self.place_joined(bit + 1)
            self.came_joined = self.links.exchange(self.joined, (bit, bit))

    def place_joined(self, bit):
        self.joined = jnp.concatenate(
            self.both(self.joined, self.came_joined, (bit, bit)), axis=0
        )

    def split_joined(self):
        self.place_joined(3)
        self.shares = []
        start = 0
        for shape in self.shapes:
            count = shape[0] * shape[1] // self.joint
            self.shares.append(self.joined[start : start + count].reshape(shape))
            start += count

    def gather(self, step):
        return [
            self.links.exchange(rows, order_bits(slot, step))
            for slot, rows in enumerate(self.shares)
        ]

    def place(self, step, came):
        pairs = [
            self.both(rows, other, order_bits(slot, step))
            for slot, (rows, other) in enumerate(zip(self.shares, came))
        ]
        if step == 0:
            return pairs
        self.shares = [jnp.concatenate(pair, axis=0) for pair in pairs]


def unfold(rows, count):
    return jnp.concatenate(
        [rows[start : start + count] for start in range(0, rows.shape[0], count)], axis=1
    )


def per_device(
    features,
    token_ids,
    mel_target,
    token_target,
    segments,
    row_device,
    offset_bucket,
    speech_weight,
    speech_bias,
    token_table,
    first_gain,
    first_shift,
    query_weight,
    key_weight,
    value_weight,
    bias_table,
    out_weight,
    second_gain,
    second_shift,
    up_weight,
    up_bias,
    down_weight,
    down_bias,
    mel_weight,
    mel_bias,
    vocab_weight,
    vocab_bias,
):
    devices = lax.axis_size("dp")
    device_index = lax.axis_index("dp")
    core = lax.axis_index("mp")
    cores = lax.axis_size("mp")
    rows_speech, part_len, feat_width = features.shape
    rows_text = token_ids.shape[0]
    rows_total, length = segments.shape
    model_width = speech_weight.shape[1]
    vocab_size = token_table.shape[0]
    mel_width = mel_weight.shape[1]
    local_heads = bias_table.shape[1]
    buckets = bias_table.shape[0]
    head_width = query_weight.shape[1]
    head_size = head_width // local_heads
    units = up_weight.shape[1]
    is_speech = device_index < rows_speech
    links = Links(devices, cores, device_index, core)

    def flags_of(wave_half):
        return jnp.stack(
            [core, is_speech.astype(jnp.int32)]
            + [
                half if wave_half == 0 else 1 - half
                for half in (1 - links.mine(order_bits(0, 0)), 1 - links.mine(order_bits(1, 0)))
            ]
        ).astype(jnp.int32)

    sent_flags, kept_flags = flags_of(0), flags_of(1)

    plain_width = feat_width + mel_width
    core_width = -(-(plain_width + 2) // (LANES * cores)) * LANES
    sent_width = core_width * cores
    speech_part = jnp.concatenate(
        [features, mel_target, jnp.zeros((rows_speech, part_len, sent_width - plain_width), BF16)],
        axis=2,
    )
    text_part = jnp.concatenate(
        [
            jnp.zeros((rows_text, part_len, plain_width), BF16),
            token_ids[:, :, None].astype(BF16),
            token_target[:, :, None].astype(BF16),
            jnp.zeros((rows_text, part_len, sent_width - plain_width - 2), BF16),
        ],
        axis=2,
    )
    arrived = lax.all_to_all(
        lax.dynamic_slice_in_dim(
            jnp.concatenate([speech_part, text_part], axis=0), core * core_width, core_width, axis=2
        ),
        "dp",
        split_axis=0,
        concat_axis=0,
        tiled=True,
    ).reshape(length, core_width)

    my_segments = lax.dynamic_slice_in_dim(segments, device_index, 1)
    segment_column = my_segments.reshape(length, 1)
    padded_bucket = jnp.pad(offset_bucket, (0, 1), constant_values=-1)
    bucket_hot = (padded_bucket[:, None] == jnp.arange(buckets)[None, :]).astype(F32)
    window = bias_window(jnp.dot(bucket_hot, bias_table, precision=HIGHEST).T)
    input_weight = jnp.concatenate(
        [speech_weight, jnp.pad(token_table, ((0, LANES - vocab_size), (0, 0)))], axis=0
    )
    post_weight = jnp.concatenate(
        [
            jnp.pad(mel_weight, ((0, 0), (0, LANES - mel_width))),
            jnp.pad(vocab_weight, ((0, 0), (0, LANES - vocab_size))),
        ],
        axis=1,
    )
    post_bias = jnp.concatenate(
        [jnp.pad(mel_bias, (0, LANES - mel_width)), jnp.pad(vocab_bias, (0, LANES - vocab_size))]
    )
    line = lambda vector: vector.reshape(1, -1)
    arrived, window, segment_column, input_weight, post_weight = tie(
        arrived, window, segment_column, input_weight, post_weight
    )

    model_low = ((length, model_width), BF16)
    head_low = ((length, head_width), BF16)
    line_out = ((1, model_width), F32)
    (
        embedded,
        normed_one,
        queries,
        key_rows,
        value_rows,
        heads_flat,
        attended,
        inputs,
        extra,
    ) = run_kernel(
        functools.partial(attend_kernel, head_size, plain_width),
        "embed_and_attend",
        10,
        sent_flags,
        [
            arrived,
            swap_cores(arrived),
            input_weight,
            line(speech_bias),
            line(first_gain),
            line(first_shift),
            query_weight,
            key_weight,
            value_weight,
            out_weight,
            window,
            segment_column,
            my_segments,
        ],
        [
            model_low,
            model_low,
            head_low,
            head_low,
            head_low,
            head_low,
            model_low,
            ((length, feat_width + LANES), BF16),
            ((length, LANES), BF16),
        ],
        [pltpu.VMEM((length, length), F32)],
    )
    mixed, normed_two, active, slope, branch = run_kernel(
        forward_kernel,
        "feed_forward",
        5,
        sent_flags,
        [
            embedded,
            attended,
            swap_cores(attended),
            line(second_gain),
            line(second_shift),
            up_weight,
            line(up_bias),
            down_weight,
        ],
        [
            ((length, model_width), F32),
            model_low,
            ((length, units), BF16),
            ((length, units), F32),
            model_low,
        ],
    )
    (
        final_low,
        grad_post,
        grad_final,
        grad_hidden,
        grad_normed_two,
        loss_row,
        post_sum,
        final_sum,
        hidden_sum,
    ) = run_kernel(
        functools.partial(loss_kernel, mel_width, vocab_size),
        "loss_and_feed_back",
        6,
        sent_flags,
        [
            mixed,
            branch,
            swap_cores(branch),
            line(down_bias),
            post_weight,
            line(post_bias),
            extra,
            slope,
            up_weight,
            down_weight,
        ],
        [
            model_low,
            ((length, 2 * LANES), BF16),
            model_low,
            ((length, units), BF16),
            model_low,
            ((1, LANES), F32),
            ((1, 2 * LANES), F32),
            line_out,
            ((1, units), F32),
        ],
    )

    early = Wave(links)
    model_cut = model_width // 3
    unit_part = units // 2
    post_end = unit_part + LANES // 2

    def early_half(flags):
        return run_kernel(
            early_kernel,
            "early_weights",
            3,
            flags,
            [active, normed_two, grad_final, grad_hidden, grad_post, final_low],
            [
                ((post_end + model_cut // 2 * units // model_width, model_width), BF16),
                (((model_width - model_cut) // 2, units), BF16),
            ],
            [pltpu.VMEM((LANES, model_width), F32)],
        )

    early.sent = list(early_half(sent_flags))
    early_came = [early.scatter(0, 0), early.scatter(1, 0)]
    other_normed_two = swap_cores(grad_normed_two)
    early.kept = list(early_half(kept_flags))
    (
        grad_mixed,
        grad_mixed_low,
        grad_projected,
        grad_normed_one,
        grad_offsets,
        second_gain_sum,
        second_shift_sum,
    ) = run_kernel(
        functools.partial(back_kernel, head_size),
        "attend_back",
        10,
        sent_flags,
        [
            grad_normed_two,
            other_normed_two,
            mixed,
            grad_final,
            line(second_gain),
            out_weight,
            queries,
            key_rows,
            value_rows,
            window,
            segment_column,
            my_segments,
            query_weight,
            key_weight,
            value_weight,
        ],
        [
            ((length, model_width), F32),
            model_low,
            ((length, 3 * head_width), BF16),
            model_low,
            ((local_heads, 2 * length), F32),
            line_out,
            line_out,
        ],
        [
            pltpu.VMEM((length, head_width), BF16),
            pltpu.VMEM((length, length), F32),
            pltpu.VMEM((length, length), BF16),
            pltpu.VMEM((length, length), BF16),
            pltpu.VMEM((LANES, 2 * length), F32),
        ],
    )
    other_normed_one = swap_cores(grad_normed_one)

    def late_half(flags):
        return run_kernel(
            late_kernel,
            "late_weights",
            2,
            flags,
            [normed_one, grad_projected, heads_flat, grad_mixed_low],
            [((model_width // 2 + head_width // 2, model_width), BF16)],
        )[0]

    late_sent = late_half(sent_flags)
    late_kept = late_half(kept_flags)
    early.add(0, 0, early_came[0])
    early.add(1, 0, early_came[1])
    early_came = [early.scatter(0, 1), early.scatter(1, 1)]
    grad_table = jnp.dot(grad_offsets, bucket_hot, precision=HIGHEST)
    late_rows = model_width // 4 + feat_width // 4 + LANES // 4
    late_second_sent, late_second_kept, feature_back, terms = run_kernel(
        input_kernel,
        "input_back",
        4,
        sent_flags,
        [
            grad_normed_one,
            other_normed_one,
            embedded,
            grad_mixed,
            line(first_gain),
            speech_weight,
            inputs,
            normed_one,
            grad_projected,
            loss_row,
            post_sum,
            final_sum,
            second_gain_sum,
            second_shift_sum,
            hidden_sum,
            grad_table,
        ],
        [
            ((late_rows + 2 * SMALL_ROWS, model_width), BF16),
            ((late_rows, model_width), BF16),
            ((length, feat_width // cores), BF16),
            ((SMALL_ROWS, model_width), F32),
        ],
        [
            pltpu.VMEM((length, model_width), BF16),
            pltpu.VMEM((LANES, model_width), F32),
        ],
    )
    late = Wave(links, terms)
    late.sent = [late_sent, late_second_sent]
    late.kept = [late_kept, late_second_kept]
    early.add(0, 1, early_came[0])
    early.add(1, 1, early_came[1])
    early_came = [early.scatter(0, 2), early.scatter(1, 2)]
    early.add(0, 2, early_came[0])
    early.add(1, 2, early_came[1])
    early.join()
    feature_half = lax.all_to_all(
        feature_back.reshape(devices, part_len, feat_width // cores),
        "dp",
        split_axis=0,
        concat_axis=0,
        tiled=True,
    )[:rows_speech]
    other_feature = swap_cores(feature_half)
    feature_grad = jnp.concatenate(
        [
            jnp.where(core == 0, feature_half, other_feature),
            jnp.where(core == 0, other_feature, feature_half),
        ],
        axis=2,
    )
    late_came = [late.scatter(0, 0), late.scatter(1, 0)]
    late.add(0, 0, late_came[0])
    late_came[0] = late.scatter(0, 1)
    early.came_joined, late.kept[0] = tie(early.came_joined, late.kept[0])
    early.add_joined()
    early.gather_joined()
    late_came[1], early.joined = tie(late_came[1], early.joined)
    late.add(1, 0, late_came[1])
    late_came[1] = late.scatter(1, 1)
    late_came[0], late.kept[1] = tie(late_came[0], late.kept[1])
    late.add(0, 1, late_came[0])
    late_came[0] = late.scatter(0, 2)
    early.came_joined, late.kept[0] = tie(early.came_joined, late.kept[0])
    early.split_joined()
    early_came = early.gather(2)
    late_came[1], *early.shares = tie(late_came[1], *early.shares)
    late.add(1, 1, late_came[1])
    late_came[1] = late.scatter(1, 2)
    late_came[0], late.kept[1] = tie(late_came[0], late.kept[1])
    late.add(0, 2, late_came[0])
    late.add(1, 2, late_came[1])
    late.join()
    both = tie(*early_came, late.joined)
    early_came, late.joined = both[:2], both[2]
    early.place(2, early_came)
    early_came = early.gather(1)
    late.came_joined, *early.shares = tie(late.came_joined, *early.shares)
    late.add_joined()
    late.gather_joined()
    both = tie(*early_came, late.joined)
    early_came, late.joined = both[:2], both[2]
    early.place(1, early_came)
    early_came = early.gather(0)
    late.came_joined, *early.shares = tie(late.came_joined, *early.shares)
    late.split_joined()
    late.place(2, late.gather(2))
    late.place(1, late.gather(1))
    late_came = late.gather(0)
    both = tie(*early_came, *late.shares)
    early_came, late.shares = both[:2], both[2:]
    early_parts = early.place(0, early_came)
    late_parts = late.place(0, late_came)
    small = late.small
    first_rows = 7
    bias_rows = units // model_width
    loss_total = small[0, 0]
    grad_mel_bias = small[0, LANES : LANES + mel_width]
    grad_vocab_bias = small[0, 2 * LANES : 2 * LANES + vocab_size]
    grad_down_bias, grad_second_gain, grad_second_shift = small[1], small[2], small[3]
    grad_first_gain, grad_first_shift, grad_speech_bias = small[4], small[5], small[6]
    grad_up_bias = small[first_rows : first_rows + bias_rows].reshape(-1)
    table_start = first_rows + bias_rows
    grad_table = small[table_start : table_start + local_heads, :buckets].T

    grad_down = jnp.concatenate(
        [half[:unit_part].astype(F32) for half in early_parts[0]], axis=0
    )
    grad_up = jnp.concatenate(
        [unfold(half[post_end:], model_cut // 2).astype(F32) for half in early_parts[0]]
        + [half.astype(F32) for half in early_parts[1]],
        axis=0,
    )
    grad_post = jnp.concatenate([half[unit_part:post_end] for half in early_parts[0]], axis=0)
    model_part = model_width // 2
    value_part = model_part // 2
    grad_query = jnp.concatenate(
        [half[:model_part, :head_width].astype(F32) for half in late_parts[0]], axis=0
    )
    grad_key = jnp.concatenate(
        [half[:model_part, head_width:].astype(F32) for half in late_parts[0]], axis=0
    )
    grad_out = jnp.concatenate(
        [
            jnp.concatenate(
                [half[model_part:, :model_part], half[model_part:, model_part:]], axis=0
            ).astype(F32)
            for half in late_parts[0]
        ],
        axis=1,
    )
    grad_value = jnp.concatenate(
        [
            half[:value_part, columns].astype(F32)
            for half in late_parts[1]
            for columns in (slice(0, head_width), slice(head_width, 2 * head_width))
        ],
        axis=0,
    )
    hot_start = value_part + feat_width // 4
    shared = jnp.concatenate(
        [grad_post]
        + [half[value_part:hot_start] for half in late_parts[1]]
        + [half[hot_start:] for half in late_parts[1]],
        axis=0,
    )
    other = swap_cores(shared)
    low = jnp.where(core == 0, shared, other)
    high = jnp.where(core == 0, other, shared)
    grad_mel_weight = low[:mel_width].T.astype(F32)
    grad_vocab_weight = high[:vocab_size].T.astype(F32)
    from_half, to_half = LANES, LANES + feat_width // cores
    grad_speech_weight = jnp.concatenate(
        [low[from_half:to_half], high[from_half:to_half]], axis=0
    ).astype(F32)
    grad_token_table = jnp.concatenate([low[to_half:], high[to_half:]], axis=0)[
        :vocab_size
    ].astype(F32)
    return (
        loss_total / rows_total,
        feature_grad,
        grad_speech_weight,
        grad_speech_bias,
        grad_token_table,
        grad_first_gain,
        grad_first_shift,
        grad_query,
        grad_key,
        grad_value,
        grad_table,
        grad_out,
        grad_second_gain,
        grad_second_shift,
        grad_up,
        grad_up_bias,
        grad_down,
        grad_down_bias,
        grad_mel_weight,
        grad_mel_bias,
        grad_vocab_weight,
        grad_vocab_bias,
    )


def solution(mesh):
    placed = (
        P(None, "dp", None),
        P(None, "dp"),
        P(None, "dp", None),
        P(None, "dp"),
        P(),
        P(),
        P(),
        P(),
        P(),
        P(),
        P(),
        P(),
        P(None, "mp"),
        P(None, "mp"),
        P(None, "mp"),
        P(None, "mp"),
        P("mp", None),
        P(),
        P(),
        P(None, "mp"),
        P("mp"),
        P("mp", None),
        P(),
        P(),
        P(),
        P(),
        P(),
    )
    return jax.shard_map(
        per_device,
        mesh=mesh,
        in_specs=placed,
        out_specs=(
            P(),
            P(None, "dp", None),
            P(),
            P(),
            P(),
            P(),
            P(),
            P(None, "mp"),
            P(None, "mp"),
            P(None, "mp"),
            P(None, "mp"),
            P("mp", None),
            P(),
            P(),
            P(None, "mp"),
            P("mp"),
            P("mp", None),
            P(),
            P(),
            P(),
            P(),
            P(),
        ),
        check_vma=False,
    )
```

```python
import functools

import jax
import jax.numpy as jnp
from jax import lax
from jax.experimental import pallas as pl
from jax.experimental.pallas import tpu as pltpu
from jax.sharding import PartitionSpec as P

EPSILON = 1e-05
NEGATIVE = -1e30
HIGHEST = lax.Precision.HIGHEST
BF16 = jnp.bfloat16
F32 = jnp.float32
LANES = 128
SMALL_ROWS = 16


def contract_rows(left_side, right_side):
    return lax.dot_general(
        left_side, right_side, (((0,), (0,)), ((), ())), preferred_element_type=F32
    )


def times_transposed(left_side, right_side):
    return lax.dot_general(
        left_side, right_side, (((1,), (1,)), ((), ())), preferred_element_type=F32
    )


def matmul(left_side, right_side):
    return jnp.dot(left_side, right_side, preferred_element_type=F32)


def normalize(row_data):
    center = row_data - jnp.mean(row_data, axis=-1, keepdims=True)
    inverse = lax.rsqrt(jnp.mean(center * center, axis=-1, keepdims=True) + EPSILON)
    return center * inverse, inverse


def norm_back(grad_out, normal, inverse, norm_gain):
    scaled = grad_out * norm_gain
    return inverse * (
        scaled
        - jnp.mean(scaled, axis=-1, keepdims=True)
        - normal * jnp.mean(scaled * normal, axis=-1, keepdims=True)
    )


def column_sum(array):
    return jnp.sum(array, axis=0, keepdims=True)


def cost(microseconds):
    return pl.CostEstimate(
        flops=0, bytes_accessed=int(microseconds * 3.5e6), transcendentals=0
    )


class Fetched:
    def __init__(self, source, target, semaphore):
        self.copy = pltpu.make_async_copy(source, target, semaphore)
        self.target = target
        self.begun = False
        self.waited = False
        self.shape = target.shape

    def begin(self):
        if not self.begun:
            self.copy.start()
            self.begun = True

    def ready(self):
        self.begin()
        if not self.waited:
            self.copy.wait()
            self.waited = True
        return self.target

    def __getitem__(self, places):
        return self.ready()[places]


class Stored:
    def __init__(self, target, source, semaphore):
        self.copy = pltpu.make_async_copy(source, target, semaphore)
        self.source = source
        self.started = False
        self.shape = source.shape

    def __getitem__(self, places):
        return self.source[places]

    def __setitem__(self, places, value):
        self.source[places] = value

    def flush(self):
        if not self.started:
            self.copy.start()
            self.started = True


def run_kernel(
    kernel, name, microseconds, flags, operands, outputs, scratch=(), mebibytes=16, after=()
):
    in_place = pl.BlockSpec(memory_space=pltpu.VMEM)
    distant = pl.BlockSpec(memory_space=pltpu.HBM)
    far = [isinstance(operand, tuple) for operand in operands]
    arrays = [
        pltpu.with_memory_space_constraint(operand[1], pltpu.HBM) if is_far else operand
        for operand, is_far in zip(operands, far)
    ]
    out_far = [len(output) == 3 and output[2] == "far" for output in outputs]
    copied = {output[2]: place for place, output in enumerate(outputs) if len(output) == 3}
    fetched = [
        pltpu.VMEM(array.shape, array.dtype)
        for place, (array, is_far) in enumerate(zip(arrays, far))
        if is_far and place not in copied
    ]
    stored = [
        pltpu.VMEM(output[0], output[1]) for output, is_far in zip(outputs, out_far) if is_far
    ]
    moves = sum(far) + sum(out_far)
    semaphores = [pltpu.SemaphoreType.DMA((moves,))] if moves else []

    def with_moves(*refs):
        refs = list(refs)
        semaphore = refs.pop() if moves else None
        buffers = refs[len(refs) - len(fetched) - len(stored) :]
        refs = refs[: len(refs) - len(fetched) - len(stored)]
        first_out = 1 + len(arrays) + len(after)
        count = 0
        came = []
        for place, is_far in enumerate(far):
            if is_far:
                target = refs[first_out + copied[place]] if place in copied else buffers.pop(0)
                refs[place + 1] = Fetched(refs[place + 1], target, semaphore.at[count])
                if operands[place][0] == "far":
                    refs[place + 1].begin()
                came.append(refs[place + 1])
                count += 1
        kept = []
        for place, is_far in enumerate(out_far):
            if is_far:
                refs[first_out + place] = Stored(
                    refs[first_out + place], buffers.pop(0), semaphore.at[count]
                )
                kept.append(refs[first_out + place])
                count += 1
        token_ref = refs[first_out + len(outputs)]
        token_ref[...] = jnp.zeros_like(token_ref)
        kernel(
            *refs[: 1 + len(arrays)],
            *refs[first_out : first_out + len(outputs)],
            *refs[first_out + len(outputs) + 1 :],
        )
        for ref in kept:
            ref.flush()
        for ref in came:
            ref.ready()
        for ref in kept:
            ref.copy.wait()

    *results, token = pl.pallas_call(
        with_moves,
        in_specs=[pl.BlockSpec(memory_space=pltpu.SMEM)]
        + [distant if is_far else in_place for is_far in far]
        + [pl.BlockSpec(memory_space=pl.ANY)] * len(after),
        out_specs=[distant if is_far else in_place for is_far in out_far] + [in_place],
        out_shape=[
            pltpu.HBM(output[0], output[1])
            if is_far
            else jax.ShapeDtypeStruct(output[0], output[1])
            for output, is_far in zip(outputs, out_far)
        ]
        + [jax.ShapeDtypeStruct((8, LANES), F32)],
        scratch_shapes=list(scratch) + fetched + stored + semaphores,
        compiler_params=pltpu.CompilerParams(vmem_limit_bytes=mebibytes * 1024 * 1024),
        cost_estimate=cost(microseconds),
        name=name,
    )(flags, *arrays, *after)
    return results, token


def far(array):
    return ("far", array)


def later(array):
    return ("later", array)


def begin(*refs):
    for ref in refs:
        ref.begin()


def blocks_of(length, size):
    return [slice(start, start + size) for start in range(0, length, size)]


def times_hot(left_side, hot, dims):
    total = 0.0
    for _ in range(3):
        term = left_side.astype(BF16)
        total += lax.dot_general(term, hot, (dims, ((), ())), preferred_element_type=F32)
        left_side = left_side - term.astype(F32)
    return total


def window_kernel(flags_ref, bucket_ref, table_ref, window_ref):
    heads, buckets = table_ref.shape
    width = bucket_ref.shape[1]
    places = lax.broadcasted_iota(jnp.int32, (buckets, width), 0)
    hot = jnp.where(places == bucket_ref[...], 1.0, 0.0).astype(BF16)
    offsets = times_hot(table_ref[...], hot, ((1,), (0,)))
    for head in range(heads):
        spread = jnp.broadcast_to(offsets[head : head + 1, :], (LANES, width))
        window_ref[head] = pltpu.roll(spread, width - LANES + 1, 1, stride=1, stride_axis=0)


def pack_kernel(flags_ref, features_ref, target_ref, ids_ref, sent_ref):
    core_width = sent_ref.shape[2]
    rest = features_ref.shape[2] - core_width
    mel_width = target_ref.shape[2]
    sent_ref[...] = jnp.zeros_like(sent_ref)

    @pl.when(flags_ref[0] == 0)
    def _():
        for row in range(features_ref.shape[0]):
            sent_ref[2 * row] = features_ref[row, :, :core_width]

    @pl.when(flags_ref[0] != 0)
    def _():
        for row in range(features_ref.shape[0]):
            sent_ref[2 * row, :, :rest] = features_ref[row, :, core_width:]
            sent_ref[2 * row, :, rest : rest + mel_width] = target_ref[row]
            start = rest + mel_width
            sent_ref[2 * row + 1, :, start : start + 2] = ids_ref[row]


def key_probs(keys, queries, window_ref, head, mask_ref):
    length = keys.shape[0]
    blocks = length // LANES
    bias = jnp.concatenate(
        [
            window_ref[head, :, LANES * (blocks - 1 - b) : LANES * (blocks - 1 - b) + length]
            for b in range(blocks)
        ],
        axis=0,
    )
    scores = times_transposed(keys, queries) + bias + mask_ref[...]
    powers = jnp.exp(scores - jnp.max(scores, axis=0, keepdims=True))
    return powers * (1.0 / column_sum(powers))


SPEECH_BIAS, FIRST_GAIN, FIRST_SHIFT, SECOND_GAIN, SECOND_SHIFT, UP_BIAS, DOWN_BIAS, POST_BIAS = range(8)


def vector(ref, row, width):
    return ref[row : row + 1, :width]


def attend_kernel(
    head_size,
    plain_width,
    flags_ref,
    own_ref,
    other_ref,
    speech_weight_ref,
    token_table_ref,
    vectors_ref,
    query_weight_ref,
    key_weight_ref,
    value_weight_ref,
    out_weight_ref,
    window_ref,
    column_ref,
    row_ref,
    embedded_ref,
    attended_ref,
    embedded_far_ref,
    normed_ref,
    queries_ref,
    keys_ref,
    values_ref,
    heads_ref,
    inputs_ref,
    extra_ref,
    mask_ref,
):
    length, half_width = own_ref.shape
    width = embedded_ref.shape[1]
    feat_width = inputs_ref.shape[1] - LANES
    first = flags_ref[0] == 0
    speech = flags_ref[1].astype(F32)
    scaling = jnp.asarray(head_size ** (-0.5), BF16)
    for rows in blocks_of(length, LANES):
        own, other = own_ref[rows, :], other_ref[rows, :]
        low = jnp.where(first, own, other)
        high = jnp.where(first, other, own)
        inputs_ref[rows, :half_width] = low
        inputs_ref[rows, half_width:feat_width] = high[:, : feat_width - half_width]
        extra = high[:, feat_width - half_width : feat_width - half_width + LANES]
        extra_ref[rows, :] = extra
        ids = extra[:, plain_width - feat_width : plain_width - feat_width + 1].astype(F32)
        places = lax.broadcasted_iota(jnp.int32, (LANES, LANES), 1).astype(F32)
        hot = jnp.where(ids == places, 1.0 - speech, 0.0)
        inputs_ref[rows, feat_width:] = hot.astype(BF16)
    inputs_ref.flush()
    speech_weight, token_table = speech_weight_ref.ready(), token_table_ref.ready()
    vectors = vectors_ref.ready()
    for rows in blocks_of(length, 2 * LANES):
        embedded = (
            matmul(inputs_ref[rows, :feat_width], speech_weight[...])
            + matmul(inputs_ref[rows, feat_width:], token_table[...])
            + vector(vectors, SPEECH_BIAS, width) * speech
        ).astype(BF16)
        embedded_ref[rows, :] = embedded
        embedded_far_ref[rows, :] = embedded
        normal, _ = normalize(embedded.astype(F32))
        normed_ref[rows, :] = (
            normal * vector(vectors, FIRST_GAIN, width) + vector(vectors, FIRST_SHIFT, width)
        ).astype(BF16)
    embedded_far_ref.flush()
    normed_ref.flush()
    query_weight, key_weight = query_weight_ref.ready(), key_weight_ref.ready()
    value_weight = value_weight_ref.ready()
    for rows in blocks_of(length, 2 * LANES):
        normed = normed_ref[rows, :]
        queries_ref[rows, :] = matmul(normed, query_weight[...]).astype(BF16) * scaling
        keys_ref[rows, :] = matmul(normed, key_weight[...]).astype(BF16)
        values_ref[rows, :] = matmul(normed, value_weight[...]).astype(BF16)
    queries_ref.flush()
    keys_ref.flush()
    values_ref.flush()
    mask_ref[...] = jnp.where(column_ref[...] == row_ref[...], 0.0, NEGATIVE)
    window = window_ref.ready()
    for head, columns in enumerate(blocks_of(queries_ref.shape[1], head_size)):
        probs = key_probs(
            keys_ref[:, columns], queries_ref[:, columns], window, head, mask_ref
        ).astype(BF16)
        heads_ref[:, columns] = contract_rows(probs, values_ref[:, columns]).astype(BF16)
    heads_ref.flush()
    out_weight = out_weight_ref.ready()
    for rows in blocks_of(length, 2 * LANES):
        attended_ref[rows, :] = matmul(heads_ref[rows, :], out_weight[...]).astype(BF16)


def forward_kernel(
    flags_ref,
    embedded_ref,
    own_ref,
    other_ref,
    vectors_ref,
    up_weight_ref,
    down_weight_ref,
    mixed_ref,
    slope_ref,
    branch_ref,
    mixed_far_ref,
    normed_ref,
    active_ref,
):
    length, width = embedded_ref.shape
    units = active_ref.shape[1]
    vectors = vectors_ref.ready()
    for rows in blocks_of(length, 2 * LANES):
        mixed = embedded_ref[rows, :].astype(F32) + (
            own_ref[rows, :].astype(F32) + other_ref[rows, :].astype(F32)
        )
        mixed_ref[rows, :] = mixed
        mixed_far_ref[rows, :] = mixed
        normal, _ = normalize(mixed)
        normed_ref[rows, :] = (
            normal * vector(vectors, SECOND_GAIN, width) + vector(vectors, SECOND_SHIFT, width)
        ).astype(BF16)
    mixed_far_ref.flush()
    for rows in blocks_of(length, 2 * LANES):
        hidden = matmul(normed_ref[rows, :], up_weight_ref[...]) + vector(vectors, UP_BIAS, units)
        square = hidden * hidden
        inner = 0.7978845608028654 * hidden * (1.0 + 0.044715 * square)
        curve = jnp.tanh(inner)
        half = 0.5 * (1.0 + curve)
        active = (hidden * half).astype(BF16)
        active_ref[rows, :] = active
        slope_ref[rows, :] = half + 0.5 * hidden * (1.0 - curve * curve) * (
            0.7978845608028654 * (1.0 + 0.134145 * square)
        )
        branch_ref[rows, :] = matmul(active, down_weight_ref[...]).astype(BF16)


def loss_kernel(
    mel_width,
    vocab_size,
    flags_ref,
    mixed_ref,
    own_ref,
    other_ref,
    vectors_ref,
    mel_weight_ref,
    vocab_weight_ref,
    extra_ref,
    slope_ref,
    up_weight_ref,
    down_weight_ref,
    active_ref,
    normed_ref,
    first_ref,
    second_ref,
    first_kept_ref,
    second_kept_ref,
    grad_normed_ref,
    grad_final_far_ref,
    final_ref,
    grad_post_ref,
    sums_ref,
    post_weight_ref,
    grad_final_ref,
    grad_hidden_ref,
):
    length, width = mixed_ref.shape
    units = slope_ref.shape[1]
    speech = flags_ref[1].astype(F32)
    mel_scale = speech * (1.0 / (mel_width * length))
    text_scale = (1.0 - speech) * (1.0 / length)
    vectors = vectors_ref.ready()
    post_weight_ref[:LANES, :] = mel_weight_ref[...]
    post_weight_ref[LANES:, :] = vocab_weight_ref[...]
    totals = None
    for rows in blocks_of(length, 2 * LANES):
        final = mixed_ref[rows, :] + (
            own_ref[rows, :].astype(F32) + other_ref[rows, :].astype(F32)
        )
        final = (final + vector(vectors, DOWN_BIAS, width)).astype(BF16)
        final_ref[rows, :] = final
        results = times_transposed(final, post_weight_ref[...])
        results += vector(vectors, POST_BIAS, 2 * LANES)
        extra = extra_ref[rows, :].astype(F32)
        places = lax.broadcasted_iota(jnp.int32, extra.shape, 1)
        error = jnp.where(places < mel_width, results[:, :LANES] - extra, 0.0)
        smooth = jnp.sqrt(error * error + 1.0)
        grad_mel = error / smooth * mel_scale
        logits = jnp.where(places < vocab_size, results[:, LANES:], NEGATIVE)
        shifted = logits - jnp.max(logits, axis=-1, keepdims=True)
        powers = jnp.exp(shifted)
        power_sum = jnp.sum(powers, axis=-1, keepdims=True)
        label = extra[:, mel_width + 1 : mel_width + 2] == places.astype(F32)
        picked = jnp.sum(jnp.where(label, shifted, 0.0), axis=-1, keepdims=True)
        text_loss = column_sum(jnp.log(power_sum) - picked) * text_scale
        mel_loss = column_sum((smooth - 1.0) * mel_scale)
        loss = mel_loss + jnp.where(places[:1] == 0, text_loss, 0.0)
        grad_text = (powers / power_sum - jnp.where(label, 1.0, 0.0)) * text_scale
        grad_post = jnp.concatenate([grad_mel, grad_text], axis=1).astype(BF16)
        grad_post_ref[rows, :] = grad_post
        grad_final = matmul(grad_post, post_weight_ref[...]).astype(BF16)
        grad_final_ref[rows, :] = grad_final
        grad_final_far_ref[rows, :] = grad_final
        sums = (loss, column_sum(grad_post.astype(F32)), column_sum(grad_final.astype(F32)))
        totals = sums if totals is None else [a + b for a, b in zip(totals, sums)]
    final_ref.flush()
    grad_post_ref.flush()
    grad_final_far_ref.flush()
    hidden_sum = 0.0
    for rows in blocks_of(length, 2 * LANES):
        grad_active = times_transposed(grad_final_ref[rows, :], down_weight_ref[...])
        grad_hidden = (slope_ref[rows, :] * grad_active).astype(BF16)
        grad_hidden_ref[rows, :] = grad_hidden
        hidden_sum += column_sum(grad_hidden.astype(F32))
        grad_normed_ref[rows, :] = times_transposed(grad_hidden, up_weight_ref[...]).astype(BF16)
    sums_ref[...] = jnp.zeros(sums_ref.shape, F32)
    sums_ref[0:1, :LANES] = jnp.broadcast_to(
        jnp.sum(totals[0], axis=1, keepdims=True), (1, LANES)
    )
    sums_ref[0:1, LANES : 3 * LANES] = totals[1]
    sums_ref[1:2, :width] = totals[2]
    sums_ref[2:3, :] = hidden_sum
    sums_ref.flush()
    cut = width // 3
    for first_half, second_half, first, second in (
        (flags_ref[2], flags_ref[3], first_ref, second_ref),
        (1 - flags_ref[2], 1 - flags_ref[3], first_kept_ref, second_kept_ref),
    ):
        count = (width - cut) // 2
        grad_up = contract_rows(
            wide(normed_ref, cut + second_half * count, count), grad_hidden_ref[...]
        )
        store_folded(second, 0, grad_up)
        second.flush()
        count = units // 2
        first[:count, :] = contract_rows(
            wide(active_ref, first_half * count, count), grad_final_ref[...]
        ).astype(BF16)
        grad_up = contract_rows(
            wide(normed_ref, first_half * (cut // 2), cut // 2), grad_hidden_ref[...]
        )
        store_folded(first, count, grad_up)
        first.flush()


def store_folded(ref, start, array):
    for columns in blocks_of(array.shape[1], ref.shape[1]):
        ref[start : start + array.shape[0], :] = array[:, columns].astype(BF16)
        start += array.shape[0]


def wide(ref, start, size):
    return ref[:, pl.ds(pl.multiple_of(start, LANES), size)]


def back_kernel(
    head_size,
    flags_ref,
    own_ref,
    other_ref,
    mixed_ref,
    grad_final_ref,
    vectors_ref,
    out_weight_ref,
    queries_ref,
    keys_ref,
    values_ref,
    window_ref,
    column_ref,
    row_ref,
    query_weight_ref,
    key_weight_ref,
    value_weight_ref,
    normed_ref,
    heads_ref,
    grad_post_ref,
    final_ref,
    grad_normed_ref,
    sent_ref,
    kept_ref,
    grad_mixed_ref,
    post_sent_ref,
    post_kept_ref,
    grad_offsets_ref,
    sums_ref,
    grad_low_ref,
    grad_heads_ref,
    grad_projected_ref,
    mask_ref,
    probs_ref,
    scores_ref,
    window_sum_ref,
    post_ref,
):
    length, head_width = queries_ref.shape
    width = grad_low_ref.shape[1]
    blocks = length // LANES
    mixed, grad_final, vectors = mixed_ref.ready(), grad_final_ref.ready(), vectors_ref.ready()
    out_weight = out_weight_ref.ready()
    gain_sum, shift_sum = 0.0, 0.0
    for rows in blocks_of(length, 2 * LANES):
        grad_normed = own_ref[rows, :].astype(F32) + other_ref[rows, :].astype(F32)
        normal, inverse = normalize(mixed[rows, :])
        gain_sum += column_sum(grad_normed * normal)
        shift_sum += column_sum(grad_normed)
        grad_mixed = grad_final[rows, :].astype(F32) + norm_back(
            grad_normed, normal, inverse, vector(vectors, SECOND_GAIN, width)
        )
        grad_mixed_ref[rows, :] = grad_mixed
        grad_low = grad_mixed.astype(BF16)
        grad_low_ref[rows, :] = grad_low
        grad_heads_ref[rows, :] = times_transposed(grad_low, out_weight[...]).astype(BF16)
    grad_mixed_ref.flush()
    sums_ref[...] = jnp.zeros(sums_ref.shape, F32)
    sums_ref[0:1, :] = gain_sum
    sums_ref[1:2, :] = shift_sum
    sums_ref.flush()
    mask_ref[...] = jnp.where(column_ref[...] == row_ref[...], 0.0, NEGATIVE)
    queries_ref, keys_ref, values_ref = queries_ref.ready(), keys_ref.ready(), values_ref.ready()
    window = window_ref.ready()
    scaling = head_size ** (-0.5)
    for head, columns in enumerate(blocks_of(head_width, head_size)):
        keys, queries = keys_ref[:, columns], queries_ref[:, columns]
        grads = grad_heads_ref[:, columns]
        probs = key_probs(keys, queries, window, head, mask_ref)
        weighted = probs * times_transposed(values_ref[:, columns], grads)
        grad_scores = weighted - probs * column_sum(weighted)
        probs_ref[...] = probs.astype(BF16)
        scores_ref[...] = grad_scores.astype(BF16)
        window_sum_ref[...] = jnp.zeros_like(window_sum_ref)
        for block in range(blocks):
            start = LANES * (blocks - 1 - block)
            window_sum_ref[:, start : start + length] += grad_scores[
                LANES * block : LANES * (block + 1)
            ]
        start = head * head_size
        for kind, value in enumerate(
            (
                contract_rows(scores_ref[...], keys) * scaling,
                matmul(scores_ref[...], queries),
                matmul(probs_ref[...], grads),
            )
        ):
            grad_projected_ref[
                :, kind * head_width + start : kind * head_width + start + head_size
            ] = value.astype(BF16)
        diagonal = window_sum_ref[...]
        half = LANES // 2
        while half >= 1:
            diagonal = pltpu.roll(diagonal[:half], half, 1) + diagonal[half:]
            half //= 2
        grad_offsets_ref[head : head + 1, :] = diagonal
    grad_offsets_ref.flush()
    for rows in blocks_of(length, 2 * LANES):
        total = 0.0
        for kind, weight_ref in enumerate((query_weight_ref, key_weight_ref, value_weight_ref)):
            total += times_transposed(
                grad_projected_ref[rows, kind * head_width : (kind + 1) * head_width],
                weight_ref.ready()[...],
            )
        grad_normed_ref[rows, :] = total.astype(BF16)
    normed, heads = normed_ref.ready(), heads_ref.ready()
    grad_post, final = grad_post_ref.ready(), final_ref.ready()
    half = width // 2
    count = head_width // 2
    post_rows = LANES // 2
    post_ref[...] = contract_rows(wide(grad_post, flags_ref[0] * LANES, LANES), final[...])
    for first_ref, post_half_ref, first, second in (
        (sent_ref, post_sent_ref, flags_ref[2], flags_ref[3]),
        (kept_ref, post_kept_ref, 1 - flags_ref[2], 1 - flags_ref[3]),
    ):
        post_half_ref[...] = post_ref[
            pl.ds(pl.multiple_of(second * post_rows, post_rows), post_rows), :
        ].astype(BF16)
        post_half_ref.flush()
        grad_project = contract_rows(
            wide(normed, first * half, half), grad_projected_ref[...]
        ).astype(BF16)
        first_ref[:half, :] = grad_project[:, : 2 * head_width]
        first_ref[half : half + count, :head_width] = grad_project[:count, 2 * head_width :]
        first_ref[half : half + count, head_width:] = grad_project[count:, 2 * head_width :]
        grad_out = contract_rows(heads[...], wide(grad_low_ref, first * half, half))
        first_ref[half + count :, :half] = grad_out[:count].astype(BF16)
        first_ref[half + count :, half:] = grad_out[count:].astype(BF16)
        first_ref.flush()


def input_kernel(
    flags_ref,
    own_ref,
    other_ref,
    embedded_ref,
    grad_mixed_ref,
    vectors_ref,
    speech_weight_ref,
    inputs_ref,
    post_sent_ref,
    post_kept_ref,
    loss_sums_ref,
    back_sums_ref,
    grad_offsets_ref,
    bucket_ref,
    sent_ref,
    kept_ref,
    feature_back_ref,
    terms_ref,
    grad_embedded_ref,
    hot_ref,
):
    length, width = own_ref.shape
    embedded, grad_mixed = embedded_ref.ready(), grad_mixed_ref.ready()
    vectors, speech_weight = vectors_ref.ready(), speech_weight_ref.ready()
    feat_width = speech_weight.shape[0]
    core_width = feat_width // 2
    speech = flags_ref[1].astype(F32)
    core = flags_ref[0]
    gain_sum, shift_sum, bias_sum = 0.0, 0.0, 0.0
    core_weight = speech_weight[pl.ds(pl.multiple_of(core * core_width, core_width), core_width), :]
    for rows in blocks_of(length, 2 * LANES):
        grad_normed = own_ref[rows, :].astype(F32) + other_ref[rows, :].astype(F32)
        normal, inverse = normalize(embedded[rows, :].astype(F32))
        gain_sum += column_sum(grad_normed * normal)
        shift_sum += column_sum(grad_normed)
        grad_embedded = (
            grad_mixed[rows, :]
            + norm_back(grad_normed, normal, inverse, vector(vectors, FIRST_GAIN, width))
        ).astype(BF16)
        grad_embedded_ref[rows, :] = grad_embedded
        bias_sum += column_sum(grad_embedded.astype(F32))
        feature_back_ref[rows, :] = times_transposed(grad_embedded, core_weight).astype(BF16)
    inputs = inputs_ref.ready()
    hot_ref[...] = contract_rows(inputs[:, feat_width:], grad_embedded_ref[...])
    post_rows = LANES // 2
    feat_rows = core_width // 2
    hot_rows = LANES // 4
    small_rows = 2 * SMALL_ROWS
    for which_ref, post_ref, half, base in (
        (sent_ref, post_sent_ref, flags_ref[3], small_rows),
        (kept_ref, post_kept_ref, 1 - flags_ref[3], 0),
    ):
        which_ref[base : base + post_rows, :] = post_ref[...]
        start = base + post_rows
        which_ref[start : start + feat_rows, :] = contract_rows(
            wide(inputs, core * core_width + half * feat_rows, feat_rows), grad_embedded_ref[...]
        ).astype(BF16)
        start += feat_rows
        which_ref[start : start + hot_rows, :] = hot_ref[
            pl.ds(pl.multiple_of(core * 2 * hot_rows + half * hot_rows, hot_rows), hot_rows), :
        ].astype(BF16)
        which_ref[start + hot_rows :, :] = jnp.zeros((hot_rows, width), BF16)
    loss_sums, back_sums = loss_sums_ref.ready(), back_sums_ref.ready()
    bias_rows = loss_sums.shape[1] // width
    rows = [loss_sums[0:1, :width], loss_sums[1:2, :width], back_sums[0:1, :], back_sums[1:2, :]]
    rows += [gain_sum, shift_sum, bias_sum * speech]
    rows += [loss_sums[2:3, part * width : (part + 1) * width] for part in range(bias_rows)]
    terms_ref[...] = jnp.zeros_like(terms_ref)
    for place, row in enumerate(rows):
        terms_ref[place : place + 1, :] = row
    start = len(rows)
    heads, offset_count = grad_offsets_ref.shape
    places = lax.broadcasted_iota(jnp.int32, (width // 2, offset_count), 0)
    hot = jnp.where(places == bucket_ref[...], 1.0, 0.0).astype(BF16)
    terms_ref[start : start + heads, : width // 2] = times_hot(
        grad_offsets_ref[...], hot, ((1,), (1,))
    )
    terms = terms_ref[...]
    high = terms.astype(BF16)
    rest = (terms - high.astype(F32)).astype(BF16)
    terms_ref[...] = high.astype(F32) + rest.astype(F32)
    sent_ref[:SMALL_ROWS, :] = high
    sent_ref[SMALL_ROWS:small_rows, :] = rest


def rows_at(ref, start, count):
    return ref[pl.ds(pl.multiple_of(start, 16), count), :]


def add_low(left_side, right_side):
    return (left_side.astype(F32) + right_side.astype(F32)).astype(BF16)


def add_small(terms_ref, came_ref):
    return terms_ref[...] + (
        came_ref[:SMALL_ROWS, :].astype(F32)
        + came_ref[SMALL_ROWS : 2 * SMALL_ROWS, :].astype(F32)
    )


def send_small(small, sent_ref, terms_ref):
    high = small.astype(BF16)
    rest = (small - high.astype(F32)).astype(BF16)
    sent_ref[:SMALL_ROWS, :] = high
    sent_ref[SMALL_ROWS : 2 * SMALL_ROWS, :] = rest
    terms_ref[...] = high.astype(F32) + rest.astype(F32)


def add_kernel(with_small, mine_ref, kept_ref, came_ref, *refs):
    half = kept_ref.shape[0] // 2
    base = 0
    if with_small:
        base = 2 * SMALL_ROWS
        terms_ref, sent_ref, next_ref, new_terms_ref = refs
        send_small(add_small(terms_ref, came_ref), sent_ref, new_terms_ref)
    else:
        sent_ref, next_ref = refs
    mine = mine_ref[0]
    start = (1 - mine) * half
    sent_ref[base:, :] = add_low(
        rows_at(kept_ref, start, half), rows_at(came_ref, base + start, half)
    )
    sent_ref.flush()
    start = mine * half
    next_ref[...] = add_low(
        rows_at(kept_ref, start, half), rows_at(came_ref, base + start, half)
    )


def finish_kernel(with_small, mine_ref, kept_ref, came_ref, *refs):
    base = 0
    if with_small:
        base = 2 * SMALL_ROWS
        terms_ref, total_far_ref, total_ref, small_ref = refs
        small_ref[...] = add_small(terms_ref, came_ref)
    else:
        total_far_ref, total_ref = refs
    total = add_low(kept_ref[...], came_ref[base:, :])
    total_far_ref[...] = total
    total_far_ref.flush()
    total_ref[...] = total


def place_kernel(mine_ref, own_ref, came_ref, out_far_ref, out_ref):
    half = own_ref.shape[0]
    mine = pl.ds(pl.multiple_of(mine_ref[0] * half, 16), half)
    other = pl.ds(pl.multiple_of((1 - mine_ref[0]) * half, 16), half)
    for ref in (out_far_ref, out_ref):
        ref[mine, :] = own_ref[...]
        ref[other, :] = came_ref[...]
    out_far_ref.flush()


def early_place_kernel(
    flags_ref, first_ref, first_came_ref, second_ref, second_came_ref, down_ref, up_ref
):
    width = down_ref.shape[1]
    units = down_ref.shape[0] // 2
    cut = width // 3
    for parts, halves in (
        ((first_ref, second_ref), (flags_ref[0], flags_ref[1])),
        ((first_came_ref, second_came_ref), (1 - flags_ref[0], 1 - flags_ref[1])),
    ):
        down_ref[pl.ds(pl.multiple_of(halves[0] * units, units), units), :] = parts[0][
            :units, :
        ].astype(F32)
        for part, half, start, first_row, count in (
            (parts[0], halves[0], units, 0, cut // 2),
            (parts[1], halves[1], 0, cut, (width - cut) // 2),
        ):
            place = pl.ds(pl.multiple_of(first_row + half * count, LANES), count)
            for columns in blocks_of(up_ref.shape[1], width):
                up_ref[place, columns] = part[start : start + count, :].astype(F32)
                start += count


def late_place_kernel(flags_ref, first_ref, first_came_ref, query_ref, key_ref, value_ref, out_ref):
    width = first_ref.shape[1]
    head_width = query_ref.shape[1]
    half = width // 2
    count = head_width // 2
    for first, first_half in ((first_ref, flags_ref[0]), (first_came_ref, 1 - flags_ref[0])):
        place = pl.ds(pl.multiple_of(first_half * half, LANES), half)
        query_ref[place, :] = first[:half, :head_width].astype(F32)
        key_ref[place, :] = first[:half, head_width:].astype(F32)
        for part in range(2):
            columns = slice(part * head_width, (part + 1) * head_width)
            rows = pl.ds(pl.multiple_of(first_half * half + part * count, 16), count)
            value_ref[rows, :] = first[half : half + count, columns].astype(F32)
            columns = slice(part * half, (part + 1) * half)
            out_ref[part * count : (part + 1) * count, place] = first[
                half + count :, columns
            ].astype(F32)


def small_kernel(
    rows,
    terms_ref,
    loss_ref,
    mel_ref,
    vocab_ref,
    down_ref,
    gain_two_ref,
    shift_two_ref,
    gain_one_ref,
    shift_one_ref,
    speech_ref,
    up_ref,
    table_ref,
):
    width = down_ref.shape[0]
    loss_ref[...] = terms_ref[0:1, 0:1] * (1.0 / rows)
    mel_ref[...] = terms_ref[0, LANES : LANES + mel_ref.shape[0]]
    vocab_ref[...] = terms_ref[0, 2 * LANES : 2 * LANES + vocab_ref.shape[0]]
    row = 1
    for ref in (down_ref, gain_two_ref, shift_two_ref, gain_one_ref, shift_one_ref, speech_ref):
        ref[...] = terms_ref[row, :]
        row += 1
    for columns in blocks_of(up_ref.shape[0], width):
        up_ref[columns] = terms_ref[row, :]
        row += 1
    table_ref[...] = terms_ref[row : row + table_ref.shape[0], : table_ref.shape[1]]


def shared_place_kernel(
    flags_ref,
    own_ref,
    own_other_ref,
    came_ref,
    came_other_ref,
    speech_ref,
    table_ref,
    mel_ref,
    vocab_ref,
    post_ref,
    hot_ref,
):
    core = flags_ref[2]
    post_rows = LANES // 2
    feat_rows = speech_ref.shape[0] // 4
    hot_rows = LANES // 4
    for ref, place, half in (
        (own_ref, core, flags_ref[1]),
        (came_ref, core, 1 - flags_ref[1]),
        (own_other_ref, 1 - core, flags_ref[1]),
        (came_other_ref, 1 - core, 1 - flags_ref[1]),
    ):
        spot = pl.multiple_of(place * LANES + half * post_rows, 16)
        post_ref[pl.ds(spot, post_rows), :] = ref[:post_rows, :].astype(F32)
        start = post_rows
        spot = pl.multiple_of((place * 2 + half) * feat_rows, 16)
        speech_ref[pl.ds(spot, feat_rows), :] = ref[start : start + feat_rows, :].astype(F32)
        start += feat_rows
        spot = pl.multiple_of((place * 2 + half) * hot_rows, 16)
        hot_ref[pl.ds(spot, hot_rows), :] = ref[start : start + hot_rows, :].astype(F32)
    table_ref[...] = hot_ref[: table_ref.shape[0], :]
    mel_ref[...] = post_ref[: mel_ref.shape[0], :]
    vocab_ref[...] = post_ref[LANES : LANES + vocab_ref.shape[0], :]


def swap_cores(array):
    return lax.ppermute(array, "mp", [(0, 1), (1, 0)])


ORDERS = (((0, 1, 2, 3), (1, 2, 0, 3)), ((2, 0, 1, 3), (2, 0, 1, 3)))
STEPS = 4


class Links:
    def __init__(self, devices, cores, index, core):
        self.devices, self.cores, self.index, self.core = devices, cores, index, core
        self.bits = devices.bit_length() - 1
        self.token = None
        self.pending = []

    def exchange(self, array, directions):
        pairs = [
            (
                place * self.cores + core,
                (place ^ (1 << directions[core])) * self.cores + core,
            )
            for place in range(self.devices)
            for core in range(self.cores)
        ]
        return lax.ppermute(array, ("dp", "mp"), pairs)

    def mine(self, directions):
        direction = jnp.where(self.core == 0, directions[0], directions[1])
        return ((self.index >> direction) & 1).astype(jnp.int32)

    def run(self, kernel, name, flags, operands, outputs, scratch=(), mebibytes=16, after=()):
        results, self.token = run_kernel(
            kernel,
            name,
            0.05,
            flags,
            operands,
            outputs,
            scratch,
            mebibytes,
            after if self.token is None else (self.token, *after),
        )
        return results

    def later(self, kernel, flags, operands, outputs, take):
        self.pending.append((kernel, flags, operands, outputs, take))

    def flush(self, name, after=()):
        pieces, self.pending = self.pending, []
        flags = [flag for piece in pieces for flag in piece[1]]
        operands = [each for piece in pieces for each in piece[2]]
        outputs = [each for piece in pieces for each in piece[3]]

        def kernel(flags_ref, *refs):
            ins, outs = list(refs[: len(operands)]), list(refs[len(operands) :])
            count = 0
            for body, piece_flags, piece_ins, piece_outs, _ in pieces:
                body(
                    *([[flags_ref[count + place] for place in range(len(piece_flags))]] if piece_flags else []),
                    *[ins.pop(0) for _ in piece_ins],
                    *[outs.pop(0) for _ in piece_outs],
                )
                count += len(piece_flags)

        results = self.run(kernel, name, jnp.stack(flags), operands, outputs, after=after)
        for piece in pieces:
            count = len(piece[3])
            piece[4](results[:count])
            results = results[count:]


def step_directions(slot, step):
    return tuple(order[step] for order in ORDERS[slot])


def shape_of(operand):
    return (operand[1] if isinstance(operand, tuple) else operand).shape


class Wave:
    def __init__(self, links, name, sent, kept, terms=None):
        self.links = links
        self.name = name
        self.terms = terms
        self.sent = list(sent)
        self.kept = list(kept)
        self.came = [None, None]

    def scatter(self, step):
        for slot in range(2):
            self.came[slot] = self.links.exchange(self.sent[slot], step_directions(slot, step))

    def piece(self, kernel, directions, operands, outputs, small, take):
        if small:
            operands = operands + [self.terms]
            outputs = outputs + [((SMALL_ROWS, outputs[0][0][1]), F32)]

        def take_all(results):
            if small:
                *results, self.terms = results
            take(results)

        self.links.later(
            functools.partial(kernel, small),
            [self.links.mine(directions)],
            operands,
            outputs,
            take_all,
        )

    def add(self, step, distant=False):
        for slot in range(2):
            small = slot == 1 and self.terms is not None
            rows, width = shape_of(self.kept[slot])
            half, extra = rows // 2, 2 * SMALL_ROWS if small else 0

            def take(results, slot=slot):
                self.sent[slot], self.kept[slot] = results

            self.piece(
                add_kernel,
                step_directions(slot, step + 1),
                [self.kept[slot], far(self.came[slot]) if distant else self.came[slot]],
                [
                    ((half + extra, width), BF16, "far"),
                    ((half, width), BF16, "far") if step == 0 and distant else ((half, width), BF16),
                ],
                small,
                take,
            )

    def finish(self):
        self.shares, self.own = [None, None], [None, None]
        for slot in range(2):

            def take(results, slot=slot):
                self.shares[slot], self.own[slot] = results

            shape = shape_of(self.kept[slot])
            self.piece(
                finish_kernel,
                step_directions(slot, STEPS - 1),
                [self.kept[slot], self.came[slot]],
                [(shape, BF16, "far"), (shape, BF16)],
                slot == 1 and self.terms is not None,
                take,
            )

    def sum_others(self):
        if self.links.bits == STEPS:
            return
        count = self.shares[0].shape[0]
        joined = jnp.concatenate([share.astype(F32) for share in self.shares], axis=0)
        terms = self.terms
        for direction in range(STEPS, self.links.bits):
            low = joined.astype(BF16)
            came = self.links.exchange(low, (direction, direction))
            joined = low.astype(F32) + came.astype(F32)
            if terms is not None:
                terms = terms + self.links.exchange(terms, (direction, direction))
        joined = joined.astype(BF16)
        self.terms = terms
        self.shares = [joined[:count], joined[count:]]
        self.own = list(self.shares)

    def gather(self, step):
        self.came = [
            self.links.exchange(rows, step_directions(slot, step))
            for slot, rows in enumerate(self.shares)
        ]

    def place(self, step):
        for slot in range(2):

            def take(results, slot=slot):
                self.shares[slot], self.own[slot] = results

            rows, width = shape_of(self.own[slot])
            self.links.later(
                place_kernel,
                [self.links.mine(step_directions(slot, step))],
                [self.own[slot], self.came[slot]],
                [((2 * rows, width), BF16, "far"), ((2 * rows, width), BF16)],
                take,
            )


def per_device(
    features,
    token_ids,
    mel_target,
    token_target,
    segments,
    row_device,
    offset_bucket,
    speech_weight,
    speech_bias,
    token_table,
    first_gain,
    first_shift,
    query_weight,
    key_weight,
    value_weight,
    bias_table,
    out_weight,
    second_gain,
    second_shift,
    up_weight,
    up_bias,
    down_weight,
    down_bias,
    mel_weight,
    mel_bias,
    vocab_weight,
    vocab_bias,
):
    devices = lax.axis_size("dp")
    device_index = lax.axis_index("dp")
    core = lax.axis_index("mp")
    cores = lax.axis_size("mp")
    rows_speech, part_len, feat_width = features.shape
    rows_total, length = segments.shape
    model_width = speech_weight.shape[1]
    vocab_size = token_table.shape[0]
    mel_width = mel_weight.shape[1]
    local_heads = bias_table.shape[1]
    buckets = bias_table.shape[0]
    head_width = query_weight.shape[1]
    head_size = head_width // local_heads
    units = up_weight.shape[1]
    is_speech = device_index % 2 == 0
    my_row = device_index // 2 + jnp.where(is_speech, 0, rows_speech)
    links = Links(devices, cores, device_index, core)
    flags = jnp.stack(
        [
            core,
            is_speech.astype(jnp.int32),
            1 - links.mine(step_directions(0, 0)),
            1 - links.mine(step_directions(1, 0)),
        ]
    ).astype(jnp.int32)

    plain_width = feat_width + mel_width
    core_width = -(-(plain_width + 2) // (LANES * cores)) * LANES
    ids = jnp.stack([token_ids, token_target], axis=2).astype(BF16)
    (packed,), _ = run_kernel(
        pack_kernel,
        "pack_rows",
        1,
        flags,
        [features, mel_target, ids],
        [((rows_total, part_len, core_width), BF16)],
    )
    arrived = lax.all_to_all(packed, "dp", split_axis=0, concat_axis=0, tiled=True)
    arrived = arrived.reshape(length, core_width)

    my_segments = lax.dynamic_slice_in_dim(segments, my_row, 1)
    segment_column = my_segments.reshape(length, 1)
    bucket_line = jnp.pad(offset_bucket, (0, 1), constant_values=-1).reshape(1, 2 * length)
    (window,), window_token = run_kernel(
        window_kernel,
        "bias_window",
        3,
        flags,
        [bucket_line, bias_table.T],
        [((local_heads, LANES, 2 * length), F32, "far")],
    )
    full_rows = lambda array: jnp.pad(array, ((0, LANES - array.shape[0]), (0, 0)))
    post_bias = jnp.concatenate(
        [jnp.pad(mel_bias, (0, LANES - mel_width)), jnp.pad(vocab_bias, (0, LANES - vocab_size))]
    )
    vectors = jnp.stack(
        [
            jnp.pad(each, (0, units - each.size))
            for each in (
                speech_bias,
                first_gain,
                first_shift,
                second_gain,
                second_shift,
                up_bias,
                down_bias,
                post_bias,
            )
        ]
    )
    token_rows, mel_rows, vocab_rows = (
        full_rows(array) for array in (token_table, mel_weight.T, vocab_weight.T)
    )
    arrived, window_token = lax.optimization_barrier((arrived, window_token))

    model_low = ((length, model_width), BF16)
    head_low = ((length, head_width), BF16)
    (
        embedded,
        attended,
        embedded_far,
        normed_one,
        queries,
        key_rows,
        value_rows,
        heads_flat,
        inputs,
        extra,
    ), _ = run_kernel(
        functools.partial(attend_kernel, head_size, plain_width),
        "embed_and_attend",
        8,
        flags,
        [
            arrived,
            swap_cores(arrived),
            far(speech_weight),
            far(token_rows),
            far(vectors),
            far(query_weight),
            far(key_weight),
            far(value_weight),
            far(out_weight),
            far(window),
            segment_column,
            my_segments,
        ],
        [
            model_low,
            model_low,
            (*model_low, "far"),
            (*model_low, "far"),
            (*head_low, "far"),
            (*head_low, "far"),
            (*head_low, "far"),
            (*head_low, "far"),
            ((length, feat_width + LANES), BF16, "far"),
            ((length, LANES), BF16),
        ],
        [pltpu.VMEM((length, length), F32)],
        mebibytes=26,
        after=(window_token,),
    )
    (mixed, slope, branch, mixed_far, normed_two, active), _ = run_kernel(
        forward_kernel,
        "feed_forward",
        5,
        flags,
        [
            embedded,
            attended,
            swap_cores(attended),
            far(vectors),
            up_weight,
            down_weight,
        ],
        [
            ((length, model_width), F32),
            ((length, units), F32),
            model_low,
            ((length, model_width), F32, "far"),
            model_low,
            ((length, units), BF16),
        ],
        mebibytes=28,
    )
    model_cut = model_width // 3
    folds = units // model_width
    early_shapes = [
        ((units // 2 + model_cut // 2 * folds, model_width), BF16, "far"),
        (((model_width - model_cut) // 2 * folds, model_width), BF16, "far"),
    ]
    (
        *early_parts,
        grad_normed_two,
        grad_final_far,
        final_low,
        grad_post,
        loss_sums,
    ), links.token = run_kernel(
        functools.partial(loss_kernel, mel_width, vocab_size),
        "loss_and_feed_back",
        0.05,
        flags,
        [
            mixed,
            branch,
            swap_cores(branch),
            far(vectors),
            mel_rows,
            vocab_rows,
            extra,
            slope,
            up_weight,
            down_weight,
            active,
            normed_two,
        ],
        early_shapes * 2
        + [
            model_low,
            (*model_low, "far"),
            (*model_low, "far"),
            ((length, 2 * LANES), BF16, "far"),
            ((8, units), F32, "far"),
        ],
        [
            pltpu.VMEM((2 * LANES, model_width), BF16),
            pltpu.VMEM((length, model_width), BF16),
            pltpu.VMEM((length, units), BF16),
        ],
        mebibytes=34,
    )

    early = Wave(links, "early", early_parts[:2], [far(kept) for kept in early_parts[2:]])
    early.scatter(0)
    other_normed_two = swap_cores(grad_normed_two)
    part = ((model_width // 2 + head_width, model_width), BF16)
    post_part = ((LANES // 2, model_width), BF16)
    (
        grad_normed_one,
        late_sent,
        late_kept,
        grad_mixed,
        post_sent,
        post_kept,
        grad_offsets,
        back_sums,
    ) = links.run(
        functools.partial(back_kernel, head_size),
        "attend_back",
        flags,
        [
            grad_normed_two,
            other_normed_two,
            far(mixed_far),
            far(grad_final_far),
            far(vectors),
            far(out_weight),
            far(queries),
            far(key_rows),
            far(value_rows),
            far(window),
            segment_column,
            my_segments,
            far(query_weight),
            far(key_weight),
            far(value_weight),
            far(normed_one),
            far(heads_flat),
            far(grad_post),
            far(final_low),
        ],
        [
            model_low,
            (*part, "far"),
            (*part, "far"),
            ((length, model_width), F32, "far"),
            (*post_part, "far"),
            (*post_part, "far"),
            ((local_heads, 2 * length), F32, "far"),
            ((8, model_width), F32, "far"),
        ],
        [
            pltpu.VMEM((length, model_width), BF16),
            pltpu.VMEM((length, head_width), BF16),
            pltpu.VMEM((length, 3 * head_width), BF16),
            pltpu.VMEM((length, length), F32),
            pltpu.VMEM((length, length), BF16),
            pltpu.VMEM((length, length), BF16),
            pltpu.VMEM((LANES, 2 * length), F32),
            pltpu.VMEM((LANES, model_width), F32),
        ],
        mebibytes=32,
    )
    other_normed_one = swap_cores(grad_normed_one)
    early.add(0, True)
    links.flush("phase_a")
    early.kept = [far(kept) for kept in early.kept]
    early.scatter(1)
    late_rows = LANES + feat_width // 4
    late_second_sent, late_second_kept, feature_back, terms = links.run(
        input_kernel,
        "input_back",
        flags,
        [
            grad_normed_one,
            other_normed_one,
            far(embedded_far),
            far(grad_mixed),
            far(vectors),
            far(speech_weight),
            far(inputs),
            far(post_sent),
            far(post_kept),
            far(loss_sums),
            far(back_sums),
            far(grad_offsets),
            far(bucket_line),
        ],
        [
            ((late_rows + 2 * SMALL_ROWS, model_width), BF16, "far"),
            ((late_rows, model_width), BF16),
            ((length, feat_width // cores), BF16, "far"),
            ((SMALL_ROWS, model_width), F32),
        ],
        [
            pltpu.VMEM((length, model_width), BF16),
            pltpu.VMEM((LANES, model_width), F32),
        ],
        mebibytes=18,
    )
    late = Wave(
        links, "late", [late_sent, late_second_sent], [far(late_kept), late_second_kept], terms
    )
    feature_half = lax.all_to_all(
        feature_back.reshape(devices, part_len, feat_width // cores),
        "dp",
        split_axis=0,
        concat_axis=0,
        tiled=True,
    )
    early.add(1, True)
    links.flush("phase_b")
    early.scatter(2)
    early.add(2)
    links.flush("phase_c", (feature_half,))
    early.scatter(3)
    *late.sent, early.sent[0] = lax.optimization_barrier((*late.sent, early.sent[0]))
    late.scatter(0)
    early.finish()
    late.add(0)
    links.flush("phase_d")
    early.sum_others()
    early.gather(3)
    late.scatter(1)
    feature_half = feature_half.reshape(rows_speech, 2, part_len, feat_width // cores)[:, 0]
    other_feature = swap_cores(feature_half)
    feature_grad = jnp.concatenate(
        [
            jnp.where(core == 0, feature_half, other_feature),
            jnp.where(core == 0, other_feature, feature_half),
        ],
        axis=2,
    )
    early.place(3)
    late.add(1)
    links.flush("phase_e", (feature_grad,))
    early.gather(2)
    late.scatter(2)
    early.place(2)
    late.add(2)
    links.flush("phase_f")
    early.gather(1)
    late.scatter(3)
    early.place(1)
    late.finish()
    links.flush("phase_g")
    late.sum_others()
    early.gather(0)
    late.gather(3)
    late.place(3)
    line_out = ((model_width,), F32)
    small = []
    links.later(
        functools.partial(small_kernel, rows_total),
        [],
        [late.terms],
        [((1, 1), F32), ((mel_width,), F32), ((vocab_size,), F32)]
        + [line_out] * 6
        + [((units,), F32), ((local_heads, buckets), F32)],
        small.extend,
    )
    links.flush("phase_h")
    late.gather(2)
    late.place(2)
    links.flush("phase_h2")
    late.gather(1)
    late.place(1)
    links.flush("phase_i", early.came)
    late.gather(0)

    place_flags = jnp.stack(
        [links.mine(step_directions(0, 0)), links.mine(step_directions(1, 0)), core]
    ).astype(jnp.int32)
    grad_down, grad_up = links.run(
        early_place_kernel,
        "early_place",
        place_flags,
        [early.own[0], far(early.came[0]), early.own[1], far(early.came[1])],
        [((units, model_width), F32), ((model_width, units), F32)],
        mebibytes=20,
    )
    early_end = links.token
    shared_own, shared_came, _ = lax.optimization_barrier(
        (late.own[1], late.came[1], early_end)
    )
    shared_own_other, shared_came_other = swap_cores(shared_own), swap_cores(shared_came)
    weight_shape = ((model_width, head_width), F32)
    grad_query, grad_key, grad_value, grad_out = links.run(
        late_place_kernel,
        "late_place",
        place_flags,
        [late.own[0], late.came[0]],
        [weight_shape, weight_shape, weight_shape, ((head_width, model_width), F32)],
    )
    grad_speech_weight, grad_token_table, grad_mel_weight, grad_vocab_weight = links.run(
        shared_place_kernel,
        "shared_place",
        place_flags,
        [shared_own, shared_own_other, shared_came, shared_came_other],
        [
            ((feat_width, model_width), F32),
            ((vocab_size, model_width), F32),
            ((mel_width, model_width), F32),
            ((vocab_size, model_width), F32),
        ],
        [pltpu.VMEM((2 * LANES, model_width), F32), pltpu.VMEM((LANES, model_width), F32)],
    )
    grad_mel_weight, grad_vocab_weight = grad_mel_weight.T, grad_vocab_weight.T
    (
        loss_total,
        grad_mel_bias,
        grad_vocab_bias,
        grad_down_bias,
        grad_second_gain,
        grad_second_shift,
        grad_first_gain,
        grad_first_shift,
        grad_speech_bias,
        grad_up_bias,
        grad_table,
    ) = small
    return (
        loss_total.reshape(()),
        feature_grad,
        grad_speech_weight,
        grad_speech_bias,
        grad_token_table,
        grad_first_gain,
        grad_first_shift,
        grad_query,
        grad_key,
        grad_value,
        grad_table.T,
        grad_out,
        grad_second_gain,
        grad_second_shift,
        grad_up,
        grad_up_bias,
        grad_down,
        grad_down_bias,
        grad_mel_weight,
        grad_mel_bias,
        grad_vocab_weight,
        grad_vocab_bias,
    )


def solution(mesh):
    placed = (
        P(None, "dp", None),
        P(None, "dp"),
        P(None, "dp", None),
        P(None, "dp"),
        P(),
        P(),
        P(),
        P(),
        P(),
        P(),
        P(),
        P(),
        P(None, "mp"),
        P(None, "mp"),
        P(None, "mp"),
        P(None, "mp"),
        P("mp", None),
        P(),
        P(),
        P(None, "mp"),
        P("mp"),
        P("mp", None),
        P(),
        P(),
        P(),
        P(),
        P(),
    )
    return jax.shard_map(
        per_device,
        mesh=mesh,
        in_specs=placed,
        out_specs=(
            P(),
            P(None, "dp", None),
            P(),
            P(),
            P(),
            P(),
            P(),
            P(None, "mp"),
            P(None, "mp"),
            P(None, "mp"),
            P(None, "mp"),
            P("mp", None),
            P(),
            P(),
            P(None, "mp"),
            P("mp"),
            P("mp", None),
            P(),
            P(),
            P(),
            P(),
            P(),
        ),
        check_vma=False,
    )
```

```python
import functools

import jax
import jax.numpy as jnp
from jax import lax
from jax.experimental import pallas as pl
from jax.experimental.pallas import tpu as pltpu
from jax.sharding import PartitionSpec as P

EPSILON = 1e-05
NEGATIVE = -1e30
HIGHEST = lax.Precision.HIGHEST
BF16 = jnp.bfloat16
F32 = jnp.float32
LANES = 128
SMALL_ROWS = 16


def contract_rows(left_side, right_side):
    return lax.dot_general(
        left_side, right_side, (((0,), (0,)), ((), ())), preferred_element_type=F32
    )


def times_transposed(left_side, right_side):
    return lax.dot_general(
        left_side, right_side, (((1,), (1,)), ((), ())), preferred_element_type=F32
    )


def matmul(left_side, right_side):
    return jnp.dot(left_side, right_side, preferred_element_type=F32)


def normalize(row_data):
    center = row_data - jnp.mean(row_data, axis=-1, keepdims=True)
    inverse = lax.rsqrt(jnp.mean(center * center, axis=-1, keepdims=True) + EPSILON)
    return center * inverse, inverse


def norm_back(grad_out, normal, inverse, norm_gain):
    scaled = grad_out * norm_gain
    return inverse * (
        scaled
        - jnp.mean(scaled, axis=-1, keepdims=True)
        - normal * jnp.mean(scaled * normal, axis=-1, keepdims=True)
    )


def column_sum(array):
    return jnp.sum(array, axis=0, keepdims=True)


def cost(microseconds):
    return pl.CostEstimate(
        flops=0, bytes_accessed=int(microseconds * 3.5e6), transcendentals=0
    )


class Fetched:
    def __init__(self, source, target, semaphore):
        self.copy = pltpu.make_async_copy(source, target, semaphore)
        self.target = target
        self.begun = False
        self.waited = False
        self.shape = target.shape

    def begin(self):
        if not self.begun:
            self.copy.start()
            self.begun = True

    def ready(self):
        self.begin()
        if not self.waited:
            self.copy.wait()
            self.waited = True
        return self.target

    def __getitem__(self, places):
        return self.ready()[places]


class Stored:
    def __init__(self, target, source, semaphore):
        self.copy = pltpu.make_async_copy(source, target, semaphore)
        self.source = source
        self.started = False
        self.shape = source.shape

    def __getitem__(self, places):
        return self.source[places]

    def __setitem__(self, places, value):
        self.source[places] = value

    def flush(self):
        if not self.started:
            self.copy.start()
            self.started = True


def run_kernel(
    kernel, name, microseconds, flags, operands, outputs, scratch=(), mebibytes=16, after=()
):
    in_place = pl.BlockSpec(memory_space=pltpu.VMEM)
    distant = pl.BlockSpec(memory_space=pltpu.HBM)
    far = [isinstance(operand, tuple) for operand in operands]
    arrays = [
        pltpu.with_memory_space_constraint(operand[1], pltpu.HBM) if is_far else operand
        for operand, is_far in zip(operands, far)
    ]
    out_far = [len(output) == 3 and output[2] == "far" for output in outputs]
    copied = {output[2]: place for place, output in enumerate(outputs) if len(output) == 3}
    fetched = [
        pltpu.VMEM(array.shape, array.dtype)
        for place, (array, is_far) in enumerate(zip(arrays, far))
        if is_far and place not in copied
    ]
    stored = [
        pltpu.VMEM(output[0], output[1]) for output, is_far in zip(outputs, out_far) if is_far
    ]
    moves = sum(far) + sum(out_far)
    semaphores = [pltpu.SemaphoreType.DMA((moves,))] if moves else []

    def with_moves(*refs):
        refs = list(refs)
        semaphore = refs.pop() if moves else None
        buffers = refs[len(refs) - len(fetched) - len(stored) :]
        refs = refs[: len(refs) - len(fetched) - len(stored)]
        first_out = 1 + len(arrays) + len(after)
        count = 0
        came = []
        for place, is_far in enumerate(far):
            if is_far:
                target = refs[first_out + copied[place]] if place in copied else buffers.pop(0)
                refs[place + 1] = Fetched(refs[place + 1], target, semaphore.at[count])
                if operands[place][0] == "far":
                    refs[place + 1].begin()
                came.append(refs[place + 1])
                count += 1
        kept = []
        for place, is_far in enumerate(out_far):
            if is_far:
                refs[first_out + place] = Stored(
                    refs[first_out + place], buffers.pop(0), semaphore.at[count]
                )
                kept.append(refs[first_out + place])
                count += 1
        token_ref = refs[first_out + len(outputs)]
        token_ref[...] = jnp.zeros_like(token_ref)
        kernel(
            *refs[: 1 + len(arrays)],
            *refs[first_out : first_out + len(outputs)],
            *refs[first_out + len(outputs) + 1 :],
        )
        for ref in kept:
            ref.flush()
        for ref in came:
            ref.ready()
        for ref in kept:
            ref.copy.wait()

    *results, token = pl.pallas_call(
        with_moves,
        in_specs=[pl.BlockSpec(memory_space=pltpu.SMEM)]
        + [distant if is_far else in_place for is_far in far]
        + [pl.BlockSpec(memory_space=pl.ANY)] * len(after),
        out_specs=[distant if is_far else in_place for is_far in out_far] + [in_place],
        out_shape=[
            pltpu.HBM(output[0], output[1])
            if is_far
            else jax.ShapeDtypeStruct(output[0], output[1])
            for output, is_far in zip(outputs, out_far)
        ]
        + [jax.ShapeDtypeStruct((8, LANES), F32)],
        scratch_shapes=list(scratch) + fetched + stored + semaphores,
        compiler_params=pltpu.CompilerParams(vmem_limit_bytes=mebibytes * 1024 * 1024),
        cost_estimate=cost(microseconds),
        name=name,
    )(flags, *arrays, *after)
    return results, token


def far(array):
    return ("far", array)


def later(array):
    return ("later", array)


def begin(*refs):
    for ref in refs:
        ref.begin()


def blocks_of(length, size):
    return [slice(start, start + size) for start in range(0, length, size)]


def times_hot(left_side, hot, dims):
    total = 0.0
    for _ in range(3):
        term = left_side.astype(BF16)
        total += lax.dot_general(term, hot, (dims, ((), ())), preferred_element_type=F32)
        left_side = left_side - term.astype(F32)
    return total


def window_kernel(flags_ref, bucket_ref, table_ref, window_ref):
    heads, buckets = table_ref.shape
    width = bucket_ref.shape[1]
    places = lax.broadcasted_iota(jnp.int32, (buckets, width), 0)
    hot = jnp.where(places == bucket_ref[...], 1.0, 0.0).astype(BF16)
    offsets = times_hot(table_ref[...], hot, ((1,), (0,)))
    for head in range(heads):
        spread = jnp.broadcast_to(offsets[head : head + 1, :], (LANES, width))
        window_ref[head] = pltpu.roll(spread, width - LANES + 1, 1, stride=1, stride_axis=0)


def pack_kernel(flags_ref, features_ref, target_ref, ids_ref, sent_ref):
    core_width = sent_ref.shape[2]
    rest = features_ref.shape[2] - core_width
    mel_width = target_ref.shape[2]
    sent_ref[...] = jnp.zeros_like(sent_ref)

    @pl.when(flags_ref[0] == 0)
    def _():
        for row in range(features_ref.shape[0]):
            sent_ref[2 * row] = features_ref[row, :, :core_width]

    @pl.when(flags_ref[0] != 0)
    def _():
        for row in range(features_ref.shape[0]):
            sent_ref[2 * row, :, :rest] = features_ref[row, :, core_width:]
            sent_ref[2 * row, :, rest : rest + mel_width] = target_ref[row]
            start = rest + mel_width
            sent_ref[2 * row + 1, :, start : start + 2] = ids_ref[row]


def key_probs(keys, queries, window_ref, head, mask_ref):
    length = keys.shape[0]
    blocks = length // LANES
    bias = jnp.concatenate(
        [
            window_ref[head, :, LANES * (blocks - 1 - b) : LANES * (blocks - 1 - b) + length]
            for b in range(blocks)
        ],
        axis=0,
    )
    scores = times_transposed(keys, queries) + bias + mask_ref[...]
    powers = jnp.exp(scores - jnp.max(scores, axis=0, keepdims=True))
    return powers * (1.0 / column_sum(powers))


SPEECH_BIAS, FIRST_GAIN, FIRST_SHIFT, SECOND_GAIN, SECOND_SHIFT, UP_BIAS, DOWN_BIAS, POST_BIAS = range(8)


def vector(ref, row, width):
    return ref[row : row + 1, :width]


def attend_kernel(
    head_size,
    plain_width,
    flags_ref,
    own_ref,
    other_ref,
    speech_weight_ref,
    token_table_ref,
    vectors_ref,
    query_weight_ref,
    key_weight_ref,
    value_weight_ref,
    out_weight_ref,
    window_ref,
    column_ref,
    row_ref,
    embedded_ref,
    attended_ref,
    embedded_far_ref,
    normed_ref,
    queries_ref,
    keys_ref,
    values_ref,
    heads_ref,
    inputs_ref,
    extra_ref,
    mask_ref,
):
    length, half_width = own_ref.shape
    width = embedded_ref.shape[1]
    feat_width = inputs_ref.shape[1] - LANES
    first = flags_ref[0] == 0
    speech = flags_ref[1].astype(F32)
    scaling = jnp.asarray(head_size ** (-0.5), BF16)
    for rows in blocks_of(length, LANES):
        own, other = own_ref[rows, :], other_ref[rows, :]
        low = jnp.where(first, own, other)
        high = jnp.where(first, other, own)
        inputs_ref[rows, :half_width] = low
        inputs_ref[rows, half_width:feat_width] = high[:, : feat_width - half_width]
        extra = high[:, feat_width - half_width : feat_width - half_width + LANES]
        extra_ref[rows, :] = extra
        ids = extra[:, plain_width - feat_width : plain_width - feat_width + 1].astype(F32)
        places = lax.broadcasted_iota(jnp.int32, (LANES, LANES), 1).astype(F32)
        hot = jnp.where(ids == places, 1.0 - speech, 0.0)
        inputs_ref[rows, feat_width:] = hot.astype(BF16)
    inputs_ref.flush()
    speech_weight, token_table = speech_weight_ref.ready(), token_table_ref.ready()
    vectors = vectors_ref.ready()
    for rows in blocks_of(length, 2 * LANES):
        embedded = (
            matmul(inputs_ref[rows, :feat_width], speech_weight[...])
            + matmul(inputs_ref[rows, feat_width:], token_table[...])
            + vector(vectors, SPEECH_BIAS, width) * speech
        ).astype(BF16)
        embedded_ref[rows, :] = embedded
        embedded_far_ref[rows, :] = embedded
        normal, _ = normalize(embedded.astype(F32))
        normed_ref[rows, :] = (
            normal * vector(vectors, FIRST_GAIN, width) + vector(vectors, FIRST_SHIFT, width)
        ).astype(BF16)
    embedded_far_ref.flush()
    normed_ref.flush()
    query_weight, key_weight = query_weight_ref.ready(), key_weight_ref.ready()
    value_weight = value_weight_ref.ready()
    for rows in blocks_of(length, 2 * LANES):
        normed = normed_ref[rows, :]
        queries_ref[rows, :] = matmul(normed, query_weight[...]).astype(BF16) * scaling
        keys_ref[rows, :] = matmul(normed, key_weight[...]).astype(BF16)
        values_ref[rows, :] = matmul(normed, value_weight[...]).astype(BF16)
    queries_ref.flush()
    keys_ref.flush()
    values_ref.flush()
    mask_ref[...] = jnp.where(column_ref[...] == row_ref[...], 0.0, NEGATIVE)
    window = window_ref.ready()
    for head, columns in enumerate(blocks_of(queries_ref.shape[1], head_size)):
        probs = key_probs(
            keys_ref[:, columns], queries_ref[:, columns], window, head, mask_ref
        ).astype(BF16)
        heads_ref[:, columns] = contract_rows(probs, values_ref[:, columns]).astype(BF16)
    heads_ref.flush()
    out_weight = out_weight_ref.ready()
    for rows in blocks_of(length, 2 * LANES):
        attended_ref[rows, :] = matmul(heads_ref[rows, :], out_weight[...]).astype(BF16)


def forward_kernel(
    flags_ref,
    embedded_ref,
    own_ref,
    other_ref,
    vectors_ref,
    up_weight_ref,
    down_weight_ref,
    mixed_ref,
    slope_ref,
    branch_ref,
    mixed_far_ref,
    normed_ref,
    active_ref,
):
    length, width = embedded_ref.shape
    units = active_ref.shape[1]
    vectors = vectors_ref.ready()
    for rows in blocks_of(length, 2 * LANES):
        mixed = embedded_ref[rows, :].astype(F32) + (
            own_ref[rows, :].astype(F32) + other_ref[rows, :].astype(F32)
        )
        mixed_ref[rows, :] = mixed
        mixed_far_ref[rows, :] = mixed
        normal, _ = normalize(mixed)
        normed_ref[rows, :] = (
            normal * vector(vectors, SECOND_GAIN, width) + vector(vectors, SECOND_SHIFT, width)
        ).astype(BF16)
    mixed_far_ref.flush()
    for rows in blocks_of(length, 2 * LANES):
        hidden = matmul(normed_ref[rows, :], up_weight_ref[...]) + vector(vectors, UP_BIAS, units)
        square = hidden * hidden
        inner = 0.7978845608028654 * hidden * (1.0 + 0.044715 * square)
        curve = jnp.tanh(inner)
        half = 0.5 * (1.0 + curve)
        active = (hidden * half).astype(BF16)
        active_ref[rows, :] = active
        slope_ref[rows, :] = half + 0.5 * hidden * (1.0 - curve * curve) * (
            0.7978845608028654 * (1.0 + 0.134145 * square)
        )
        branch_ref[rows, :] = matmul(active, down_weight_ref[...]).astype(BF16)


def loss_kernel(
    mel_width,
    vocab_size,
    flags_ref,
    mixed_ref,
    own_ref,
    other_ref,
    vectors_ref,
    mel_weight_ref,
    vocab_weight_ref,
    extra_ref,
    slope_ref,
    up_weight_ref,
    down_weight_ref,
    active_ref,
    normed_ref,
    first_ref,
    second_ref,
    first_kept_ref,
    second_kept_ref,
    grad_normed_ref,
    grad_final_far_ref,
    final_ref,
    grad_post_ref,
    sums_ref,
    post_weight_ref,
    grad_final_ref,
    grad_hidden_ref,
):
    length, width = mixed_ref.shape
    units = slope_ref.shape[1]
    speech = flags_ref[1].astype(F32)
    mel_scale = speech * (1.0 / (mel_width * length))
    text_scale = (1.0 - speech) * (1.0 / length)
    vectors = vectors_ref.ready()
    post_weight_ref[:LANES, :] = mel_weight_ref[...]
    post_weight_ref[LANES:, :] = vocab_weight_ref[...]
    totals = None
    for rows in blocks_of(length, 2 * LANES):
        final = mixed_ref[rows, :] + (
            own_ref[rows, :].astype(F32) + other_ref[rows, :].astype(F32)
        )
        final = (final + vector(vectors, DOWN_BIAS, width)).astype(BF16)
        final_ref[rows, :] = final
        results = times_transposed(final, post_weight_ref[...])
        results += vector(vectors, POST_BIAS, 2 * LANES)
        extra = extra_ref[rows, :].astype(F32)
        places = lax.broadcasted_iota(jnp.int32, extra.shape, 1)
        error = jnp.where(places < mel_width, results[:, :LANES] - extra, 0.0)
        smooth = jnp.sqrt(error * error + 1.0)
        grad_mel = error / smooth * mel_scale
        logits = jnp.where(places < vocab_size, results[:, LANES:], NEGATIVE)
        shifted = logits - jnp.max(logits, axis=-1, keepdims=True)
        powers = jnp.exp(shifted)
        power_sum = jnp.sum(powers, axis=-1, keepdims=True)
        label = extra[:, mel_width + 1 : mel_width + 2] == places.astype(F32)
        picked = jnp.sum(jnp.where(label, shifted, 0.0), axis=-1, keepdims=True)
        text_loss = column_sum(jnp.log(power_sum) - picked) * text_scale
        mel_loss = column_sum((smooth - 1.0) * mel_scale)
        loss = mel_loss + jnp.where(places[:1] == 0, text_loss, 0.0)
        grad_text = (powers / power_sum - jnp.where(label, 1.0, 0.0)) * text_scale
        grad_post = jnp.concatenate([grad_mel, grad_text], axis=1).astype(BF16)
        grad_post_ref[rows, :] = grad_post
        grad_final = matmul(grad_post, post_weight_ref[...]).astype(BF16)
        grad_final_ref[rows, :] = grad_final
        grad_final_far_ref[rows, :] = grad_final
        grad_active = times_transposed(grad_final, down_weight_ref[...])
        grad_hidden = (slope_ref[rows, :] * grad_active).astype(BF16)
        grad_hidden_ref[rows, :] = grad_hidden
        grad_normed_ref[rows, :] = times_transposed(grad_hidden, up_weight_ref[...]).astype(BF16)
        sums = (
            loss,
            column_sum(grad_post.astype(F32)),
            column_sum(grad_final.astype(F32)),
            column_sum(grad_hidden.astype(F32)),
        )
        totals = sums if totals is None else [a + b for a, b in zip(totals, sums)]
    final_ref.flush()
    grad_post_ref.flush()
    grad_final_far_ref.flush()
    sums_ref[...] = jnp.zeros(sums_ref.shape, F32)
    sums_ref[0:1, :LANES] = jnp.broadcast_to(
        jnp.sum(totals[0], axis=1, keepdims=True), (1, LANES)
    )
    sums_ref[0:1, LANES : 3 * LANES] = totals[1]
    sums_ref[1:2, :width] = totals[2]
    sums_ref[2:3, :] = totals[3]
    sums_ref.flush()
    cut = width // 3
    for first_half, second_half, first, second in (
        (flags_ref[2], flags_ref[3], first_ref, second_ref),
        (1 - flags_ref[2], 1 - flags_ref[3], first_kept_ref, second_kept_ref),
    ):
        count = (width - cut) // 2
        grad_up = contract_rows(
            wide(normed_ref, cut + second_half * count, count), grad_hidden_ref[...]
        )
        store_folded(second, 0, grad_up)
        second.flush()
        count = units // 2
        first[:count, :] = contract_rows(
            wide(active_ref, first_half * count, count), grad_final_ref[...]
        ).astype(BF16)
        grad_up = contract_rows(
            wide(normed_ref, first_half * (cut // 2), cut // 2), grad_hidden_ref[...]
        )
        store_folded(first, count, grad_up)
        first.flush()


def store_folded(ref, start, array):
    for columns in blocks_of(array.shape[1], ref.shape[1]):
        ref[start : start + array.shape[0], :] = array[:, columns].astype(BF16)
        start += array.shape[0]


def wide(ref, start, size):
    return ref[:, pl.ds(pl.multiple_of(start, LANES), size)]


def back_kernel(
    head_size,
    flags_ref,
    own_ref,
    other_ref,
    mixed_ref,
    grad_final_ref,
    vectors_ref,
    out_weight_ref,
    queries_ref,
    keys_ref,
    values_ref,
    window_ref,
    column_ref,
    row_ref,
    query_weight_ref,
    key_weight_ref,
    value_weight_ref,
    normed_ref,
    heads_ref,
    grad_post_ref,
    final_ref,
    grad_normed_ref,
    sent_ref,
    kept_ref,
    grad_mixed_ref,
    post_sent_ref,
    post_kept_ref,
    grad_offsets_ref,
    sums_ref,
    grad_low_ref,
    grad_heads_ref,
    grad_projected_ref,
    mask_ref,
    probs_ref,
    scores_ref,
    window_sum_ref,
    post_ref,
):
    length, head_width = queries_ref.shape
    width = grad_low_ref.shape[1]
    blocks = length // LANES
    mixed, grad_final, vectors = mixed_ref.ready(), grad_final_ref.ready(), vectors_ref.ready()
    out_weight = out_weight_ref.ready()
    gain_sum, shift_sum = 0.0, 0.0
    for rows in blocks_of(length, 2 * LANES):
        grad_normed = own_ref[rows, :].astype(F32) + other_ref[rows, :].astype(F32)
        normal, inverse = normalize(mixed[rows, :])
        gain_sum += column_sum(grad_normed * normal)
        shift_sum += column_sum(grad_normed)
        grad_mixed = grad_final[rows, :].astype(F32) + norm_back(
            grad_normed, normal, inverse, vector(vectors, SECOND_GAIN, width)
        )
        grad_mixed_ref[rows, :] = grad_mixed
        grad_low = grad_mixed.astype(BF16)
        grad_low_ref[rows, :] = grad_low
        grad_heads_ref[rows, :] = times_transposed(grad_low, out_weight[...]).astype(BF16)
    grad_mixed_ref.flush()
    sums_ref[...] = jnp.zeros(sums_ref.shape, F32)
    sums_ref[0:1, :] = gain_sum
    sums_ref[1:2, :] = shift_sum
    sums_ref.flush()
    mask_ref[...] = jnp.where(column_ref[...] == row_ref[...], 0.0, NEGATIVE)
    queries_ref, keys_ref, values_ref = queries_ref.ready(), keys_ref.ready(), values_ref.ready()
    window = window_ref.ready()
    scaling = head_size ** (-0.5)
    for head, columns in enumerate(blocks_of(head_width, head_size)):
        keys, queries = keys_ref[:, columns], queries_ref[:, columns]
        grads = grad_heads_ref[:, columns]
        probs = key_probs(keys, queries, window, head, mask_ref)
        weighted = probs * times_transposed(values_ref[:, columns], grads)
        grad_scores = weighted - probs * column_sum(weighted)
        probs_ref[...] = probs.astype(BF16)
        scores_ref[...] = grad_scores.astype(BF16)
        window_sum_ref[...] = jnp.zeros_like(window_sum_ref)
        for block in range(blocks):
            start = LANES * (blocks - 1 - block)
            window_sum_ref[:, start : start + length] += grad_scores[
                LANES * block : LANES * (block + 1)
            ]
        start = head * head_size
        for kind, value in enumerate(
            (
                contract_rows(scores_ref[...], keys) * scaling,
                matmul(scores_ref[...], queries),
                matmul(probs_ref[...], grads),
            )
        ):
            grad_projected_ref[
                :, kind * head_width + start : kind * head_width + start + head_size
            ] = value.astype(BF16)
        diagonal = window_sum_ref[...]
        half = LANES // 2
        while half >= 1:
            diagonal = pltpu.roll(diagonal[:half], half, 1) + diagonal[half:]
            half //= 2
        grad_offsets_ref[head : head + 1, :] = diagonal
    grad_offsets_ref.flush()
    for rows in blocks_of(length, 2 * LANES):
        total = 0.0
        for kind, weight_ref in enumerate((query_weight_ref, key_weight_ref, value_weight_ref)):
            total += times_transposed(
                grad_projected_ref[rows, kind * head_width : (kind + 1) * head_width],
                weight_ref.ready()[...],
            )
        grad_normed_ref[rows, :] = total.astype(BF16)
    normed, heads = normed_ref.ready(), heads_ref.ready()
    grad_post, final = grad_post_ref.ready(), final_ref.ready()
    half = width // 2
    count = head_width // 2
    post_rows = LANES // 2
    post_ref[...] = contract_rows(wide(grad_post, flags_ref[0] * LANES, LANES), final[...])
    for first_ref, post_half_ref, first, second in (
        (sent_ref, post_sent_ref, flags_ref[2], flags_ref[3]),
        (kept_ref, post_kept_ref, 1 - flags_ref[2], 1 - flags_ref[3]),
    ):
        post_half_ref[...] = post_ref[
            pl.ds(pl.multiple_of(second * post_rows, post_rows), post_rows), :
        ].astype(BF16)
        post_half_ref.flush()
        grad_project = contract_rows(
            wide(normed, first * half, half), grad_projected_ref[...]
        ).astype(BF16)
        first_ref[:half, :] = grad_project[:, : 2 * head_width]
        first_ref[half : half + count, :head_width] = grad_project[:count, 2 * head_width :]
        first_ref[half : half + count, head_width:] = grad_project[count:, 2 * head_width :]
        grad_out = contract_rows(heads[...], wide(grad_low_ref, first * half, half))
        first_ref[half + count :, :half] = grad_out[:count].astype(BF16)
        first_ref[half + count :, half:] = grad_out[count:].astype(BF16)
        first_ref.flush()


def input_kernel(
    flags_ref,
    own_ref,
    other_ref,
    embedded_ref,
    grad_mixed_ref,
    vectors_ref,
    speech_weight_ref,
    inputs_ref,
    post_sent_ref,
    post_kept_ref,
    loss_sums_ref,
    back_sums_ref,
    grad_offsets_ref,
    bucket_ref,
    sent_ref,
    kept_ref,
    feature_back_ref,
    terms_ref,
    grad_embedded_ref,
    hot_ref,
):
    length, width = own_ref.shape
    embedded, grad_mixed = embedded_ref.ready(), grad_mixed_ref.ready()
    vectors, speech_weight = vectors_ref.ready(), speech_weight_ref.ready()
    feat_width = speech_weight.shape[0]
    core_width = feat_width // 2
    speech = flags_ref[1].astype(F32)
    core = flags_ref[0]
    gain_sum, shift_sum, bias_sum = 0.0, 0.0, 0.0
    core_weight = speech_weight[pl.ds(pl.multiple_of(core * core_width, core_width), core_width), :]
    for rows in blocks_of(length, 2 * LANES):
        grad_normed = own_ref[rows, :].astype(F32) + other_ref[rows, :].astype(F32)
        normal, inverse = normalize(embedded[rows, :].astype(F32))
        gain_sum += column_sum(grad_normed * normal)
        shift_sum += column_sum(grad_normed)
        grad_embedded = (
            grad_mixed[rows, :]
            + norm_back(grad_normed, normal, inverse, vector(vectors, FIRST_GAIN, width))
        ).astype(BF16)
        grad_embedded_ref[rows, :] = grad_embedded
        bias_sum += column_sum(grad_embedded.astype(F32))
        feature_back_ref[rows, :] = times_transposed(grad_embedded, core_weight).astype(BF16)
    inputs = inputs_ref.ready()
    hot_ref[...] = contract_rows(inputs[:, feat_width:], grad_embedded_ref[...])
    post_rows = LANES // 2
    feat_rows = core_width // 2
    hot_rows = LANES // 4
    small_rows = 2 * SMALL_ROWS
    for which_ref, post_ref, half, base in (
        (sent_ref, post_sent_ref, flags_ref[3], small_rows),
        (kept_ref, post_kept_ref, 1 - flags_ref[3], 0),
    ):
        which_ref[base : base + post_rows, :] = post_ref[...]
        start = base + post_rows
        which_ref[start : start + feat_rows, :] = contract_rows(
            wide(inputs, core * core_width + half * feat_rows, feat_rows), grad_embedded_ref[...]
        ).astype(BF16)
        start += feat_rows
        which_ref[start : start + hot_rows, :] = hot_ref[
            pl.ds(pl.multiple_of(core * 2 * hot_rows + half * hot_rows, hot_rows), hot_rows), :
        ].astype(BF16)
        which_ref[start + hot_rows :, :] = jnp.zeros((hot_rows, width), BF16)
    loss_sums, back_sums = loss_sums_ref.ready(), back_sums_ref.ready()
    bias_rows = loss_sums.shape[1] // width
    rows = [loss_sums[0:1, :width], loss_sums[1:2, :width], back_sums[0:1, :], back_sums[1:2, :]]
    rows += [gain_sum, shift_sum, bias_sum * speech]
    rows += [loss_sums[2:3, part * width : (part + 1) * width] for part in range(bias_rows)]
    terms_ref[...] = jnp.zeros_like(terms_ref)
    for place, row in enumerate(rows):
        terms_ref[place : place + 1, :] = row
    start = len(rows)
    heads, offset_count = grad_offsets_ref.shape
    places = lax.broadcasted_iota(jnp.int32, (width // 2, offset_count), 0)
    hot = jnp.where(places == bucket_ref[...], 1.0, 0.0).astype(BF16)
    terms_ref[start : start + heads, : width // 2] = times_hot(
        grad_offsets_ref[...], hot, ((1,), (1,))
    )
    terms = terms_ref[...]
    high = terms.astype(BF16)
    rest = (terms - high.astype(F32)).astype(BF16)
    terms_ref[...] = high.astype(F32) + rest.astype(F32)
    sent_ref[:SMALL_ROWS, :] = high
    sent_ref[SMALL_ROWS:small_rows, :] = rest


def rows_at(ref, start, count):
    return ref[pl.ds(pl.multiple_of(start, 16), count), :]


def add_low(left_side, right_side):
    return (left_side.astype(F32) + right_side.astype(F32)).astype(BF16)


def add_small(terms_ref, came_ref):
    return terms_ref[...] + (
        came_ref[:SMALL_ROWS, :].astype(F32)
        + came_ref[SMALL_ROWS : 2 * SMALL_ROWS, :].astype(F32)
    )


def send_small(small, sent_ref, terms_ref):
    high = small.astype(BF16)
    rest = (small - high.astype(F32)).astype(BF16)
    sent_ref[:SMALL_ROWS, :] = high
    sent_ref[SMALL_ROWS : 2 * SMALL_ROWS, :] = rest
    terms_ref[...] = high.astype(F32) + rest.astype(F32)


def add_kernel(with_small, mine_ref, kept_ref, came_ref, *refs):
    half = kept_ref.shape[0] // 2
    base = 0
    if with_small:
        base = 2 * SMALL_ROWS
        terms_ref, sent_ref, next_ref, new_terms_ref = refs
        send_small(add_small(terms_ref, came_ref), sent_ref, new_terms_ref)
    else:
        sent_ref, next_ref = refs
    mine = mine_ref[0]
    start = (1 - mine) * half
    sent_ref[base:, :] = add_low(
        rows_at(kept_ref, start, half), rows_at(came_ref, base + start, half)
    )
    start = mine * half
    next_ref[...] = add_low(
        rows_at(kept_ref, start, half), rows_at(came_ref, base + start, half)
    )


def join_kernel(with_small, mine_ref, kept_ref, came_ref, kept_two_ref, came_two_ref, *refs):
    start = base = 0
    if with_small:
        start = base = 2 * SMALL_ROWS
        terms_ref, sent_ref, next_ref, next_two_ref, new_terms_ref = refs
        send_small(add_small(terms_ref, came_two_ref), sent_ref, new_terms_ref)
    else:
        sent_ref, next_ref, next_two_ref = refs
    for kept, came, extra, out_ref in (
        (kept_ref, came_ref, 0, next_ref),
        (kept_two_ref, came_two_ref, base, next_two_ref),
    ):
        half = out_ref.shape[0]
        place = (1 - mine_ref[0]) * half
        sent_ref[start : start + half, :] = add_low(
            rows_at(kept, place, half), rows_at(came, extra + place, half)
        )
        start += half
        place = mine_ref[0] * half
        out_ref[...] = add_low(rows_at(kept, place, half), rows_at(came, extra + place, half))


def finish_kernel(with_small, kept_ref, kept_two_ref, came_ref, *refs):
    start = 0
    if with_small:
        start = 2 * SMALL_ROWS
        terms_ref, total_ref, small_ref = refs
        small_ref[...] = add_small(terms_ref, came_ref)
    else:
        (total_ref,) = refs
    out = 0
    for kept in (kept_ref, kept_two_ref):
        count = kept.shape[0]
        total_ref[out : out + count, :] = add_low(kept[...], came_ref[start : start + count, :])
        start += count
        out += count


def place_kernel(mine_ref, own_ref, came_ref, out_ref):
    half = own_ref.shape[0]
    out_ref[pl.ds(pl.multiple_of(mine_ref[0] * half, 16), half), :] = own_ref[...]
    out_ref[pl.ds(pl.multiple_of((1 - mine_ref[0]) * half, 16), half), :] = came_ref[...]


def part_kernel(mine_ref, own_ref, came_ref, first_ref, second_ref):
    start = 0
    for out_ref in (first_ref, second_ref):
        half = out_ref.shape[0] // 2
        for ref, place in ((own_ref, mine_ref[0]), (came_ref, 1 - mine_ref[0])):
            out_ref[pl.ds(pl.multiple_of(place * half, 16), half), :] = ref[
                start : start + half, :
            ]
        start += half


def early_place_kernel(
    flags_ref, first_ref, first_came_ref, second_ref, second_came_ref, down_ref, up_ref
):
    width = down_ref.shape[1]
    units = down_ref.shape[0] // 2
    cut = width // 3
    for parts, halves in (
        ((first_ref, second_ref), (flags_ref[0], flags_ref[1])),
        ((first_came_ref, second_came_ref), (1 - flags_ref[0], 1 - flags_ref[1])),
    ):
        down_ref[pl.ds(pl.multiple_of(halves[0] * units, units), units), :] = parts[0][
            :units, :
        ].astype(F32)
        for part, half, start, first_row, count in (
            (parts[0], halves[0], units, 0, cut // 2),
            (parts[1], halves[1], 0, cut, (width - cut) // 2),
        ):
            place = pl.ds(pl.multiple_of(first_row + half * count, LANES), count)
            for columns in blocks_of(up_ref.shape[1], width):
                up_ref[place, columns] = part[start : start + count, :].astype(F32)
                start += count


def late_place_kernel(flags_ref, first_ref, first_came_ref, query_ref, key_ref, value_ref, out_ref):
    width = first_ref.shape[1]
    head_width = query_ref.shape[1]
    half = width // 2
    count = head_width // 2
    for first, first_half in ((first_ref, flags_ref[0]), (first_came_ref, 1 - flags_ref[0])):
        place = pl.ds(pl.multiple_of(first_half * half, LANES), half)
        query_ref[place, :] = first[:half, :head_width].astype(F32)
        key_ref[place, :] = first[:half, head_width:].astype(F32)
        for part in range(2):
            columns = slice(part * head_width, (part + 1) * head_width)
            rows = pl.ds(pl.multiple_of(first_half * half + part * count, 16), count)
            value_ref[rows, :] = first[half : half + count, columns].astype(F32)
            columns = slice(part * half, (part + 1) * half)
            out_ref[part * count : (part + 1) * count, place] = first[
                half + count :, columns
            ].astype(F32)


def small_kernel(
    rows,
    terms_ref,
    loss_ref,
    mel_ref,
    vocab_ref,
    down_ref,
    gain_two_ref,
    shift_two_ref,
    gain_one_ref,
    shift_one_ref,
    speech_ref,
    up_ref,
    table_ref,
):
    width = down_ref.shape[0]
    loss_ref[...] = terms_ref[0:1, 0:1] * (1.0 / rows)
    mel_ref[...] = terms_ref[0, LANES : LANES + mel_ref.shape[0]]
    vocab_ref[...] = terms_ref[0, 2 * LANES : 2 * LANES + vocab_ref.shape[0]]
    row = 1
    for ref in (down_ref, gain_two_ref, shift_two_ref, gain_one_ref, shift_one_ref, speech_ref):
        ref[...] = terms_ref[row, :]
        row += 1
    for columns in blocks_of(up_ref.shape[0], width):
        up_ref[columns] = terms_ref[row, :]
        row += 1
    table_ref[...] = terms_ref[row : row + table_ref.shape[0], : table_ref.shape[1]]


def shared_place_kernel(
    flags_ref,
    own_ref,
    own_other_ref,
    came_ref,
    came_other_ref,
    speech_ref,
    table_ref,
    mel_ref,
    vocab_ref,
    post_ref,
    hot_ref,
):
    core = flags_ref[2]
    post_rows = LANES // 2
    feat_rows = speech_ref.shape[0] // 4
    hot_rows = LANES // 4
    for ref, place, half in (
        (own_ref, core, flags_ref[1]),
        (came_ref, core, 1 - flags_ref[1]),
        (own_other_ref, 1 - core, flags_ref[1]),
        (came_other_ref, 1 - core, 1 - flags_ref[1]),
    ):
        spot = pl.multiple_of(place * LANES + half * post_rows, 16)
        post_ref[pl.ds(spot, post_rows), :] = ref[:post_rows, :].astype(F32)
        start = post_rows
        spot = pl.multiple_of((place * 2 + half) * feat_rows, 16)
        speech_ref[pl.ds(spot, feat_rows), :] = ref[start : start + feat_rows, :].astype(F32)
        start += feat_rows
        spot = pl.multiple_of((place * 2 + half) * hot_rows, 16)
        hot_ref[pl.ds(spot, hot_rows), :] = ref[start : start + hot_rows, :].astype(F32)
    table_ref[...] = hot_ref[: table_ref.shape[0], :]
    mel_ref[...] = post_ref[: mel_ref.shape[0], :]
    vocab_ref[...] = post_ref[LANES : LANES + vocab_ref.shape[0], :]


def swap_cores(array):
    return lax.ppermute(array, "mp", [(0, 1), (1, 0)])


ORDERS = (((0, 1, 2, 3), (1, 2, 0, 3)), ((2, 0, 1, 3), (2, 0, 1, 3)))
STEPS = 4


class Links:
    def __init__(self, devices, cores, index, core):
        self.devices, self.cores, self.index, self.core = devices, cores, index, core
        self.bits = devices.bit_length() - 1
        self.token = None
        self.pending = []

    def exchange(self, array, directions):
        pairs = [
            (
                place * self.cores + core,
                (place ^ (1 << directions[core])) * self.cores + core,
            )
            for place in range(self.devices)
            for core in range(self.cores)
        ]
        return lax.ppermute(array, ("dp", "mp"), pairs)

    def mine(self, directions):
        direction = jnp.where(self.core == 0, directions[0], directions[1])
        return ((self.index >> direction) & 1).astype(jnp.int32)

    def run(self, kernel, name, flags, operands, outputs, scratch=(), mebibytes=16, after=()):
        results, self.token = run_kernel(
            kernel,
            name,
            0.05,
            flags,
            operands,
            outputs,
            scratch,
            mebibytes,
            after if self.token is None else (self.token, *after),
        )
        return results

    def later(self, kernel, flags, operands, outputs, take):
        self.pending.append((kernel, flags, operands, outputs, take))

    def flush(self, name, after=()):
        pieces, self.pending = self.pending, []
        flags = [flag for piece in pieces for flag in piece[1]]
        operands = [each for piece in pieces for each in piece[2]]
        outputs = [each for piece in pieces for each in piece[3]]

        def kernel(flags_ref, *refs):
            ins, outs = list(refs[: len(operands)]), list(refs[len(operands) :])
            count = 0
            for body, piece_flags, piece_ins, piece_outs, _ in pieces:
                body(
                    *([[flags_ref[count + place] for place in range(len(piece_flags))]] if piece_flags else []),
                    *[ins.pop(0) for _ in piece_ins],
                    *[outs.pop(0) for _ in piece_outs],
                )
                count += len(piece_flags)

        results = self.run(kernel, name, jnp.stack(flags), operands, outputs, after=after)
        for piece in pieces:
            count = len(piece[3])
            piece[4](results[:count])
            results = results[count:]


def step_directions(slot, step):
    return tuple(order[step] for order in ORDERS[slot])


def shape_of(operand):
    return (operand[1] if isinstance(operand, tuple) else operand).shape


class Wave:
    def __init__(self, links, name, sent, kept, terms=None):
        self.links = links
        self.name = name
        self.terms = terms
        self.sent = list(sent)
        self.kept = list(kept)
        self.came = [None, None]

    def scatter(self, step):
        for slot in range(2):
            self.came[slot] = self.links.exchange(self.sent[slot], step_directions(slot, step))

    def piece(self, kernel, directions, operands, outputs, small, take):
        if small:
            operands = operands + [self.terms]
            outputs = outputs + [((SMALL_ROWS, outputs[0][0][1]), F32)]

        def take_all(results):
            if small:
                *results, self.terms = results
            take(results)

        self.links.later(
            functools.partial(kernel, small),
            [] if directions is None else [self.links.mine(directions)],
            operands,
            outputs,
            take_all,
        )

    def add(self, step, distant=False):
        for slot in range(2):
            small = slot == 1 and self.terms is not None
            rows, width = shape_of(self.kept[slot])
            half, extra = rows // 2, 2 * SMALL_ROWS if small else 0

            def take(results, slot=slot):
                self.sent[slot], self.kept[slot] = results

            self.piece(
                add_kernel,
                step_directions(slot, step + 1),
                [self.kept[slot], far(self.came[slot]) if distant else self.came[slot]],
                [
                    ((half + extra, width), BF16),
                    ((half, width), BF16, "far") if step == 0 and distant else ((half, width), BF16),
                ],
                small,
                take,
            )

    def join(self):
        halves = [shape_of(kept)[0] // 2 for kept in self.kept]
        width = shape_of(self.kept[0])[1]
        small = self.terms is not None

        def take(results):
            self.sent_joint, *self.kept = results

        self.piece(
            join_kernel,
            step_directions(0, STEPS - 1),
            [self.kept[0], self.came[0], self.kept[1], self.came[1]],
            [((sum(halves) + (2 * SMALL_ROWS if small else 0), width), BF16)]
            + [((half, width), BF16) for half in halves],
            small,
            take,
        )

    def scatter_joint(self):
        self.came_joint = self.links.exchange(self.sent_joint, step_directions(0, STEPS - 1))

    def finish(self):
        self.counts = [shape_of(kept)[0] for kept in self.kept]
        width = shape_of(self.kept[0])[1]

        def take(results):
            (self.joint,) = results

        self.piece(
            finish_kernel,
            None,
            [*self.kept, self.came_joint],
            [((sum(self.counts), width), BF16)],
            self.terms is not None,
            take,
        )

    def sum_others(self):
        for direction in range(STEPS, self.links.bits):
            both = (direction, direction)
            came = self.links.exchange(self.joint, both)
            self.joint = (self.joint.astype(F32) + came.astype(F32)).astype(BF16)
            if self.terms is not None:
                self.terms = self.terms + self.links.exchange(self.terms, both)

    def gather_joint(self):
        self.came_joint = self.links.exchange(self.joint, step_directions(0, STEPS - 1))

    def part(self):
        width = self.joint.shape[1]

        def take(results):
            self.shares = list(results)

        self.links.later(
            part_kernel,
            [self.links.mine(step_directions(0, STEPS - 1))],
            [self.joint, self.came_joint],
            [((2 * count, width), BF16) for count in self.counts],
            take,
        )

    def gather(self, step):
        self.came = [
            self.links.exchange(rows, step_directions(slot, step))
            for slot, rows in enumerate(self.shares)
        ]

    def place(self, step):
        for slot in range(2):

            def take(results, slot=slot):
                (self.shares[slot],) = results

            rows, width = shape_of(self.shares[slot])
            self.links.later(
                place_kernel,
                [self.links.mine(step_directions(slot, step))],
                [self.shares[slot], self.came[slot]],
                [((2 * rows, width), BF16)],
                take,
            )


def per_device(
    features,
    token_ids,
    mel_target,
    token_target,
    segments,
    row_device,
    offset_bucket,
    speech_weight,
    speech_bias,
    token_table,
    first_gain,
    first_shift,
    query_weight,
    key_weight,
    value_weight,
    bias_table,
    out_weight,
    second_gain,
    second_shift,
    up_weight,
    up_bias,
    down_weight,
    down_bias,
    mel_weight,
    mel_bias,
    vocab_weight,
    vocab_bias,
):
    devices = lax.axis_size("dp")
    device_index = lax.axis_index("dp")
    core = lax.axis_index("mp")
    cores = lax.axis_size("mp")
    rows_speech, part_len, feat_width = features.shape
    rows_total, length = segments.shape
    model_width = speech_weight.shape[1]
    vocab_size = token_table.shape[0]
    mel_width = mel_weight.shape[1]
    local_heads = bias_table.shape[1]
    buckets = bias_table.shape[0]
    head_width = query_weight.shape[1]
    head_size = head_width // local_heads
    units = up_weight.shape[1]
    is_speech = device_index % 2 == 0
    my_row = device_index // 2 + jnp.where(is_speech, 0, rows_speech)
    links = Links(devices, cores, device_index, core)
    flags = jnp.stack(
        [
            core,
            is_speech.astype(jnp.int32),
            1 - links.mine(step_directions(0, 0)),
            1 - links.mine(step_directions(1, 0)),
        ]
    ).astype(jnp.int32)

    plain_width = feat_width + mel_width
    core_width = -(-(plain_width + 2) // (LANES * cores)) * LANES
    ids = jnp.stack([token_ids, token_target], axis=2).astype(BF16)
    (packed,), _ = run_kernel(
        pack_kernel,
        "pack_rows",
        1,
        flags,
        [features, mel_target, ids],
        [((rows_total, part_len, core_width), BF16)],
    )
    arrived = lax.all_to_all(packed, "dp", split_axis=0, concat_axis=0, tiled=True)
    arrived = arrived.reshape(length, core_width)

    my_segments = lax.dynamic_slice_in_dim(segments, my_row, 1)
    segment_column = my_segments.reshape(length, 1)
    bucket_line = jnp.pad(offset_bucket, (0, 1), constant_values=-1).reshape(1, 2 * length)
    (window,), window_token = run_kernel(
        window_kernel,
        "bias_window",
        3,
        flags,
        [bucket_line, bias_table.T],
        [((local_heads, LANES, 2 * length), F32, "far")],
    )
    full_rows = lambda array: jnp.pad(array, ((0, LANES - array.shape[0]), (0, 0)))
    post_bias = jnp.concatenate(
        [jnp.pad(mel_bias, (0, LANES - mel_width)), jnp.pad(vocab_bias, (0, LANES - vocab_size))]
    )
    vectors = jnp.stack(
        [
            jnp.pad(each, (0, units - each.size))
            for each in (
                speech_bias,
                first_gain,
                first_shift,
                second_gain,
                second_shift,
                up_bias,
                down_bias,
                post_bias,
            )
        ]
    )
    token_rows, mel_rows, vocab_rows = (
        full_rows(array) for array in (token_table, mel_weight.T, vocab_weight.T)
    )
    arrived, window_token = lax.optimization_barrier((arrived, window_token))

    model_low = ((length, model_width), BF16)
    head_low = ((length, head_width), BF16)
    (
        embedded,
        attended,
        embedded_far,
        normed_one,
        queries,
        key_rows,
        value_rows,
        heads_flat,
        inputs,
        extra,
    ), _ = run_kernel(
        functools.partial(attend_kernel, head_size, plain_width),
        "embed_and_attend",
        8,
        flags,
        [
            arrived,
            swap_cores(arrived),
            far(speech_weight),
            far(token_rows),
            far(vectors),
            far(query_weight),
            far(key_weight),
            far(value_weight),
            far(out_weight),
            far(window),
            segment_column,
            my_segments,
        ],
        [
            model_low,
            model_low,
            (*model_low, "far"),
            (*model_low, "far"),
            (*head_low, "far"),
            (*head_low, "far"),
            (*head_low, "far"),
            (*head_low, "far"),
            ((length, feat_width + LANES), BF16, "far"),
            ((length, LANES), BF16),
        ],
        [pltpu.VMEM((length, length), F32)],
        mebibytes=26,
        after=(window_token,),
    )
    (mixed, slope, branch, mixed_far, normed_two, active), _ = run_kernel(
        forward_kernel,
        "feed_forward",
        5,
        flags,
        [
            embedded,
            attended,
            swap_cores(attended),
            far(vectors),
            up_weight,
            down_weight,
        ],
        [
            ((length, model_width), F32),
            ((length, units), F32),
            model_low,
            ((length, model_width), F32, "far"),
            model_low,
            ((length, units), BF16),
        ],
        mebibytes=28,
    )
    model_cut = model_width // 3
    folds = units // model_width
    early_shapes = [
        ((units // 2 + model_cut // 2 * folds, model_width), BF16, "far"),
        (((model_width - model_cut) // 2 * folds, model_width), BF16, "far"),
    ]
    (
        *early_parts,
        grad_normed_two,
        grad_final_far,
        final_low,
        grad_post,
        loss_sums,
    ), links.token = run_kernel(
        functools.partial(loss_kernel, mel_width, vocab_size),
        "loss_and_feed_back",
        0.05,
        flags,
        [
            mixed,
            branch,
            swap_cores(branch),
            far(vectors),
            mel_rows,
            vocab_rows,
            extra,
            slope,
            up_weight,
            down_weight,
            active,
            normed_two,
        ],
        early_shapes * 2
        + [
            model_low,
            (*model_low, "far"),
            (*model_low, "far"),
            ((length, 2 * LANES), BF16, "far"),
            ((8, units), F32, "far"),
        ],
        [
            pltpu.VMEM((2 * LANES, model_width), BF16),
            pltpu.VMEM((length, model_width), BF16),
            pltpu.VMEM((length, units), BF16),
        ],
        mebibytes=34,
    )

    early = Wave(links, "early", early_parts[:2], [far(kept) for kept in early_parts[2:]])
    early.scatter(0)
    other_normed_two = swap_cores(grad_normed_two)
    part = ((model_width // 2 + head_width, model_width), BF16)
    post_part = ((LANES // 2, model_width), BF16)
    (
        grad_normed_one,
        late_sent,
        late_kept,
        grad_mixed,
        post_sent,
        post_kept,
        grad_offsets,
        back_sums,
    ) = links.run(
        functools.partial(back_kernel, head_size),
        "attend_back",
        flags,
        [
            grad_normed_two,
            other_normed_two,
            far(mixed_far),
            far(grad_final_far),
            far(vectors),
            far(out_weight),
            far(queries),
            far(key_rows),
            far(value_rows),
            far(window),
            segment_column,
            my_segments,
            far(query_weight),
            far(key_weight),
            far(value_weight),
            far(normed_one),
            far(heads_flat),
            far(grad_post),
            far(final_low),
        ],
        [
            model_low,
            (*part, "far"),
            (*part, "far"),
            ((length, model_width), F32, "far"),
            (*post_part, "far"),
            (*post_part, "far"),
            ((local_heads, 2 * length), F32, "far"),
            ((8, model_width), F32, "far"),
        ],
        [
            pltpu.VMEM((length, model_width), BF16),
            pltpu.VMEM((length, head_width), BF16),
            pltpu.VMEM((length, 3 * head_width), BF16),
            pltpu.VMEM((length, length), F32),
            pltpu.VMEM((length, length), BF16),
            pltpu.VMEM((length, length), BF16),
            pltpu.VMEM((LANES, 2 * length), F32),
            pltpu.VMEM((LANES, model_width), F32),
        ],
        mebibytes=32,
    )
    other_normed_one = swap_cores(grad_normed_one)
    early.add(0, True)
    links.flush("phase_a")
    early.kept = [far(kept) for kept in early.kept]
    early.scatter(1)
    late_rows = LANES + feat_width // 4
    late_second_sent, late_second_kept, feature_back, terms = links.run(
        input_kernel,
        "input_back",
        flags,
        [
            grad_normed_one,
            other_normed_one,
            far(embedded_far),
            far(grad_mixed),
            far(vectors),
            far(speech_weight),
            far(inputs),
            far(post_sent),
            far(post_kept),
            far(loss_sums),
            far(back_sums),
            far(grad_offsets),
            far(bucket_line),
        ],
        [
            ((late_rows + 2 * SMALL_ROWS, model_width), BF16, "far"),
            ((late_rows, model_width), BF16),
            ((length, feat_width // cores), BF16, "far"),
            ((SMALL_ROWS, model_width), F32),
        ],
        [
            pltpu.VMEM((length, model_width), BF16),
            pltpu.VMEM((LANES, model_width), F32),
        ],
        mebibytes=18,
    )
    late = Wave(
        links, "late", [late_sent, late_second_sent], [far(late_kept), late_second_kept], terms
    )
    feature_half = lax.all_to_all(
        feature_back.reshape(devices, part_len, feat_width // cores),
        "dp",
        split_axis=0,
        concat_axis=0,
        tiled=True,
    )
    early.add(1, True)
    links.flush("phase_b")
    early.scatter(2)
    early.join()
    links.flush("phase_c", (feature_half,))
    early.scatter_joint()
    *late.sent, early.sent_joint = lax.optimization_barrier((*late.sent, early.sent_joint))
    late.scatter(0)
    early.finish()
    late.add(0)
    links.flush("phase_d")
    early.sum_others()
    early.gather_joint()
    late.scatter(1)
    feature_half = feature_half.reshape(rows_speech, 2, part_len, feat_width // cores)[:, 0]
    other_feature = swap_cores(feature_half)
    feature_grad = jnp.concatenate(
        [
            jnp.where(core == 0, feature_half, other_feature),
            jnp.where(core == 0, other_feature, feature_half),
        ],
        axis=2,
    )
    early.part()
    late.add(1)
    links.flush("phase_e", (feature_grad,))
    early.gather(2)
    late.scatter(2)
    early.place(2)
    late.join()
    links.flush("phase_f")
    early.gather(1)
    late.scatter_joint()
    early.place(1)
    late.finish()
    links.flush("phase_g")
    late.sum_others()
    early.gather(0)
    late.gather_joint()
    late.part()
    line_out = ((model_width,), F32)
    small = []
    links.later(
        functools.partial(small_kernel, rows_total),
        [],
        [late.terms],
        [((1, 1), F32), ((mel_width,), F32), ((vocab_size,), F32)]
        + [line_out] * 6
        + [((units,), F32), ((local_heads, buckets), F32)],
        small.extend,
    )
    links.flush("phase_h")
    late.gather(2)
    late.place(2)
    links.flush("phase_h2")
    late.gather(1)
    late.place(1)
    links.flush("phase_i", early.came)
    late.gather(0)

    place_flags = jnp.stack(
        [links.mine(step_directions(0, 0)), links.mine(step_directions(1, 0)), core]
    ).astype(jnp.int32)
    grad_down, grad_up = links.run(
        early_place_kernel,
        "early_place",
        place_flags,
        [early.shares[0], far(early.came[0]), early.shares[1], far(early.came[1])],
        [((units, model_width), F32), ((model_width, units), F32)],
        mebibytes=20,
    )
    early_end = links.token
    shared_own, shared_came, _ = lax.optimization_barrier(
        (late.shares[1], late.came[1], early_end)
    )
    shared_own_other, shared_came_other = swap_cores(shared_own), swap_cores(shared_came)
    weight_shape = ((model_width, head_width), F32)
    grad_query, grad_key, grad_value, grad_out = links.run(
        late_place_kernel,
        "late_place",
        place_flags,
        [late.shares[0], late.came[0]],
        [weight_shape, weight_shape, weight_shape, ((head_width, model_width), F32)],
    )
    grad_speech_weight, grad_token_table, grad_mel_weight, grad_vocab_weight = links.run(
        shared_place_kernel,
        "shared_place",
        place_flags,
        [shared_own, shared_own_other, shared_came, shared_came_other],
        [
            ((feat_width, model_width), F32),
            ((vocab_size, model_width), F32),
            ((mel_width, model_width), F32),
            ((vocab_size, model_width), F32),
        ],
        [pltpu.VMEM((2 * LANES, model_width), F32), pltpu.VMEM((LANES, model_width), F32)],
    )
    grad_mel_weight, grad_vocab_weight = grad_mel_weight.T, grad_vocab_weight.T
    (
        loss_total,
        grad_mel_bias,
        grad_vocab_bias,
        grad_down_bias,
        grad_second_gain,
        grad_second_shift,
        grad_first_gain,
        grad_first_shift,
        grad_speech_bias,
        grad_up_bias,
        grad_table,
    ) = small
    return (
        loss_total.reshape(()),
        feature_grad,
        grad_speech_weight,
        grad_speech_bias,
        grad_token_table,
        grad_first_gain,
        grad_first_shift,
        grad_query,
        grad_key,
        grad_value,
        grad_table.T,
        grad_out,
        grad_second_gain,
        grad_second_shift,
        grad_up,
        grad_up_bias,
        grad_down,
        grad_down_bias,
        grad_mel_weight,
        grad_mel_bias,
        grad_vocab_weight,
        grad_vocab_bias,
    )


def solution(mesh):
    placed = (
        P(None, "dp", None),
        P(None, "dp"),
        P(None, "dp", None),
        P(None, "dp"),
        P(),
        P(),
        P(),
        P(),
        P(),
        P(),
        P(),
        P(),
        P(None, "mp"),
        P(None, "mp"),
        P(None, "mp"),
        P(None, "mp"),
        P("mp", None),
        P(),
        P(),
        P(None, "mp"),
        P("mp"),
        P("mp", None),
        P(),
        P(),
        P(),
        P(),
        P(),
    )
    return jax.shard_map(
        per_device,
        mesh=mesh,
        in_specs=placed,
        out_specs=(
            P(),
            P(None, "dp", None),
            P(),
            P(),
            P(),
            P(),
            P(),
            P(None, "mp"),
            P(None, "mp"),
            P(None, "mp"),
            P(None, "mp"),
            P("mp", None),
            P(),
            P(),
            P(None, "mp"),
            P("mp"),
            P("mp", None),
            P(),
            P(),
            P(),
            P(),
            P(),
        ),
        check_vma=False,
    )
```

```python
import functools

import jax
import jax.numpy as jnp
from jax import lax
from jax.experimental import pallas as pl
from jax.experimental.pallas import tpu as pltpu
from jax.sharding import PartitionSpec as P

EPSILON = 1e-05
NEGATIVE = -1e30
HIGHEST = lax.Precision.HIGHEST
BF16 = jnp.bfloat16
F32 = jnp.float32
LANES = 128
SMALL_ROWS = 16


def contract_rows(left_side, right_side):
    return lax.dot_general(
        left_side, right_side, (((0,), (0,)), ((), ())), preferred_element_type=F32
    )


def times_transposed(left_side, right_side):
    return lax.dot_general(
        left_side, right_side, (((1,), (1,)), ((), ())), preferred_element_type=F32
    )


def matmul(left_side, right_side):
    return jnp.dot(left_side, right_side, preferred_element_type=F32)


def normalize(row_data):
    center = row_data - jnp.mean(row_data, axis=-1, keepdims=True)
    inverse = lax.rsqrt(jnp.mean(center * center, axis=-1, keepdims=True) + EPSILON)
    return center * inverse, inverse


def norm_back(grad_out, normal, inverse, norm_gain):
    scaled = grad_out * norm_gain
    return inverse * (
        scaled
        - jnp.mean(scaled, axis=-1, keepdims=True)
        - normal * jnp.mean(scaled * normal, axis=-1, keepdims=True)
    )


def column_sum(array):
    return jnp.sum(array, axis=0, keepdims=True)


def cost(microseconds):
    return pl.CostEstimate(
        flops=0, bytes_accessed=int(microseconds * 3.5e6), transcendentals=0
    )


class Fetched:
    def __init__(self, source, target, semaphore):
        self.copy = pltpu.make_async_copy(source, target, semaphore)
        self.target = target
        self.begun = False
        self.waited = False
        self.shape = target.shape

    def begin(self):
        if not self.begun:
            self.copy.start()
            self.begun = True

    def ready(self):
        self.begin()
        if not self.waited:
            self.copy.wait()
            self.waited = True
        return self.target

    def __getitem__(self, places):
        return self.ready()[places]


class Stored:
    def __init__(self, target, source, semaphore):
        self.copy = pltpu.make_async_copy(source, target, semaphore)
        self.source = source
        self.started = False
        self.shape = source.shape

    def __getitem__(self, places):
        return self.source[places]

    def __setitem__(self, places, value):
        self.source[places] = value

    def flush(self):
        if not self.started:
            self.copy.start()
            self.started = True


def run_kernel(
    kernel, name, microseconds, flags, operands, outputs, scratch=(), mebibytes=16, after=()
):
    in_place = pl.BlockSpec(memory_space=pltpu.VMEM)
    distant = pl.BlockSpec(memory_space=pltpu.HBM)
    after = [
        pltpu.with_memory_space_constraint(array[1], pltpu.HBM)
        if isinstance(array, tuple)
        else array
        for array in after
    ]
    far = [isinstance(operand, tuple) for operand in operands]
    arrays = [
        pltpu.with_memory_space_constraint(operand[1], pltpu.HBM) if is_far else operand
        for operand, is_far in zip(operands, far)
    ]
    out_far = [len(output) == 3 and output[2] == "far" for output in outputs]
    copied = {output[2]: place for place, output in enumerate(outputs) if len(output) == 3}
    fetched = [
        pltpu.VMEM(array.shape, array.dtype)
        for place, (array, is_far) in enumerate(zip(arrays, far))
        if is_far and place not in copied
    ]
    stored = [
        pltpu.VMEM(output[0], output[1]) for output, is_far in zip(outputs, out_far) if is_far
    ]
    moves = sum(far) + sum(out_far)
    semaphores = [pltpu.SemaphoreType.DMA((moves,))] if moves else []

    def with_moves(*refs):
        refs = list(refs)
        semaphore = refs.pop() if moves else None
        buffers = refs[len(refs) - len(fetched) - len(stored) :]
        refs = refs[: len(refs) - len(fetched) - len(stored)]
        first_out = 1 + len(arrays) + len(after)
        count = 0
        came = []
        for place, is_far in enumerate(far):
            if is_far:
                target = refs[first_out + copied[place]] if place in copied else buffers.pop(0)
                refs[place + 1] = Fetched(refs[place + 1], target, semaphore.at[count])
                if operands[place][0] == "far":
                    refs[place + 1].begin()
                came.append(refs[place + 1])
                count += 1
        kept = []
        for place, is_far in enumerate(out_far):
            if is_far:
                refs[first_out + place] = Stored(
                    refs[first_out + place], buffers.pop(0), semaphore.at[count]
                )
                kept.append(refs[first_out + place])
                count += 1
        token_ref = refs[first_out + len(outputs)]
        token_ref[...] = jnp.zeros_like(token_ref)
        kernel(
            *refs[: 1 + len(arrays)],
            *refs[first_out : first_out + len(outputs)],
            *refs[first_out + len(outputs) + 1 :],
        )
        for ref in kept:
            ref.flush()
        for ref in came:
            ref.ready()
        for ref in kept:
            ref.copy.wait()

    *results, token = pl.pallas_call(
        with_moves,
        in_specs=[pl.BlockSpec(memory_space=pltpu.SMEM)]
        + [distant if is_far else in_place for is_far in far]
        + [pl.BlockSpec(memory_space=pl.ANY)] * len(after),
        out_specs=[distant if is_far else in_place for is_far in out_far] + [in_place],
        out_shape=[
            pltpu.HBM(output[0], output[1])
            if is_far
            else jax.ShapeDtypeStruct(output[0], output[1])
            for output, is_far in zip(outputs, out_far)
        ]
        + [jax.ShapeDtypeStruct((8, LANES), F32)],
        scratch_shapes=list(scratch) + fetched + stored + semaphores,
        compiler_params=pltpu.CompilerParams(vmem_limit_bytes=mebibytes * 1024 * 1024),
        cost_estimate=cost(microseconds),
        name=name,
    )(flags, *arrays, *after)
    return results, token


def far(array):
    return ("far", array)


def later(array):
    return ("later", array)


def begin(*refs):
    for ref in refs:
        ref.begin()


def blocks_of(length, size):
    return [slice(start, start + size) for start in range(0, length, size)]


def times_hot(left_side, hot, dims):
    total = 0.0
    for _ in range(3):
        term = left_side.astype(BF16)
        total += lax.dot_general(term, hot, (dims, ((), ())), preferred_element_type=F32)
        left_side = left_side - term.astype(F32)
    return total


def window_kernel(flags_ref, bucket_ref, table_ref, window_ref):
    heads, buckets = table_ref.shape
    width = bucket_ref.shape[1]
    places = lax.broadcasted_iota(jnp.int32, (buckets, width), 0)
    hot = jnp.where(places == bucket_ref[...], 1.0, 0.0).astype(BF16)
    offsets = times_hot(table_ref[...], hot, ((1,), (0,)))
    for head in range(heads):
        spread = jnp.broadcast_to(offsets[head : head + 1, :], (LANES, width))
        window_ref[head] = pltpu.roll(spread, width - LANES + 1, 1, stride=1, stride_axis=0)


def pack_kernel(flags_ref, features_ref, target_ref, ids_ref, sent_ref):
    core_width = sent_ref.shape[2]
    rest = features_ref.shape[2] - core_width
    mel_width = target_ref.shape[2]
    sent_ref[...] = jnp.zeros_like(sent_ref)

    @pl.when(flags_ref[0] == 0)
    def _():
        for row in range(features_ref.shape[0]):
            sent_ref[2 * row] = features_ref[row, :, :core_width]

    @pl.when(flags_ref[0] != 0)
    def _():
        for row in range(features_ref.shape[0]):
            sent_ref[2 * row, :, :rest] = features_ref[row, :, core_width:]
            sent_ref[2 * row, :, rest : rest + mel_width] = target_ref[row]
            start = rest + mel_width
            sent_ref[2 * row + 1, :, start : start + 2] = ids_ref[row]


def key_probs(keys, queries, window_ref, head, mask_ref):
    length = keys.shape[0]
    blocks = length // LANES
    bias = jnp.concatenate(
        [
            window_ref[head, :, LANES * (blocks - 1 - b) : LANES * (blocks - 1 - b) + length]
            for b in range(blocks)
        ],
        axis=0,
    )
    scores = times_transposed(keys, queries) + bias + mask_ref[...]
    powers = jnp.exp(scores - jnp.max(scores, axis=0, keepdims=True))
    return powers * (1.0 / column_sum(powers))


SPEECH_BIAS, FIRST_GAIN, FIRST_SHIFT, SECOND_GAIN, SECOND_SHIFT, UP_BIAS, DOWN_BIAS, POST_BIAS = range(8)


def vector(ref, row, width):
    return ref[row : row + 1, :width]


def attend_kernel(
    head_size,
    plain_width,
    flags_ref,
    own_ref,
    other_ref,
    speech_weight_ref,
    token_table_ref,
    vectors_ref,
    query_weight_ref,
    key_weight_ref,
    value_weight_ref,
    out_weight_ref,
    window_ref,
    column_ref,
    row_ref,
    embedded_ref,
    attended_ref,
    embedded_far_ref,
    normed_ref,
    queries_ref,
    keys_ref,
    values_ref,
    heads_ref,
    inputs_ref,
    extra_ref,
    mask_ref,
):
    length, half_width = own_ref.shape
    width = embedded_ref.shape[1]
    feat_width = inputs_ref.shape[1] - LANES
    first = flags_ref[0] == 0
    speech = flags_ref[1].astype(F32)
    scaling = jnp.asarray(head_size ** (-0.5), BF16)
    for rows in blocks_of(length, LANES):
        own, other = own_ref[rows, :], other_ref[rows, :]
        low = jnp.where(first, own, other)
        high = jnp.where(first, other, own)
        inputs_ref[rows, :half_width] = low
        inputs_ref[rows, half_width:feat_width] = high[:, : feat_width - half_width]
        extra = high[:, feat_width - half_width : feat_width - half_width + LANES]
        extra_ref[rows, :] = extra
        ids = extra[:, plain_width - feat_width : plain_width - feat_width + 1].astype(F32)
        places = lax.broadcasted_iota(jnp.int32, (LANES, LANES), 1).astype(F32)
        hot = jnp.where(ids == places, 1.0 - speech, 0.0)
        inputs_ref[rows, feat_width:] = hot.astype(BF16)
    inputs_ref.flush()
    speech_weight, token_table = speech_weight_ref.ready(), token_table_ref.ready()
    vectors = vectors_ref.ready()
    for rows in blocks_of(length, 2 * LANES):
        embedded = (
            matmul(inputs_ref[rows, :feat_width], speech_weight[...])
            + matmul(inputs_ref[rows, feat_width:], token_table[...])
            + vector(vectors, SPEECH_BIAS, width) * speech
        ).astype(BF16)
        embedded_ref[rows, :] = embedded
        embedded_far_ref[rows, :] = embedded
        normal, _ = normalize(embedded.astype(F32))
        normed_ref[rows, :] = (
            normal * vector(vectors, FIRST_GAIN, width) + vector(vectors, FIRST_SHIFT, width)
        ).astype(BF16)
    embedded_far_ref.flush()
    normed_ref.flush()
    query_weight, key_weight = query_weight_ref.ready(), key_weight_ref.ready()
    value_weight = value_weight_ref.ready()
    for rows in blocks_of(length, 2 * LANES):
        normed = normed_ref[rows, :]
        queries_ref[rows, :] = matmul(normed, query_weight[...]).astype(BF16) * scaling
        keys_ref[rows, :] = matmul(normed, key_weight[...]).astype(BF16)
        values_ref[rows, :] = matmul(normed, value_weight[...]).astype(BF16)
    queries_ref.flush()
    keys_ref.flush()
    values_ref.flush()
    mask_ref[...] = jnp.where(column_ref[...] == row_ref[...], 0.0, NEGATIVE)
    window = window_ref.ready()
    for head, columns in enumerate(blocks_of(queries_ref.shape[1], head_size)):
        probs = key_probs(
            keys_ref[:, columns], queries_ref[:, columns], window, head, mask_ref
        ).astype(BF16)
        heads_ref[:, columns] = contract_rows(probs, values_ref[:, columns]).astype(BF16)
    heads_ref.flush()
    out_weight = out_weight_ref.ready()
    for rows in blocks_of(length, 2 * LANES):
        attended_ref[rows, :] = matmul(heads_ref[rows, :], out_weight[...]).astype(BF16)


def forward_kernel(
    flags_ref,
    embedded_ref,
    own_ref,
    other_ref,
    vectors_ref,
    up_weight_ref,
    down_weight_ref,
    mixed_ref,
    slope_ref,
    branch_ref,
    mixed_far_ref,
    normed_ref,
    active_ref,
):
    length, width = embedded_ref.shape
    units = active_ref.shape[1]
    vectors = vectors_ref.ready()
    for rows in blocks_of(length, 2 * LANES):
        mixed = embedded_ref[rows, :].astype(F32) + (
            own_ref[rows, :].astype(F32) + other_ref[rows, :].astype(F32)
        )
        mixed_ref[rows, :] = mixed
        mixed_far_ref[rows, :] = mixed
        normal, _ = normalize(mixed)
        normed_ref[rows, :] = (
            normal * vector(vectors, SECOND_GAIN, width) + vector(vectors, SECOND_SHIFT, width)
        ).astype(BF16)
    mixed_far_ref.flush()
    for rows in blocks_of(length, 2 * LANES):
        hidden = matmul(normed_ref[rows, :], up_weight_ref[...]) + vector(vectors, UP_BIAS, units)
        square = hidden * hidden
        inner = 0.7978845608028654 * hidden * (1.0 + 0.044715 * square)
        curve = jnp.tanh(inner)
        half = 0.5 * (1.0 + curve)
        active = (hidden * half).astype(BF16)
        active_ref[rows, :] = active
        slope_ref[rows, :] = half + 0.5 * hidden * (1.0 - curve * curve) * (
            0.7978845608028654 * (1.0 + 0.134145 * square)
        )
        branch_ref[rows, :] = matmul(active, down_weight_ref[...]).astype(BF16)


def loss_kernel(
    mel_width,
    vocab_size,
    flags_ref,
    mixed_ref,
    own_ref,
    other_ref,
    vectors_ref,
    mel_weight_ref,
    vocab_weight_ref,
    extra_ref,
    slope_ref,
    up_weight_ref,
    down_weight_ref,
    active_ref,
    normed_ref,
    first_ref,
    second_ref,
    first_kept_ref,
    second_kept_ref,
    grad_normed_ref,
    grad_final_far_ref,
    final_ref,
    grad_post_ref,
    sums_ref,
    post_weight_ref,
    grad_final_ref,
    grad_hidden_ref,
):
    length, width = mixed_ref.shape
    units = slope_ref.shape[1]
    speech = flags_ref[1].astype(F32)
    mel_scale = speech * (1.0 / (mel_width * length))
    text_scale = (1.0 - speech) * (1.0 / length)
    vectors = vectors_ref.ready()
    post_weight_ref[:LANES, :] = mel_weight_ref[...]
    post_weight_ref[LANES:, :] = vocab_weight_ref[...]
    totals = None
    for rows in blocks_of(length, 2 * LANES):
        final = mixed_ref[rows, :] + (
            own_ref[rows, :].astype(F32) + other_ref[rows, :].astype(F32)
        )
        final = (final + vector(vectors, DOWN_BIAS, width)).astype(BF16)
        final_ref[rows, :] = final
        results = times_transposed(final, post_weight_ref[...])
        results += vector(vectors, POST_BIAS, 2 * LANES)
        extra = extra_ref[rows, :].astype(F32)
        places = lax.broadcasted_iota(jnp.int32, extra.shape, 1)
        error = jnp.where(places < mel_width, results[:, :LANES] - extra, 0.0)
        smooth = jnp.sqrt(error * error + 1.0)
        grad_mel = error / smooth * mel_scale
        logits = jnp.where(places < vocab_size, results[:, LANES:], NEGATIVE)
        shifted = logits - jnp.max(logits, axis=-1, keepdims=True)
        powers = jnp.exp(shifted)
        power_sum = jnp.sum(powers, axis=-1, keepdims=True)
        label = extra[:, mel_width + 1 : mel_width + 2] == places.astype(F32)
        picked = jnp.sum(jnp.where(label, shifted, 0.0), axis=-1, keepdims=True)
        text_loss = column_sum(jnp.log(power_sum) - picked) * text_scale
        mel_loss = column_sum((smooth - 1.0) * mel_scale)
        loss = mel_loss + jnp.where(places[:1] == 0, text_loss, 0.0)
        grad_text = (powers / power_sum - jnp.where(label, 1.0, 0.0)) * text_scale
        grad_post = jnp.concatenate([grad_mel, grad_text], axis=1).astype(BF16)
        grad_post_ref[rows, :] = grad_post
        grad_final = matmul(grad_post, post_weight_ref[...]).astype(BF16)
        grad_final_ref[rows, :] = grad_final
        grad_final_far_ref[rows, :] = grad_final
        grad_active = times_transposed(grad_final, down_weight_ref[...])
        grad_hidden = (slope_ref[rows, :] * grad_active).astype(BF16)
        grad_hidden_ref[rows, :] = grad_hidden
        grad_normed_ref[rows, :] = times_transposed(grad_hidden, up_weight_ref[...]).astype(BF16)
        sums = (
            loss,
            column_sum(grad_post.astype(F32)),
            column_sum(grad_final.astype(F32)),
            column_sum(grad_hidden.astype(F32)),
        )
        totals = sums if totals is None else [a + b for a, b in zip(totals, sums)]
    final_ref.flush()
    grad_post_ref.flush()
    grad_final_far_ref.flush()
    sums_ref[...] = jnp.zeros(sums_ref.shape, F32)
    sums_ref[0:1, :LANES] = jnp.broadcast_to(
        jnp.sum(totals[0], axis=1, keepdims=True), (1, LANES)
    )
    sums_ref[0:1, LANES : 3 * LANES] = totals[1]
    sums_ref[1:2, :width] = totals[2]
    sums_ref[2:3, :] = totals[3]
    sums_ref.flush()
    count, block, cut = units // 2, units // 2, width // 2
    for first_half, second_half, first, second in (
        (flags_ref[2], flags_ref[3], first_ref, second_ref),
        (1 - flags_ref[2], 1 - flags_ref[3], first_kept_ref, second_kept_ref),
    ):
        second[...] = contract_rows(
            normed_ref[:, cut:], wide(grad_hidden_ref, second_half * block, block)
        ).astype(BF16)
        second.flush()
        first[:count, :] = contract_rows(
            wide(active_ref, first_half * count, count), grad_final_ref[...]
        ).astype(BF16)
        first[count:, :] = contract_rows(
            normed_ref[:, :cut], wide(grad_hidden_ref, first_half * block, block)
        ).astype(BF16)
        first.flush()


def wide(ref, start, size):
    return ref[:, pl.ds(pl.multiple_of(start, LANES), size)]


def back_kernel(
    head_size,
    flags_ref,
    own_ref,
    other_ref,
    mixed_ref,
    grad_final_ref,
    vectors_ref,
    out_weight_ref,
    queries_ref,
    keys_ref,
    values_ref,
    window_ref,
    column_ref,
    row_ref,
    query_weight_ref,
    key_weight_ref,
    value_weight_ref,
    normed_ref,
    heads_ref,
    grad_post_ref,
    final_ref,
    grad_normed_ref,
    sent_ref,
    kept_ref,
    grad_mixed_ref,
    post_sent_ref,
    post_kept_ref,
    grad_offsets_ref,
    sums_ref,
    grad_low_ref,
    grad_heads_ref,
    grad_projected_ref,
    mask_ref,
    probs_ref,
    scores_ref,
    window_sum_ref,
    post_ref,
):
    length, head_width = queries_ref.shape
    width = grad_low_ref.shape[1]
    blocks = length // LANES
    mixed, grad_final, vectors = mixed_ref.ready(), grad_final_ref.ready(), vectors_ref.ready()
    out_weight = out_weight_ref.ready()
    gain_sum, shift_sum = 0.0, 0.0
    for rows in blocks_of(length, 2 * LANES):
        grad_normed = own_ref[rows, :].astype(F32) + other_ref[rows, :].astype(F32)
        normal, inverse = normalize(mixed[rows, :])
        gain_sum += column_sum(grad_normed * normal)
        shift_sum += column_sum(grad_normed)
        grad_mixed = grad_final[rows, :].astype(F32) + norm_back(
            grad_normed, normal, inverse, vector(vectors, SECOND_GAIN, width)
        )
        grad_mixed_ref[rows, :] = grad_mixed
        grad_low = grad_mixed.astype(BF16)
        grad_low_ref[rows, :] = grad_low
        grad_heads_ref[rows, :] = times_transposed(grad_low, out_weight[...]).astype(BF16)
    grad_mixed_ref.flush()
    sums_ref[...] = jnp.zeros(sums_ref.shape, F32)
    sums_ref[0:1, :] = gain_sum
    sums_ref[1:2, :] = shift_sum
    sums_ref.flush()
    mask_ref[...] = jnp.where(column_ref[...] == row_ref[...], 0.0, NEGATIVE)
    queries_ref, keys_ref, values_ref = queries_ref.ready(), keys_ref.ready(), values_ref.ready()
    window = window_ref.ready()
    scaling = head_size ** (-0.5)
    for head, columns in enumerate(blocks_of(head_width, head_size)):
        keys, queries = keys_ref[:, columns], queries_ref[:, columns]
        grads = grad_heads_ref[:, columns]
        probs = key_probs(keys, queries, window, head, mask_ref)
        weighted = probs * times_transposed(values_ref[:, columns], grads)
        grad_scores = weighted - probs * column_sum(weighted)
        probs_ref[...] = probs.astype(BF16)
        scores_ref[...] = grad_scores.astype(BF16)
        window_sum_ref[...] = jnp.zeros_like(window_sum_ref)
        for block in range(blocks):
            start = LANES * (blocks - 1 - block)
            window_sum_ref[:, start : start + length] += grad_scores[
                LANES * block : LANES * (block + 1)
            ]
        start = head * head_size
        for kind, value in enumerate(
            (
                contract_rows(scores_ref[...], keys) * scaling,
                matmul(scores_ref[...], queries),
                matmul(probs_ref[...], grads),
            )
        ):
            grad_projected_ref[
                :, kind * head_width + start : kind * head_width + start + head_size
            ] = value.astype(BF16)
        diagonal = window_sum_ref[...]
        half = LANES // 2
        while half >= 1:
            diagonal = pltpu.roll(diagonal[:half], half, 1) + diagonal[half:]
            half //= 2
        grad_offsets_ref[head : head + 1, :] = diagonal
    grad_offsets_ref.flush()
    for rows in blocks_of(length, 2 * LANES):
        total = 0.0
        for kind, weight_ref in enumerate((query_weight_ref, key_weight_ref, value_weight_ref)):
            total += times_transposed(
                grad_projected_ref[rows, kind * head_width : (kind + 1) * head_width],
                weight_ref.ready()[...],
            )
        grad_normed_ref[rows, :] = total.astype(BF16)
    normed, heads = normed_ref.ready(), heads_ref.ready()
    grad_post, final = grad_post_ref.ready(), final_ref.ready()
    half = width // 2
    count = head_width // 2
    post_rows = LANES // 2
    post_ref[...] = contract_rows(wide(grad_post, flags_ref[0] * LANES, LANES), final[...])
    for first_ref, post_half_ref, first, second in (
        (sent_ref, post_sent_ref, flags_ref[2], flags_ref[3]),
        (kept_ref, post_kept_ref, 1 - flags_ref[2], 1 - flags_ref[3]),
    ):
        post_half_ref[...] = post_ref[
            pl.ds(pl.multiple_of(second * post_rows, post_rows), post_rows), :
        ].astype(BF16)
        post_half_ref.flush()
        grad_project = contract_rows(
            wide(normed, first * half, half), grad_projected_ref[...]
        ).astype(BF16)
        first_ref[:half, :] = grad_project[:, : 2 * head_width]
        first_ref[half : half + count, :head_width] = grad_project[:count, 2 * head_width :]
        first_ref[half : half + count, head_width:] = grad_project[count:, 2 * head_width :]
        grad_out = contract_rows(heads[...], wide(grad_low_ref, first * half, half))
        first_ref[half + count :, :half] = grad_out[:count].astype(BF16)
        first_ref[half + count :, half:] = grad_out[count:].astype(BF16)
        first_ref.flush()


def input_kernel(
    flags_ref,
    own_ref,
    other_ref,
    embedded_ref,
    grad_mixed_ref,
    vectors_ref,
    speech_weight_ref,
    inputs_ref,
    post_sent_ref,
    post_kept_ref,
    loss_sums_ref,
    back_sums_ref,
    grad_offsets_ref,
    bucket_ref,
    sent_ref,
    kept_ref,
    feature_back_ref,
    terms_ref,
    grad_embedded_ref,
    hot_ref,
):
    length, width = own_ref.shape
    embedded, grad_mixed = embedded_ref.ready(), grad_mixed_ref.ready()
    vectors, speech_weight = vectors_ref.ready(), speech_weight_ref.ready()
    feat_width = speech_weight.shape[0]
    core_width = feat_width // 2
    speech = flags_ref[1].astype(F32)
    core = flags_ref[0]
    gain_sum, shift_sum, bias_sum = 0.0, 0.0, 0.0
    core_weight = speech_weight[pl.ds(pl.multiple_of(core * core_width, core_width), core_width), :]
    for rows in blocks_of(length, 2 * LANES):
        grad_normed = own_ref[rows, :].astype(F32) + other_ref[rows, :].astype(F32)
        normal, inverse = normalize(embedded[rows, :].astype(F32))
        gain_sum += column_sum(grad_normed * normal)
        shift_sum += column_sum(grad_normed)
        grad_embedded = (
            grad_mixed[rows, :]
            + norm_back(grad_normed, normal, inverse, vector(vectors, FIRST_GAIN, width))
        ).astype(BF16)
        grad_embedded_ref[rows, :] = grad_embedded
        bias_sum += column_sum(grad_embedded.astype(F32))
        feature_back_ref[rows, :] = times_transposed(grad_embedded, core_weight).astype(BF16)
    inputs = inputs_ref.ready()
    hot_ref[...] = contract_rows(inputs[:, feat_width:], grad_embedded_ref[...])
    post_rows = LANES // 2
    feat_rows = core_width // 2
    hot_rows = LANES // 4
    small_rows = 2 * SMALL_ROWS
    for which_ref, post_ref, half, base in (
        (sent_ref, post_sent_ref, flags_ref[3], small_rows),
        (kept_ref, post_kept_ref, 1 - flags_ref[3], 0),
    ):
        which_ref[base : base + post_rows, :] = post_ref[...]
        start = base + post_rows
        which_ref[start : start + feat_rows, :] = contract_rows(
            wide(inputs, core * core_width + half * feat_rows, feat_rows), grad_embedded_ref[...]
        ).astype(BF16)
        start += feat_rows
        which_ref[start : start + hot_rows, :] = hot_ref[
            pl.ds(pl.multiple_of(core * 2 * hot_rows + half * hot_rows, hot_rows), hot_rows), :
        ].astype(BF16)
        which_ref[start + hot_rows :, :] = jnp.zeros((hot_rows, width), BF16)
    loss_sums, back_sums = loss_sums_ref.ready(), back_sums_ref.ready()
    bias_rows = loss_sums.shape[1] // width
    rows = [loss_sums[0:1, :width], loss_sums[1:2, :width], back_sums[0:1, :], back_sums[1:2, :]]
    rows += [gain_sum, shift_sum, bias_sum * speech]
    rows += [loss_sums[2:3, part * width : (part + 1) * width] for part in range(bias_rows)]
    terms_ref[...] = jnp.zeros_like(terms_ref)
    for place, row in enumerate(rows):
        terms_ref[place : place + 1, :] = row
    start = len(rows)
    heads, offset_count = grad_offsets_ref.shape
    places = lax.broadcasted_iota(jnp.int32, (width // 2, offset_count), 0)
    hot = jnp.where(places == bucket_ref[...], 1.0, 0.0).astype(BF16)
    terms_ref[start : start + heads, : width // 2] = times_hot(
        grad_offsets_ref[...], hot, ((1,), (1,))
    )
    terms = terms_ref[...]
    high = terms.astype(BF16)
    rest = (terms - high.astype(F32)).astype(BF16)
    terms_ref[...] = high.astype(F32) + rest.astype(F32)
    sent_ref[:SMALL_ROWS, :] = high
    sent_ref[SMALL_ROWS:small_rows, :] = rest


def rows_at(ref, start, count):
    return ref[pl.ds(pl.multiple_of(start, 16), count), :]


def add_low(left_side, right_side):
    return (left_side.astype(F32) + right_side.astype(F32)).astype(BF16)


def add_small(terms_ref, came_ref):
    return terms_ref[...] + (
        came_ref[:SMALL_ROWS, :].astype(F32)
        + came_ref[SMALL_ROWS : 2 * SMALL_ROWS, :].astype(F32)
    )


def send_small(small, sent_ref, terms_ref):
    high = small.astype(BF16)
    rest = (small - high.astype(F32)).astype(BF16)
    sent_ref[:SMALL_ROWS, :] = high
    sent_ref[SMALL_ROWS : 2 * SMALL_ROWS, :] = rest
    terms_ref[...] = high.astype(F32) + rest.astype(F32)


def add_kernel(with_small, mine_ref, kept_ref, came_ref, *refs):
    half = kept_ref.shape[0] // 2
    base = 0
    if with_small:
        base = 2 * SMALL_ROWS
        terms_ref, sent_ref, next_ref, new_terms_ref = refs
        send_small(add_small(terms_ref, came_ref), sent_ref, new_terms_ref)
    else:
        sent_ref, next_ref = refs
    mine = mine_ref[0]
    start = (1 - mine) * half
    sent_ref[base:, :] = add_low(
        rows_at(kept_ref, start, half), rows_at(came_ref, base + start, half)
    )
    start = mine * half
    next_ref[...] = add_low(
        rows_at(kept_ref, start, half), rows_at(came_ref, base + start, half)
    )


def join_kernel(with_small, mine_ref, kept_ref, came_ref, kept_two_ref, came_two_ref, *refs):
    start = base = 0
    if with_small:
        start = base = 2 * SMALL_ROWS
        terms_ref, sent_ref, next_ref, next_two_ref, new_terms_ref = refs
        send_small(add_small(terms_ref, came_two_ref), sent_ref, new_terms_ref)
    else:
        sent_ref, next_ref, next_two_ref = refs
    for kept, came, extra, out_ref in (
        (kept_ref, came_ref, 0, next_ref),
        (kept_two_ref, came_two_ref, base, next_two_ref),
    ):
        half = out_ref.shape[0]
        place = (1 - mine_ref[0]) * half
        sent_ref[start : start + half, :] = add_low(
            rows_at(kept, place, half), rows_at(came, extra + place, half)
        )
        start += half
        place = mine_ref[0] * half
        out_ref[...] = add_low(rows_at(kept, place, half), rows_at(came, extra + place, half))


def finish_kernel(with_small, kept_ref, kept_two_ref, came_ref, *refs):
    start = 0
    if with_small:
        start = 2 * SMALL_ROWS
        terms_ref, total_ref, small_ref = refs
        small_ref[...] = add_small(terms_ref, came_ref)
    else:
        (total_ref,) = refs
    out = 0
    for kept in (kept_ref, kept_two_ref):
        count = kept.shape[0]
        total_ref[out : out + count, :] = add_low(kept[...], came_ref[start : start + count, :])
        start += count
        out += count


def whole_join_kernel(with_small, kept_ref, came_ref, kept_two_ref, came_two_ref, *refs):
    start = base = 0
    if with_small:
        start = base = 2 * SMALL_ROWS
        terms_ref, joint_ref, new_terms_ref = refs
        send_small(add_small(terms_ref, came_two_ref), joint_ref, new_terms_ref)
    else:
        (joint_ref,) = refs
    count = kept_ref.shape[0]
    joint_ref[start : start + count, :] = add_low(kept_ref[...], came_ref[...])
    joint_ref[start + count :, :] = add_low(kept_two_ref[...], came_two_ref[base:, :])


def whole_finish_kernel(with_small, joint_ref, came_ref, *refs):
    start = 0
    if with_small:
        start = 2 * SMALL_ROWS
        terms_ref, *outs, small_ref = refs
        small_ref[...] = add_small(terms_ref, came_ref)
    else:
        outs = refs
    for out_ref in outs:
        rows = slice(start, start + out_ref.shape[0])
        out_ref[...] = add_low(joint_ref[rows, :], came_ref[rows, :])
        start += out_ref.shape[0]


def place_kernel(mine_ref, own_ref, came_ref, out_ref):
    half = own_ref.shape[0]
    out_ref[pl.ds(pl.multiple_of(mine_ref[0] * half, 16), half), :] = own_ref[...]
    out_ref[pl.ds(pl.multiple_of((1 - mine_ref[0]) * half, 16), half), :] = came_ref[...]


def part_kernel(mine_ref, own_ref, came_ref, first_ref, second_ref):
    start = 0
    for out_ref in (first_ref, second_ref):
        half = out_ref.shape[0] // 2
        for ref, place in ((own_ref, mine_ref[0]), (came_ref, 1 - mine_ref[0])):
            out_ref[pl.ds(pl.multiple_of(place * half, 16), half), :] = ref[
                start : start + half, :
            ]
        start += half


def early_place_kernel(
    flags_ref, first_ref, first_came_ref, second_ref, second_came_ref, down_ref, up_ref
):
    width = down_ref.shape[1]
    units = down_ref.shape[0] // 2
    cut = width // 2
    for first, second, first_half, second_half in (
        (first_ref, second_ref, flags_ref[0], flags_ref[1]),
        (first_came_ref, second_came_ref, 1 - flags_ref[0], 1 - flags_ref[1]),
    ):
        down_ref[pl.ds(pl.multiple_of(first_half * units, units), units), :] = first[
            :units, :
        ].astype(F32)
        columns = pl.ds(pl.multiple_of(first_half * units, LANES), units)
        up_ref[:cut, columns] = first[units:, :].astype(F32)
        columns = pl.ds(pl.multiple_of(second_half * units, LANES), units)
        up_ref[cut:, columns] = second[...].astype(F32)


def late_place_kernel(
    half_ref, part_ref, query_ref, key_ref, value_ref, out_ref, *buffers_and_semaphore
):
    *buffers, semaphore = buffers_and_semaphore
    query_buffer, key_buffer, value_buffer, out_buffer = buffers
    width = part_ref.shape[1]
    head_width = query_ref.shape[1]
    half = width // 2
    count = head_width // 2
    place = pl.ds(pl.multiple_of(half_ref[0] * half, LANES), half)
    copies = [
        pltpu.make_async_copy(buffer, target, semaphore.at[number])
        for number, (buffer, target) in enumerate(
            (
                (query_buffer, query_ref.at[place, :]),
                (key_buffer, key_ref.at[place, :]),
                (value_buffer, value_ref.at[place, :]),
                (out_buffer, out_ref.at[:, place]),
            )
        )
    ]
    query_buffer[...] = part_ref[:half, :head_width].astype(F32)
    copies[0].start()
    key_buffer[...] = part_ref[:half, head_width:].astype(F32)
    copies[1].start()
    for part in range(2):
        columns = slice(part * head_width, (part + 1) * head_width)
        value_buffer[part * count : (part + 1) * count, :] = part_ref[
            half : half + count, columns
        ].astype(F32)
    copies[2].start()
    for part in range(2):
        columns = slice(part * half, (part + 1) * half)
        out_buffer[part * count : (part + 1) * count, :] = part_ref[
            half + count :, columns
        ].astype(F32)
    copies[3].start()
    for copy in copies:
        copy.wait()


def place_late(links, half, part, outputs, head_width, after=()):
    width = part.shape[1]
    shapes = [(width, head_width)] * 3 + [(head_width, width)]
    buffers = [(width // 2, head_width)] * 3 + [(head_width, width // 2)]
    distant = pl.BlockSpec(memory_space=pltpu.HBM)
    near = pl.BlockSpec(memory_space=pltpu.VMEM)
    outputs = [] if outputs is None else list(outputs)

    def kernel(half_ref, part_ref, *refs):
        late_place_kernel(half_ref, part_ref, *refs[len(outputs) + len(after) :])

    return pl.pallas_call(
        kernel,
        in_specs=[pl.BlockSpec(memory_space=pltpu.SMEM), near]
        + [distant] * len(outputs)
        + [pl.BlockSpec(memory_space=pl.ANY)] * len(after),
        out_specs=[distant] * 4,
        out_shape=[jax.ShapeDtypeStruct(shape, F32) for shape in shapes],
        input_output_aliases={2 + number: number for number in range(len(outputs))},
        scratch_shapes=[pltpu.VMEM(shape, F32) for shape in buffers]
        + [pltpu.SemaphoreType.DMA((4,))],
        compiler_params=pltpu.CompilerParams(vmem_limit_bytes=16 * 1024 * 1024),
        name="late_place",
    )(half, part, *outputs, *after)


def small_kernel(
    rows,
    terms_ref,
    loss_ref,
    mel_ref,
    vocab_ref,
    down_ref,
    gain_two_ref,
    shift_two_ref,
    gain_one_ref,
    shift_one_ref,
    speech_ref,
    up_ref,
    table_ref,
):
    width = down_ref.shape[0]
    loss_ref[...] = terms_ref[0:1, 0:1] * (1.0 / rows)
    mel_ref[...] = terms_ref[0, LANES : LANES + mel_ref.shape[0]]
    vocab_ref[...] = terms_ref[0, 2 * LANES : 2 * LANES + vocab_ref.shape[0]]
    row = 1
    for ref in (down_ref, gain_two_ref, shift_two_ref, gain_one_ref, shift_one_ref, speech_ref):
        ref[...] = terms_ref[row, :]
        row += 1
    for columns in blocks_of(up_ref.shape[0], width):
        up_ref[columns] = terms_ref[row, :]
        row += 1
    table_ref[...] = terms_ref[row : row + table_ref.shape[0], : table_ref.shape[1]]


def shared_place_kernel(
    flags_ref,
    own_ref,
    own_other_ref,
    came_ref,
    came_other_ref,
    speech_ref,
    table_ref,
    mel_ref,
    vocab_ref,
    post_ref,
    hot_ref,
):
    core = flags_ref[2]
    post_rows = LANES // 2
    feat_rows = speech_ref.shape[0] // 4
    hot_rows = LANES // 4
    for ref, place, half in (
        (own_ref, core, flags_ref[1]),
        (came_ref, core, 1 - flags_ref[1]),
        (own_other_ref, 1 - core, flags_ref[1]),
        (came_other_ref, 1 - core, 1 - flags_ref[1]),
    ):
        spot = pl.multiple_of(place * LANES + half * post_rows, 16)
        post_ref[pl.ds(spot, post_rows), :] = ref[:post_rows, :].astype(F32)
        start = post_rows
        spot = pl.multiple_of((place * 2 + half) * feat_rows, 16)
        speech_ref[pl.ds(spot, feat_rows), :] = ref[start : start + feat_rows, :].astype(F32)
        start += feat_rows
        spot = pl.multiple_of((place * 2 + half) * hot_rows, 16)
        hot_ref[pl.ds(spot, hot_rows), :] = ref[start : start + hot_rows, :].astype(F32)
    table_ref[...] = hot_ref[: table_ref.shape[0], :]
    mel_ref[...] = post_ref[: mel_ref.shape[0], :]
    vocab_ref[...] = post_ref[LANES : LANES + vocab_ref.shape[0], :]


def swap_cores(array):
    return lax.ppermute(array, "mp", [(0, 1), (1, 0)])


ORDERS = (((0, 1, 2, 3), (1, 2, 0, 3)), ((2, 0, 1, 3), (2, 0, 1, 3)))
STEPS = 4


class Links:
    def __init__(self, devices, cores, index, core):
        self.devices, self.cores, self.index, self.core = devices, cores, index, core
        self.bits = devices.bit_length() - 1
        self.token = None
        self.pending = []

    def exchange(self, array, directions):
        pairs = [
            (
                place * self.cores + core,
                (place ^ (1 << directions[core])) * self.cores + core,
            )
            for place in range(self.devices)
            for core in range(self.cores)
        ]
        return lax.ppermute(array, ("dp", "mp"), pairs)

    def mine(self, directions):
        direction = jnp.where(self.core == 0, directions[0], directions[1])
        return ((self.index >> direction) & 1).astype(jnp.int32)

    def run(self, kernel, name, flags, operands, outputs, scratch=(), mebibytes=16, after=()):
        results, self.token = run_kernel(
            kernel,
            name,
            0.05,
            flags,
            operands,
            outputs,
            scratch,
            mebibytes,
            after if self.token is None else (self.token, *after),
        )
        return results

    def later(self, kernel, flags, operands, outputs, take):
        self.pending.append((kernel, flags, operands, outputs, take))

    def flush(self, name, after=()):
        pieces, self.pending = self.pending, []
        flags = [flag for piece in pieces for flag in piece[1]] or [jnp.int32(0)]
        operands = [each for piece in pieces for each in piece[2]]
        outputs = [each for piece in pieces for each in piece[3]]

        def kernel(flags_ref, *refs):
            ins, outs = list(refs[: len(operands)]), list(refs[len(operands) :])
            count = 0
            for body, piece_flags, piece_ins, piece_outs, _ in pieces:
                body(
                    *([[flags_ref[count + place] for place in range(len(piece_flags))]] if piece_flags else []),
                    *[ins.pop(0) for _ in piece_ins],
                    *[outs.pop(0) for _ in piece_outs],
                )
                count += len(piece_flags)

        results = self.run(kernel, name, jnp.stack(flags), operands, outputs, after=after)
        for piece in pieces:
            count = len(piece[3])
            piece[4](results[:count])
            results = results[count:]


def step_directions(slot, step):
    return tuple(order[step] for order in ORDERS[slot])


def shape_of(operand):
    return (operand[1] if isinstance(operand, tuple) else operand).shape


class Wave:
    def __init__(self, links, name, sent, kept, terms=None):
        self.links = links
        self.name = name
        self.terms = terms
        self.sent = list(sent)
        self.kept = list(kept)
        self.came = [None, None]

    def scatter(self, step):
        for slot in range(2):
            self.came[slot] = self.links.exchange(self.sent[slot], step_directions(slot, step))

    def piece(self, kernel, directions, operands, outputs, small, take):
        if small:
            operands = operands + [self.terms]
            outputs = outputs + [((SMALL_ROWS, outputs[0][0][1]), F32)]

        def take_all(results):
            if small:
                *results, self.terms = results
            take(results)

        self.links.later(
            functools.partial(kernel, small),
            [] if directions is None else [self.links.mine(directions)],
            operands,
            outputs,
            take_all,
        )

    def add(self, step, distant=False):
        for slot in range(2):
            small = slot == 1 and self.terms is not None
            rows, width = shape_of(self.kept[slot])
            half, extra = rows // 2, 2 * SMALL_ROWS if small else 0

            def take(results, slot=slot):
                self.sent[slot], self.kept[slot] = results

            self.piece(
                add_kernel,
                step_directions(slot, step + 1),
                [self.kept[slot], far(self.came[slot]) if distant else self.came[slot]],
                [
                    ((half + extra, width), BF16),
                    ((half, width), BF16, "far") if step == 0 and distant else ((half, width), BF16),
                ],
                small,
                take,
            )

    def join(self):
        halves = [shape_of(kept)[0] // 2 for kept in self.kept]
        width = shape_of(self.kept[0])[1]
        small = self.terms is not None

        def take(results):
            self.sent_joint, *self.kept = results

        self.piece(
            join_kernel,
            step_directions(0, STEPS - 1),
            [self.kept[0], self.came[0], self.kept[1], self.came[1]],
            [((sum(halves) + (2 * SMALL_ROWS if small else 0), width), BF16)]
            + [((half, width), BF16) for half in halves],
            small,
            take,
        )

    def scatter_joint(self):
        self.came_joint = self.links.exchange(self.sent_joint, step_directions(0, STEPS - 1))

    def finish(self):
        self.counts = [shape_of(kept)[0] for kept in self.kept]
        width = shape_of(self.kept[0])[1]

        def take(results):
            (self.joint,) = results

        self.piece(
            finish_kernel,
            None,
            [*self.kept, self.came_joint],
            [((sum(self.counts), width), BF16)],
            self.terms is not None,
            take,
        )

    def sum_others(self):
        for direction in range(STEPS, self.links.bits):
            both = (direction, direction)
            came = self.links.exchange(self.joint, both)
            self.joint = (self.joint.astype(F32) + came.astype(F32)).astype(BF16)
            if self.terms is not None:
                self.terms = self.terms + self.links.exchange(self.terms, both)

    def gather_joint(self):
        self.came_joint = self.links.exchange(self.joint, step_directions(0, STEPS - 1))

    def part(self):
        width = self.joint.shape[1]

        def take(results):
            self.shares = list(results)

        self.links.later(
            part_kernel,
            [self.links.mine(step_directions(0, STEPS - 1))],
            [self.joint, self.came_joint],
            [((2 * count, width), BF16) for count in self.counts],
            take,
        )

    def join_whole(self):
        self.counts = [shape_of(kept)[0] for kept in self.kept]
        width = shape_of(self.kept[0])[1]
        small = self.terms is not None

        def take(results):
            (self.joint,) = results

        self.piece(
            whole_join_kernel,
            None,
            [self.kept[0], self.came[0], self.kept[1], self.came[1]],
            [((sum(self.counts) + (2 * SMALL_ROWS if small else 0), width), BF16)],
            small,
            take,
        )

    def exchange_whole(self):
        self.came_joint = self.links.exchange(self.joint, step_directions(0, STEPS - 1))

    def finish_whole(self):
        width = self.joint.shape[1]

        def take(results):
            self.shares = list(results)

        self.piece(
            whole_finish_kernel,
            None,
            [self.joint, self.came_joint],
            [((count, width), BF16) for count in self.counts],
            self.terms is not None,
            take,
        )

    def sum_others_whole(self):
        for direction in range(STEPS, self.links.bits):
            both = (direction, direction)
            self.shares = [
                (share.astype(F32) + self.links.exchange(share, both).astype(F32)).astype(BF16)
                for share in self.shares
            ]

    def gather(self, step):
        self.came = [
            self.links.exchange(rows, step_directions(slot, step))
            for slot, rows in enumerate(self.shares)
        ]

    def place(self, step):
        for slot in range(2):

            def take(results, slot=slot):
                (self.shares[slot],) = results

            rows, width = shape_of(self.shares[slot])
            self.links.later(
                place_kernel,
                [self.links.mine(step_directions(slot, step))],
                [self.shares[slot], self.came[slot]],
                [((2 * rows, width), BF16)],
                take,
            )


def per_device(
    features,
    token_ids,
    mel_target,
    token_target,
    segments,
    row_device,
    offset_bucket,
    speech_weight,
    speech_bias,
    token_table,
    first_gain,
    first_shift,
    query_weight,
    key_weight,
    value_weight,
    bias_table,
    out_weight,
    second_gain,
    second_shift,
    up_weight,
    up_bias,
    down_weight,
    down_bias,
    mel_weight,
    mel_bias,
    vocab_weight,
    vocab_bias,
):
    devices = lax.axis_size("dp")
    device_index = lax.axis_index("dp")
    core = lax.axis_index("mp")
    cores = lax.axis_size("mp")
    rows_speech, part_len, feat_width = features.shape
    rows_total, length = segments.shape
    model_width = speech_weight.shape[1]
    vocab_size = token_table.shape[0]
    mel_width = mel_weight.shape[1]
    local_heads = bias_table.shape[1]
    buckets = bias_table.shape[0]
    head_width = query_weight.shape[1]
    head_size = head_width // local_heads
    units = up_weight.shape[1]
    is_speech = device_index % 2 == 0
    my_row = device_index // 2 + jnp.where(is_speech, 0, rows_speech)
    links = Links(devices, cores, device_index, core)
    flags = jnp.stack(
        [
            core,
            is_speech.astype(jnp.int32),
            1 - links.mine(step_directions(0, 0)),
            1 - links.mine(step_directions(1, 0)),
        ]
    ).astype(jnp.int32)

    plain_width = feat_width + mel_width
    core_width = -(-(plain_width + 2) // (LANES * cores)) * LANES
    ids = jnp.stack([token_ids, token_target], axis=2).astype(BF16)
    (packed,), _ = run_kernel(
        pack_kernel,
        "pack_rows",
        1,
        flags,
        [features, mel_target, ids],
        [((rows_total, part_len, core_width), BF16)],
    )
    arrived = lax.all_to_all(packed, "dp", split_axis=0, concat_axis=0, tiled=True)
    arrived = arrived.reshape(length, core_width)

    my_segments = lax.dynamic_slice_in_dim(segments, my_row, 1)
    segment_column = my_segments.reshape(length, 1)
    bucket_line = jnp.pad(offset_bucket, (0, 1), constant_values=-1).reshape(1, 2 * length)
    (window,), window_token = run_kernel(
        window_kernel,
        "bias_window",
        3,
        flags,
        [bucket_line, bias_table.T],
        [((local_heads, LANES, 2 * length), F32, "far")],
    )
    full_rows = lambda array: jnp.pad(array, ((0, LANES - array.shape[0]), (0, 0)))
    post_bias = jnp.concatenate(
        [jnp.pad(mel_bias, (0, LANES - mel_width)), jnp.pad(vocab_bias, (0, LANES - vocab_size))]
    )
    vectors = jnp.stack(
        [
            jnp.pad(each, (0, units - each.size))
            for each in (
                speech_bias,
                first_gain,
                first_shift,
                second_gain,
                second_shift,
                up_bias,
                down_bias,
                post_bias,
            )
        ]
    )
    token_rows, mel_rows, vocab_rows = (
        full_rows(array) for array in (token_table, mel_weight.T, vocab_weight.T)
    )
    arrived, window_token = lax.optimization_barrier((arrived, window_token))

    model_low = ((length, model_width), BF16)
    head_low = ((length, head_width), BF16)
    (
        embedded,
        attended,
        embedded_far,
        normed_one,
        queries,
        key_rows,
        value_rows,
        heads_flat,
        inputs,
        extra,
    ), _ = run_kernel(
        functools.partial(attend_kernel, head_size, plain_width),
        "embed_and_attend",
        8,
        flags,
        [
            arrived,
            swap_cores(arrived),
            far(speech_weight),
            far(token_rows),
            far(vectors),
            far(query_weight),
            far(key_weight),
            far(value_weight),
            far(out_weight),
            far(window),
            segment_column,
            my_segments,
        ],
        [
            model_low,
            model_low,
            (*model_low, "far"),
            (*model_low, "far"),
            (*head_low, "far"),
            (*head_low, "far"),
            (*head_low, "far"),
            (*head_low, "far"),
            ((length, feat_width + LANES), BF16, "far"),
            ((length, LANES), BF16),
        ],
        [pltpu.VMEM((length, length), F32)],
        mebibytes=26,
        after=(window_token,),
    )
    (mixed, slope, branch, mixed_far, normed_two, active), _ = run_kernel(
        forward_kernel,
        "feed_forward",
        5,
        flags,
        [
            embedded,
            attended,
            swap_cores(attended),
            far(vectors),
            up_weight,
            down_weight,
        ],
        [
            ((length, model_width), F32),
            ((length, units), F32),
            model_low,
            ((length, model_width), F32, "far"),
            model_low,
            ((length, units), BF16),
        ],
        mebibytes=28,
    )
    early_shapes = [
        ((units // 2 + model_width // 2, model_width), BF16, "far"),
        ((model_width // 2, model_width), BF16, "far"),
    ]
    (
        *early_parts,
        grad_normed_two,
        grad_final_far,
        final_low,
        grad_post,
        loss_sums,
    ), links.token = run_kernel(
        functools.partial(loss_kernel, mel_width, vocab_size),
        "loss_and_feed_back",
        0.05,
        flags,
        [
            mixed,
            branch,
            swap_cores(branch),
            far(vectors),
            mel_rows,
            vocab_rows,
            extra,
            slope,
            up_weight,
            down_weight,
            active,
            normed_two,
        ],
        early_shapes * 2
        + [
            model_low,
            (*model_low, "far"),
            (*model_low, "far"),
            ((length, 2 * LANES), BF16, "far"),
            ((8, units), F32, "far"),
        ],
        [
            pltpu.VMEM((2 * LANES, model_width), BF16),
            pltpu.VMEM((length, model_width), BF16),
            pltpu.VMEM((length, units), BF16),
        ],
        mebibytes=34,
    )

    early = Wave(links, "early", early_parts[:2], [far(kept) for kept in early_parts[2:]])
    early.scatter(0)
    other_normed_two = swap_cores(grad_normed_two)
    part = ((model_width // 2 + head_width, model_width), BF16)
    post_part = ((LANES // 2, model_width), BF16)
    (
        grad_normed_one,
        late_sent,
        late_kept,
        grad_mixed,
        post_sent,
        post_kept,
        grad_offsets,
        back_sums,
    ) = links.run(
        functools.partial(back_kernel, head_size),
        "attend_back",
        flags,
        [
            grad_normed_two,
            other_normed_two,
            far(mixed_far),
            far(grad_final_far),
            far(vectors),
            far(out_weight),
            far(queries),
            far(key_rows),
            far(value_rows),
            far(window),
            segment_column,
            my_segments,
            far(query_weight),
            far(key_weight),
            far(value_weight),
            far(normed_one),
            far(heads_flat),
            far(grad_post),
            far(final_low),
        ],
        [
            model_low,
            (*part, "far"),
            (*part, "far"),
            ((length, model_width), F32, "far"),
            (*post_part, "far"),
            (*post_part, "far"),
            ((local_heads, 2 * length), F32, "far"),
            ((8, model_width), F32, "far"),
        ],
        [
            pltpu.VMEM((length, model_width), BF16),
            pltpu.VMEM((length, head_width), BF16),
            pltpu.VMEM((length, 3 * head_width), BF16),
            pltpu.VMEM((length, length), F32),
            pltpu.VMEM((length, length), BF16),
            pltpu.VMEM((length, length), BF16),
            pltpu.VMEM((LANES, 2 * length), F32),
            pltpu.VMEM((LANES, model_width), F32),
        ],
        mebibytes=32,
    )
    other_normed_one = swap_cores(grad_normed_one)
    early.add(0, True)
    links.flush("phase_a")
    early.kept = [far(kept) for kept in early.kept]
    early.scatter(1)
    late_rows = LANES + feat_width // 4
    late_second_sent, late_second_kept, feature_back, terms = links.run(
        input_kernel,
        "input_back",
        flags,
        [
            grad_normed_one,
            other_normed_one,
            far(embedded_far),
            far(grad_mixed),
            far(vectors),
            far(speech_weight),
            far(inputs),
            far(post_sent),
            far(post_kept),
            far(loss_sums),
            far(back_sums),
            far(grad_offsets),
            far(bucket_line),
        ],
        [
            ((late_rows + 2 * SMALL_ROWS, model_width), BF16, "far"),
            ((late_rows, model_width), BF16),
            ((length, feat_width // cores), BF16, "far"),
            ((SMALL_ROWS, model_width), F32),
        ],
        [
            pltpu.VMEM((length, model_width), BF16),
            pltpu.VMEM((LANES, model_width), F32),
        ],
        mebibytes=18,
    )
    late = Wave(
        links, "late", [late_sent, late_second_sent], [far(late_kept), late_second_kept], terms
    )
    feature_half = lax.all_to_all(
        feature_back.reshape(devices, part_len, feat_width // cores),
        "dp",
        split_axis=0,
        concat_axis=0,
        tiled=True,
    )
    early.add(1, True)
    links.flush("phase_b")
    early.scatter(2)
    early.join_whole()
    links.flush("phase_c", (feature_half,))
    early.exchange_whole()
    *late.sent, early.joint = lax.optimization_barrier((*late.sent, early.joint))
    late.scatter(0)
    late.add(0)
    links.flush("phase_d")
    late.scatter(1)
    feature_half = feature_half.reshape(rows_speech, 2, part_len, feat_width // cores)[:, 0]
    other_feature = swap_cores(feature_half)
    feature_grad = jnp.concatenate(
        [
            jnp.where(core == 0, feature_half, other_feature),
            jnp.where(core == 0, other_feature, feature_half),
        ],
        axis=2,
    )
    early.finish_whole()
    late.add(1)
    links.flush("phase_e", (feature_grad,))
    early.sum_others_whole()
    early.gather(2)
    late.scatter(2)
    early.place(2)
    late.join()
    links.flush("phase_f")
    early.gather(1)
    late.scatter_joint()
    early.place(1)
    late.finish()
    links.flush("phase_g")
    late.sum_others()
    early.gather(0)
    late.gather_joint()
    late.part()
    line_out = ((model_width,), F32)
    small = []
    links.later(
        functools.partial(small_kernel, rows_total),
        [],
        [late.terms],
        [((1, 1), F32), ((mel_width,), F32), ((vocab_size,), F32)]
        + [line_out] * 6
        + [((units,), F32), ((local_heads, buckets), F32)],
        small.extend,
    )
    links.flush("phase_h")
    late.gather(2)
    late.place(2)
    links.flush("phase_h2")
    late.gather(1)
    late.place(1)
    links.flush("phase_i", early.came)
    late.gather(0)

    place_flags = jnp.stack(
        [links.mine(step_directions(0, 0)), links.mine(step_directions(1, 0)), core]
    ).astype(jnp.int32)
    grad_down, grad_up = links.run(
        early_place_kernel,
        "early_place",
        place_flags,
        [early.shares[0], far(early.came[0]), early.shares[1], far(early.came[1])],
        [((units, model_width), F32), ((model_width, units), F32)],
        mebibytes=20,
    )
    early_end = links.token
    grad_query, grad_key, grad_value, grad_out = place_late(
        links, place_flags[:1], late.shares[0], None, head_width, after=(early_end,)
    )
    shared_own, shared_came, _ = lax.optimization_barrier(
        (late.shares[1], late.came[1], early_end)
    )
    shared_own_other, shared_came_other = swap_cores(shared_own), swap_cores(shared_came)
    grad_speech_weight, grad_token_table, grad_mel_weight, grad_vocab_weight = links.run(
        shared_place_kernel,
        "shared_place",
        place_flags,
        [shared_own, shared_own_other, shared_came, shared_came_other],
        [
            ((feat_width, model_width), F32),
            ((vocab_size, model_width), F32),
            ((mel_width, model_width), F32),
            ((vocab_size, model_width), F32),
        ],
        [pltpu.VMEM((2 * LANES, model_width), F32), pltpu.VMEM((LANES, model_width), F32)],
        after=(far(grad_query),),
    )
    grad_query, grad_key, grad_value, grad_out = place_late(
        links,
        1 - place_flags[:1],
        late.came[0],
        (grad_query, grad_key, grad_value, grad_out),
        head_width,
    )
    grad_mel_weight, grad_vocab_weight = grad_mel_weight.T, grad_vocab_weight.T
    (
        loss_total,
        grad_mel_bias,
        grad_vocab_bias,
        grad_down_bias,
        grad_second_gain,
        grad_second_shift,
        grad_first_gain,
        grad_first_shift,
        grad_speech_bias,
        grad_up_bias,
        grad_table,
    ) = small
    return (
        loss_total.reshape(()),
        feature_grad,
        grad_speech_weight,
        grad_speech_bias,
        grad_token_table,
        grad_first_gain,
        grad_first_shift,
        grad_query,
        grad_key,
        grad_value,
        grad_table.T,
        grad_out,
        grad_second_gain,
        grad_second_shift,
        grad_up,
        grad_up_bias,
        grad_down,
        grad_down_bias,
        grad_mel_weight,
        grad_mel_bias,
        grad_vocab_weight,
        grad_vocab_bias,
    )


def solution(mesh):
    placed = (
        P(None, "dp", None),
        P(None, "dp"),
        P(None, "dp", None),
        P(None, "dp"),
        P(),
        P(),
        P(),
        P(),
        P(),
        P(),
        P(),
        P(),
        P(None, "mp"),
        P(None, "mp"),
        P(None, "mp"),
        P(None, "mp"),
        P("mp", None),
        P(),
        P(),
        P(None, "mp"),
        P("mp"),
        P("mp", None),
        P(),
        P(),
        P(),
        P(),
        P(),
    )
    return jax.shard_map(
        per_device,
        mesh=mesh,
        in_specs=placed,
        out_specs=(
            P(),
            P(None, "dp", None),
            P(),
            P(),
            P(),
            P(),
            P(),
            P(None, "mp"),
            P(None, "mp"),
            P(None, "mp"),
            P(None, "mp"),
            P("mp", None),
            P(),
            P(),
            P(None, "mp"),
            P("mp"),
            P("mp", None),
            P(),
            P(),
            P(),
            P(),
            P(),
        ),
        check_vma=False,
    )
```

```python
import functools

import jax
import jax.numpy as jnp
from jax import lax
from jax.experimental import pallas as pl
from jax.experimental.pallas import tpu as pltpu
from jax.sharding import PartitionSpec as P

EPSILON = 1e-05
NEGATIVE = -1e30
HIGHEST = lax.Precision.HIGHEST
BF16 = jnp.bfloat16
F32 = jnp.float32
LANES = 128
SMALL_ROWS = 16


def contract_rows(left_side, right_side):
    return lax.dot_general(
        left_side, right_side, (((0,), (0,)), ((), ())), preferred_element_type=F32
    )


def times_transposed(left_side, right_side):
    return lax.dot_general(
        left_side, right_side, (((1,), (1,)), ((), ())), preferred_element_type=F32
    )


def matmul(left_side, right_side):
    return jnp.dot(left_side, right_side, preferred_element_type=F32)


def normalize(row_data):
    center = row_data - jnp.mean(row_data, axis=-1, keepdims=True)
    inverse = lax.rsqrt(jnp.mean(center * center, axis=-1, keepdims=True) + EPSILON)
    return center * inverse, inverse


def norm_back(grad_out, normal, inverse, norm_gain):
    scaled = grad_out * norm_gain
    return inverse * (
        scaled
        - jnp.mean(scaled, axis=-1, keepdims=True)
        - normal * jnp.mean(scaled * normal, axis=-1, keepdims=True)
    )


def column_sum(array):
    return jnp.sum(array, axis=0, keepdims=True)


def cost(microseconds):
    return pl.CostEstimate(
        flops=0, bytes_accessed=int(microseconds * 3.5e6), transcendentals=0
    )


class Fetched:
    def __init__(self, source, target, semaphore):
        self.copy = pltpu.make_async_copy(source, target, semaphore)
        self.target = target
        self.begun = False
        self.waited = False
        self.shape = target.shape

    def begin(self):
        if not self.begun:
            self.copy.start()
            self.begun = True

    def ready(self):
        self.begin()
        if not self.waited:
            self.copy.wait()
            self.waited = True
        return self.target

    def __getitem__(self, places):
        return self.ready()[places]


class Stored:
    def __init__(self, target, source, semaphore):
        self.copy = pltpu.make_async_copy(source, target, semaphore)
        self.source = source
        self.started = False
        self.shape = source.shape

    def __getitem__(self, places):
        return self.source[places]

    def __setitem__(self, places, value):
        self.source[places] = value

    def flush(self):
        if not self.started:
            self.copy.start()
            self.started = True


def run_kernel(
    kernel, name, microseconds, flags, operands, outputs, scratch=(), mebibytes=16, after=()
):
    in_place = pl.BlockSpec(memory_space=pltpu.VMEM)
    distant = pl.BlockSpec(memory_space=pltpu.HBM)
    after = [
        pltpu.with_memory_space_constraint(array[1], pltpu.HBM)
        if isinstance(array, tuple)
        else array
        for array in after
    ]
    far = [isinstance(operand, tuple) for operand in operands]
    arrays = [
        pltpu.with_memory_space_constraint(operand[1], pltpu.HBM) if is_far else operand
        for operand, is_far in zip(operands, far)
    ]
    out_far = [len(output) == 3 and output[2] == "far" for output in outputs]
    copied = {output[2]: place for place, output in enumerate(outputs) if len(output) == 3}
    fetched = [
        pltpu.VMEM(array.shape, array.dtype)
        for place, (array, is_far) in enumerate(zip(arrays, far))
        if is_far and place not in copied
    ]
    stored = [
        pltpu.VMEM(output[0], output[1]) for output, is_far in zip(outputs, out_far) if is_far
    ]
    moves = sum(far) + sum(out_far)
    semaphores = [pltpu.SemaphoreType.DMA((moves,))] if moves else []

    def with_moves(*refs):
        refs = list(refs)
        semaphore = refs.pop() if moves else None
        buffers = refs[len(refs) - len(fetched) - len(stored) :]
        refs = refs[: len(refs) - len(fetched) - len(stored)]
        first_out = 1 + len(arrays) + len(after)
        count = 0
        came = []
        for place, is_far in enumerate(far):
            if is_far:
                target = refs[first_out + copied[place]] if place in copied else buffers.pop(0)
                refs[place + 1] = Fetched(refs[place + 1], target, semaphore.at[count])
                if operands[place][0] == "far":
                    refs[place + 1].begin()
                came.append(refs[place + 1])
                count += 1
        kept = []
        for place, is_far in enumerate(out_far):
            if is_far:
                refs[first_out + place] = Stored(
                    refs[first_out + place], buffers.pop(0), semaphore.at[count]
                )
                kept.append(refs[first_out + place])
                count += 1
        token_ref = refs[first_out + len(outputs)]
        token_ref[...] = jnp.zeros_like(token_ref)
        kernel(
            *refs[: 1 + len(arrays)],
            *refs[first_out : first_out + len(outputs)],
            *refs[first_out + len(outputs) + 1 :],
        )
        for ref in kept:
            ref.flush()
        for ref in came:
            ref.ready()
        for ref in kept:
            ref.copy.wait()

    *results, token = pl.pallas_call(
        with_moves,
        in_specs=[pl.BlockSpec(memory_space=pltpu.SMEM)]
        + [distant if is_far else in_place for is_far in far]
        + [pl.BlockSpec(memory_space=pl.ANY)] * len(after),
        out_specs=[distant if is_far else in_place for is_far in out_far] + [in_place],
        out_shape=[
            pltpu.HBM(output[0], output[1])
            if is_far
            else jax.ShapeDtypeStruct(output[0], output[1])
            for output, is_far in zip(outputs, out_far)
        ]
        + [jax.ShapeDtypeStruct((8, LANES), F32)],
        scratch_shapes=list(scratch) + fetched + stored + semaphores,
        compiler_params=pltpu.CompilerParams(vmem_limit_bytes=mebibytes * 1024 * 1024),
        cost_estimate=cost(microseconds),
        name=name,
    )(flags, *arrays, *after)
    return results, token


def far(array):
    return ("far", array)


def later(array):
    return ("later", array)


def begin(*refs):
    for ref in refs:
        ref.begin()


def blocks_of(length, size):
    return [slice(start, start + size) for start in range(0, length, size)]


def times_hot(left_side, hot, dims):
    total = 0.0
    for _ in range(3):
        term = left_side.astype(BF16)
        total += lax.dot_general(term, hot, (dims, ((), ())), preferred_element_type=F32)
        left_side = left_side - term.astype(F32)
    return total


def window_kernel(flags_ref, bucket_ref, table_ref, window_ref):
    heads, buckets = table_ref.shape
    width = bucket_ref.shape[1]
    places = lax.broadcasted_iota(jnp.int32, (buckets, width), 0)
    hot = jnp.where(places == bucket_ref[...], 1.0, 0.0).astype(BF16)
    offsets = times_hot(table_ref[...], hot, ((1,), (0,)))
    for head in range(heads):
        spread = jnp.broadcast_to(offsets[head : head + 1, :], (LANES, width))
        window_ref[head] = pltpu.roll(spread, width - LANES + 1, 1, stride=1, stride_axis=0)


def pack_kernel(flags_ref, features_ref, target_ref, ids_ref, sent_ref):
    core_width = sent_ref.shape[2]
    rest = features_ref.shape[2] - core_width
    mel_width = target_ref.shape[2]
    sent_ref[...] = jnp.zeros_like(sent_ref)
    features, target = features_ref.ready(), target_ref.ready()

    @pl.when(flags_ref[0] == 0)
    def _():
        for row in range(features_ref.shape[0]):
            sent_ref[2 * row] = features[row, :, :core_width]

    @pl.when(flags_ref[0] != 0)
    def _():
        for row in range(features_ref.shape[0]):
            sent_ref[2 * row, :, :rest] = features[row, :, core_width:]
            sent_ref[2 * row, :, rest : rest + mel_width] = target[row]
            start = rest + mel_width
            sent_ref[2 * row + 1, :, start : start + 2] = ids_ref[row]


def key_probs(keys, queries, window_ref, head, mask_ref):
    length = keys.shape[0]
    blocks = length // LANES
    bias = jnp.concatenate(
        [
            window_ref[head, :, LANES * (blocks - 1 - b) : LANES * (blocks - 1 - b) + length]
            for b in range(blocks)
        ],
        axis=0,
    )
    scores = times_transposed(keys, queries) + bias + mask_ref[...]
    powers = jnp.exp(scores - jnp.max(scores, axis=0, keepdims=True))
    return powers * (1.0 / column_sum(powers))


SPEECH_BIAS, FIRST_GAIN, FIRST_SHIFT, SECOND_GAIN, SECOND_SHIFT, UP_BIAS, DOWN_BIAS, POST_BIAS = range(8)


def vector(ref, row, width):
    return ref[row : row + 1, :width]


def attend_kernel(
    head_size,
    plain_width,
    flags_ref,
    own_ref,
    other_ref,
    speech_weight_ref,
    token_table_ref,
    vectors_ref,
    query_weight_ref,
    key_weight_ref,
    value_weight_ref,
    out_weight_ref,
    window_ref,
    column_ref,
    row_ref,
    embedded_ref,
    attended_ref,
    embedded_far_ref,
    normed_ref,
    queries_ref,
    keys_ref,
    values_ref,
    heads_ref,
    inputs_ref,
    extra_ref,
    mask_ref,
):
    length, half_width = own_ref.shape
    width = embedded_ref.shape[1]
    feat_width = inputs_ref.shape[1] - LANES
    first = flags_ref[0] == 0
    speech = flags_ref[1].astype(F32)
    scaling = jnp.asarray(head_size ** (-0.5), BF16)
    for rows in blocks_of(length, LANES):
        own, other = own_ref[rows, :], other_ref[rows, :]
        low = jnp.where(first, own, other)
        high = jnp.where(first, other, own)
        inputs_ref[rows, :half_width] = low
        inputs_ref[rows, half_width:feat_width] = high[:, : feat_width - half_width]
        extra = high[:, feat_width - half_width : feat_width - half_width + LANES]
        extra_ref[rows, :] = extra
        ids = extra[:, plain_width - feat_width : plain_width - feat_width + 1].astype(F32)
        places = lax.broadcasted_iota(jnp.int32, (LANES, LANES), 1).astype(F32)
        hot = jnp.where(ids == places, 1.0 - speech, 0.0)
        inputs_ref[rows, feat_width:] = hot.astype(BF16)
    inputs_ref.flush()
    speech_weight, token_table = speech_weight_ref.ready(), token_table_ref.ready()
    vectors = vectors_ref.ready()
    for rows in blocks_of(length, 2 * LANES):
        embedded = (
            matmul(inputs_ref[rows, :feat_width], speech_weight[...])
            + matmul(inputs_ref[rows, feat_width:], token_table[...])
            + vector(vectors, SPEECH_BIAS, width) * speech
        ).astype(BF16)
        embedded_ref[rows, :] = embedded
        embedded_far_ref[rows, :] = embedded
        normal, _ = normalize(embedded.astype(F32))
        normed_ref[rows, :] = (
            normal * vector(vectors, FIRST_GAIN, width) + vector(vectors, FIRST_SHIFT, width)
        ).astype(BF16)
    embedded_far_ref.flush()
    normed_ref.flush()
    query_weight, key_weight = query_weight_ref.ready(), key_weight_ref.ready()
    value_weight = value_weight_ref.ready()
    for rows in blocks_of(length, 2 * LANES):
        normed = normed_ref[rows, :]
        queries_ref[rows, :] = matmul(normed, query_weight[...]).astype(BF16) * scaling
        keys_ref[rows, :] = matmul(normed, key_weight[...]).astype(BF16)
        values_ref[rows, :] = matmul(normed, value_weight[...]).astype(BF16)
    queries_ref.flush()
    keys_ref.flush()
    values_ref.flush()
    mask_ref[...] = jnp.where(column_ref[...] == row_ref[...], 0.0, NEGATIVE)
    window = window_ref.ready()
    for head, columns in enumerate(blocks_of(queries_ref.shape[1], head_size)):
        probs = key_probs(
            keys_ref[:, columns], queries_ref[:, columns], window, head, mask_ref
        ).astype(BF16)
        heads_ref[:, columns] = contract_rows(probs, values_ref[:, columns]).astype(BF16)
    heads_ref.flush()
    out_weight = out_weight_ref.ready()
    for rows in blocks_of(length, 2 * LANES):
        attended_ref[rows, :] = matmul(heads_ref[rows, :], out_weight[...]).astype(BF16)


def forward_kernel(
    flags_ref,
    embedded_ref,
    own_ref,
    other_ref,
    vectors_ref,
    up_weight_ref,
    down_weight_ref,
    mixed_ref,
    slope_ref,
    branch_ref,
    mixed_far_ref,
    normed_ref,
    active_ref,
):
    length, width = embedded_ref.shape
    units = active_ref.shape[1]
    vectors = vectors_ref.ready()
    for rows in blocks_of(length, 2 * LANES):
        mixed = embedded_ref[rows, :].astype(F32) + (
            own_ref[rows, :].astype(F32) + other_ref[rows, :].astype(F32)
        )
        mixed_ref[rows, :] = mixed
        mixed_far_ref[rows, :] = mixed
        normal, _ = normalize(mixed)
        normed_ref[rows, :] = (
            normal * vector(vectors, SECOND_GAIN, width) + vector(vectors, SECOND_SHIFT, width)
        ).astype(BF16)
    mixed_far_ref.flush()
    for rows in blocks_of(length, 2 * LANES):
        hidden = matmul(normed_ref[rows, :], up_weight_ref[...]) + vector(vectors, UP_BIAS, units)
        square = hidden * hidden
        inner = 0.7978845608028654 * hidden * (1.0 + 0.044715 * square)
        curve = jnp.tanh(inner)
        half = 0.5 * (1.0 + curve)
        active = (hidden * half).astype(BF16)
        active_ref[rows, :] = active
        slope_ref[rows, :] = half + 0.5 * hidden * (1.0 - curve * curve) * (
            0.7978845608028654 * (1.0 + 0.134145 * square)
        )
        branch_ref[rows, :] = matmul(active, down_weight_ref[...]).astype(BF16)


def loss_kernel(
    mel_width,
    vocab_size,
    flags_ref,
    mixed_ref,
    own_ref,
    other_ref,
    vectors_ref,
    mel_weight_ref,
    vocab_weight_ref,
    extra_ref,
    slope_ref,
    up_weight_ref,
    down_weight_ref,
    active_ref,
    normed_ref,
    first_ref,
    second_ref,
    first_kept_ref,
    second_kept_ref,
    grad_normed_ref,
    grad_final_far_ref,
    final_ref,
    grad_post_ref,
    sums_ref,
    post_weight_ref,
    grad_final_ref,
    grad_hidden_ref,
):
    length, width = mixed_ref.shape
    units = slope_ref.shape[1]
    speech = flags_ref[1].astype(F32)
    mel_scale = speech * (1.0 / (mel_width * length))
    text_scale = (1.0 - speech) * (1.0 / length)
    vectors = vectors_ref.ready()
    post_weight_ref[:LANES, :] = mel_weight_ref[...]
    post_weight_ref[LANES:, :] = vocab_weight_ref[...]
    totals = None
    for rows in blocks_of(length, 2 * LANES):
        final = mixed_ref[rows, :] + (
            own_ref[rows, :].astype(F32) + other_ref[rows, :].astype(F32)
        )
        final = (final + vector(vectors, DOWN_BIAS, width)).astype(BF16)
        final_ref[rows, :] = final
        results = times_transposed(final, post_weight_ref[...])
        results += vector(vectors, POST_BIAS, 2 * LANES)
        extra = extra_ref[rows, :].astype(F32)
        places = lax.broadcasted_iota(jnp.int32, extra.shape, 1)
        error = jnp.where(places < mel_width, results[:, :LANES] - extra, 0.0)
        smooth = jnp.sqrt(error * error + 1.0)
        grad_mel = error / smooth * mel_scale
        logits = jnp.where(places < vocab_size, results[:, LANES:], NEGATIVE)
        shifted = logits - jnp.max(logits, axis=-1, keepdims=True)
        powers = jnp.exp(shifted)
        power_sum = jnp.sum(powers, axis=-1, keepdims=True)
        label = extra[:, mel_width + 1 : mel_width + 2] == places.astype(F32)
        picked = jnp.sum(jnp.where(label, shifted, 0.0), axis=-1, keepdims=True)
        text_loss = column_sum(jnp.log(power_sum) - picked) * text_scale
        mel_loss = column_sum((smooth - 1.0) * mel_scale)
        loss = mel_loss + jnp.where(places[:1] == 0, text_loss, 0.0)
        grad_text = (powers / power_sum - jnp.where(label, 1.0, 0.0)) * text_scale
        grad_post = jnp.concatenate([grad_mel, grad_text], axis=1).astype(BF16)
        grad_post_ref[rows, :] = grad_post
        grad_final = matmul(grad_post, post_weight_ref[...]).astype(BF16)
        grad_final_ref[rows, :] = grad_final
        grad_final_far_ref[rows, :] = grad_final
        grad_active = times_transposed(grad_final, down_weight_ref[...])
        grad_hidden = (slope_ref[rows, :] * grad_active).astype(BF16)
        grad_hidden_ref[rows, :] = grad_hidden
        grad_normed_ref[rows, :] = times_transposed(grad_hidden, up_weight_ref[...]).astype(BF16)
        sums = (
            loss,
            column_sum(grad_post.astype(F32)),
            column_sum(grad_final.astype(F32)),
            column_sum(grad_hidden.astype(F32)),
        )
        totals = sums if totals is None else [a + b for a, b in zip(totals, sums)]
    final_ref.flush()
    grad_post_ref.flush()
    grad_final_far_ref.flush()
    sums_ref[...] = jnp.zeros(sums_ref.shape, F32)
    sums_ref[0:1, :LANES] = jnp.broadcast_to(
        jnp.sum(totals[0], axis=1, keepdims=True), (1, LANES)
    )
    sums_ref[0:1, LANES : 3 * LANES] = totals[1]
    sums_ref[1:2, :width] = totals[2]
    sums_ref[2:3, :] = totals[3]
    sums_ref.flush()
    count, block, cut = units // 2, units // 2, width // 2
    for first_half, second_half, first, second in (
        (flags_ref[2], flags_ref[3], first_ref, second_ref),
        (1 - flags_ref[2], 1 - flags_ref[3], first_kept_ref, second_kept_ref),
    ):
        second[...] = contract_rows(
            normed_ref[:, cut:], wide(grad_hidden_ref, second_half * block, block)
        ).astype(BF16)
        second.flush()
        first[:count, :] = contract_rows(
            wide(active_ref, first_half * count, count), grad_final_ref[...]
        ).astype(BF16)
        first[count:, :] = contract_rows(
            normed_ref[:, :cut], wide(grad_hidden_ref, first_half * block, block)
        ).astype(BF16)
        first.flush()


def wide(ref, start, size):
    return ref[:, pl.ds(pl.multiple_of(start, LANES), size)]


def back_kernel(
    head_size,
    flags_ref,
    own_ref,
    other_ref,
    mixed_ref,
    grad_final_ref,
    vectors_ref,
    out_weight_ref,
    queries_ref,
    keys_ref,
    values_ref,
    window_ref,
    column_ref,
    row_ref,
    query_weight_ref,
    key_weight_ref,
    value_weight_ref,
    normed_ref,
    heads_ref,
    grad_post_ref,
    final_ref,
    grad_normed_ref,
    sent_ref,
    kept_ref,
    grad_mixed_ref,
    post_sent_ref,
    post_kept_ref,
    grad_offsets_ref,
    sums_ref,
    grad_low_ref,
    grad_heads_ref,
    grad_projected_ref,
    mask_ref,
    probs_ref,
    scores_ref,
    window_sum_ref,
    post_ref,
):
    length, head_width = queries_ref.shape
    width = grad_low_ref.shape[1]
    blocks = length // LANES
    mixed, grad_final, vectors = mixed_ref.ready(), grad_final_ref.ready(), vectors_ref.ready()
    out_weight = out_weight_ref.ready()
    gain_sum, shift_sum = 0.0, 0.0
    for rows in blocks_of(length, 2 * LANES):
        grad_normed = own_ref[rows, :].astype(F32) + other_ref[rows, :].astype(F32)
        normal, inverse = normalize(mixed[rows, :])
        gain_sum += column_sum(grad_normed * normal)
        shift_sum += column_sum(grad_normed)
        grad_mixed = grad_final[rows, :].astype(F32) + norm_back(
            grad_normed, normal, inverse, vector(vectors, SECOND_GAIN, width)
        )
        grad_mixed_ref[rows, :] = grad_mixed
        grad_low = grad_mixed.astype(BF16)
        grad_low_ref[rows, :] = grad_low
        grad_heads_ref[rows, :] = times_transposed(grad_low, out_weight[...]).astype(BF16)
    grad_mixed_ref.flush()
    sums_ref[...] = jnp.zeros(sums_ref.shape, F32)
    sums_ref[0:1, :] = gain_sum
    sums_ref[1:2, :] = shift_sum
    sums_ref.flush()
    mask_ref[...] = jnp.where(column_ref[...] == row_ref[...], 0.0, NEGATIVE)
    queries_ref, keys_ref, values_ref = queries_ref.ready(), keys_ref.ready(), values_ref.ready()
    window = window_ref.ready()
    scaling = head_size ** (-0.5)
    for head, columns in enumerate(blocks_of(head_width, head_size)):
        keys, queries = keys_ref[:, columns], queries_ref[:, columns]
        grads = grad_heads_ref[:, columns]
        probs = key_probs(keys, queries, window, head, mask_ref)
        weighted = probs * times_transposed(values_ref[:, columns], grads)
        grad_scores = weighted - probs * column_sum(weighted)
        probs_ref[...] = probs.astype(BF16)
        scores_ref[...] = grad_scores.astype(BF16)
        window_sum_ref[...] = jnp.zeros_like(window_sum_ref)
        for block in range(blocks):
            start = LANES * (blocks - 1 - block)
            window_sum_ref[:, start : start + length] += grad_scores[
                LANES * block : LANES * (block + 1)
            ]
        start = head * head_size
        for kind, value in enumerate(
            (
                contract_rows(scores_ref[...], keys) * scaling,
                matmul(scores_ref[...], queries),
                matmul(probs_ref[...], grads),
            )
        ):
            grad_projected_ref[
                :, kind * head_width + start : kind * head_width + start + head_size
            ] = value.astype(BF16)
        diagonal = window_sum_ref[...]
        half = LANES // 2
        while half >= 1:
            diagonal = pltpu.roll(diagonal[:half], half, 1) + diagonal[half:]
            half //= 2
        grad_offsets_ref[head : head + 1, :] = diagonal
    grad_offsets_ref.flush()
    for rows in blocks_of(length, 2 * LANES):
        total = 0.0
        for kind, weight_ref in enumerate((query_weight_ref, key_weight_ref, value_weight_ref)):
            total += times_transposed(
                grad_projected_ref[rows, kind * head_width : (kind + 1) * head_width],
                weight_ref.ready()[...],
            )
        grad_normed_ref[rows, :] = total.astype(BF16)
    normed, heads = normed_ref.ready(), heads_ref.ready()
    grad_post, final = grad_post_ref.ready(), final_ref.ready()
    half = width // 2
    count = head_width // 2
    post_rows = LANES // 2
    post_ref[...] = contract_rows(wide(grad_post, flags_ref[0] * LANES, LANES), final[...])
    for first_ref, post_half_ref, first, second in (
        (sent_ref, post_sent_ref, flags_ref[2], flags_ref[3]),
        (kept_ref, post_kept_ref, 1 - flags_ref[2], 1 - flags_ref[3]),
    ):
        post_half_ref[...] = post_ref[
            pl.ds(pl.multiple_of(second * post_rows, post_rows), post_rows), :
        ].astype(BF16)
        post_half_ref.flush()
        grad_project = contract_rows(
            wide(normed, first * half, half), grad_projected_ref[...]
        ).astype(BF16)
        first_ref[:half, :] = grad_project[:, : 2 * head_width]
        first_ref[half : half + count, :head_width] = grad_project[:count, 2 * head_width :]
        first_ref[half : half + count, head_width:] = grad_project[count:, 2 * head_width :]
        grad_out = contract_rows(heads[...], wide(grad_low_ref, first * half, half))
        first_ref[half + count :, :half] = grad_out[:count].astype(BF16)
        first_ref[half + count :, half:] = grad_out[count:].astype(BF16)
        first_ref.flush()


def input_kernel(
    flags_ref,
    own_ref,
    other_ref,
    embedded_ref,
    grad_mixed_ref,
    vectors_ref,
    speech_weight_ref,
    inputs_ref,
    post_sent_ref,
    post_kept_ref,
    loss_sums_ref,
    back_sums_ref,
    grad_offsets_ref,
    bucket_ref,
    sent_ref,
    kept_ref,
    feature_back_ref,
    terms_ref,
    grad_embedded_ref,
    hot_ref,
):
    length, width = own_ref.shape
    embedded, grad_mixed = embedded_ref.ready(), grad_mixed_ref.ready()
    vectors, speech_weight = vectors_ref.ready(), speech_weight_ref.ready()
    feat_width = speech_weight.shape[0]
    core_width = feat_width // 2
    speech = flags_ref[1].astype(F32)
    core = flags_ref[0]
    gain_sum, shift_sum, bias_sum = 0.0, 0.0, 0.0
    core_weight = speech_weight[pl.ds(pl.multiple_of(core * core_width, core_width), core_width), :]
    for rows in blocks_of(length, 2 * LANES):
        grad_normed = own_ref[rows, :].astype(F32) + other_ref[rows, :].astype(F32)
        normal, inverse = normalize(embedded[rows, :].astype(F32))
        gain_sum += column_sum(grad_normed * normal)
        shift_sum += column_sum(grad_normed)
        grad_embedded = (
            grad_mixed[rows, :]
            + norm_back(grad_normed, normal, inverse, vector(vectors, FIRST_GAIN, width))
        ).astype(BF16)
        grad_embedded_ref[rows, :] = grad_embedded
        bias_sum += column_sum(grad_embedded.astype(F32))
        feature_back_ref[rows, :] = times_transposed(grad_embedded, core_weight).astype(BF16)
    inputs = inputs_ref.ready()
    hot_ref[...] = contract_rows(inputs[:, feat_width:], grad_embedded_ref[...])
    post_rows = LANES // 2
    feat_rows = core_width // 2
    hot_rows = LANES // 4
    small_rows = 2 * SMALL_ROWS
    for which_ref, post_ref, half, base in (
        (sent_ref, post_sent_ref, flags_ref[3], small_rows),
        (kept_ref, post_kept_ref, 1 - flags_ref[3], 0),
    ):
        which_ref[base : base + post_rows, :] = post_ref[...]
        start = base + post_rows
        which_ref[start : start + feat_rows, :] = contract_rows(
            wide(inputs, core * core_width + half * feat_rows, feat_rows), grad_embedded_ref[...]
        ).astype(BF16)
        start += feat_rows
        which_ref[start : start + hot_rows, :] = hot_ref[
            pl.ds(pl.multiple_of(core * 2 * hot_rows + half * hot_rows, hot_rows), hot_rows), :
        ].astype(BF16)
        which_ref[start + hot_rows :, :] = jnp.zeros((hot_rows, width), BF16)
    loss_sums, back_sums = loss_sums_ref.ready(), back_sums_ref.ready()
    bias_rows = loss_sums.shape[1] // width
    rows = [loss_sums[0:1, :width], loss_sums[1:2, :width], back_sums[0:1, :], back_sums[1:2, :]]
    rows += [gain_sum, shift_sum, bias_sum * speech]
    rows += [loss_sums[2:3, part * width : (part + 1) * width] for part in range(bias_rows)]
    terms_ref[...] = jnp.zeros_like(terms_ref)
    for place, row in enumerate(rows):
        terms_ref[place : place + 1, :] = row
    start = len(rows)
    heads, offset_count = grad_offsets_ref.shape
    places = lax.broadcasted_iota(jnp.int32, (width // 2, offset_count), 0)
    hot = jnp.where(places == bucket_ref[...], 1.0, 0.0).astype(BF16)
    terms_ref[start : start + heads, : width // 2] = times_hot(
        grad_offsets_ref[...], hot, ((1,), (1,))
    )
    terms = terms_ref[...]
    high = terms.astype(BF16)
    rest = (terms - high.astype(F32)).astype(BF16)
    terms_ref[...] = high.astype(F32) + rest.astype(F32)
    sent_ref[:SMALL_ROWS, :] = high
    sent_ref[SMALL_ROWS:small_rows, :] = rest


def rows_at(ref, start, count):
    return ref[pl.ds(pl.multiple_of(start, 16), count), :]


def add_low(left_side, right_side):
    return (left_side.astype(F32) + right_side.astype(F32)).astype(BF16)


def add_small(terms_ref, came_ref):
    return terms_ref[...] + (
        came_ref[:SMALL_ROWS, :].astype(F32)
        + came_ref[SMALL_ROWS : 2 * SMALL_ROWS, :].astype(F32)
    )


def send_small(small, sent_ref, terms_ref):
    high = small.astype(BF16)
    rest = (small - high.astype(F32)).astype(BF16)
    sent_ref[:SMALL_ROWS, :] = high
    sent_ref[SMALL_ROWS : 2 * SMALL_ROWS, :] = rest
    terms_ref[...] = high.astype(F32) + rest.astype(F32)


def add_kernel(with_small, mine_ref, kept_ref, came_ref, *refs):
    half = kept_ref.shape[0] // 2
    base = 0
    if with_small:
        base = 2 * SMALL_ROWS
        terms_ref, sent_ref, next_ref, new_terms_ref = refs
        send_small(add_small(terms_ref, came_ref), sent_ref, new_terms_ref)
    else:
        sent_ref, next_ref = refs
    mine = mine_ref[0]
    start = (1 - mine) * half
    sent_ref[base:, :] = add_low(
        rows_at(kept_ref, start, half), rows_at(came_ref, base + start, half)
    )
    start = mine * half
    next_ref[...] = add_low(
        rows_at(kept_ref, start, half), rows_at(came_ref, base + start, half)
    )


def join_kernel(with_small, mine_ref, kept_ref, came_ref, kept_two_ref, came_two_ref, *refs):
    start = base = 0
    if with_small:
        start = base = 2 * SMALL_ROWS
        terms_ref, sent_ref, next_ref, next_two_ref, new_terms_ref = refs
        send_small(add_small(terms_ref, came_two_ref), sent_ref, new_terms_ref)
    else:
        sent_ref, next_ref, next_two_ref = refs
    for kept, came, extra, out_ref in (
        (kept_ref, came_ref, 0, next_ref),
        (kept_two_ref, came_two_ref, base, next_two_ref),
    ):
        half = out_ref.shape[0]
        place = (1 - mine_ref[0]) * half
        sent_ref[start : start + half, :] = add_low(
            rows_at(kept, place, half), rows_at(came, extra + place, half)
        )
        start += half
        place = mine_ref[0] * half
        out_ref[...] = add_low(rows_at(kept, place, half), rows_at(came, extra + place, half))


def finish_kernel(with_small, kept_ref, kept_two_ref, came_ref, *refs):
    start = 0
    if with_small:
        start = 2 * SMALL_ROWS
        terms_ref, total_ref, small_ref = refs
        small_ref[...] = add_small(terms_ref, came_ref)
    else:
        (total_ref,) = refs
    out = 0
    for kept in (kept_ref, kept_two_ref):
        count = kept.shape[0]
        total_ref[out : out + count, :] = add_low(kept[...], came_ref[start : start + count, :])
        start += count
        out += count


def whole_join_kernel(with_small, kept_ref, came_ref, kept_two_ref, came_two_ref, *refs):
    start = base = 0
    if with_small:
        start = base = 2 * SMALL_ROWS
        terms_ref, joint_ref, new_terms_ref = refs
        send_small(add_small(terms_ref, came_two_ref), joint_ref, new_terms_ref)
    else:
        (joint_ref,) = refs
    count = kept_ref.shape[0]
    joint_ref[start : start + count, :] = add_low(kept_ref[...], came_ref[...])
    joint_ref[start + count :, :] = add_low(kept_two_ref[...], came_two_ref[base:, :])


def whole_finish_kernel(with_small, joint_ref, came_ref, *refs):
    start = 0
    if with_small:
        start = 2 * SMALL_ROWS
        terms_ref, *outs, small_ref = refs
        small_ref[...] = add_small(terms_ref, came_ref)
    else:
        outs = refs
    for out_ref in outs:
        rows = slice(start, start + out_ref.shape[0])
        out_ref[...] = add_low(joint_ref[rows, :], came_ref[rows, :])
        start += out_ref.shape[0]


def place_kernel(mine_ref, own_ref, came_ref, out_ref):
    half = own_ref.shape[0]
    out_ref[pl.ds(pl.multiple_of(mine_ref[0] * half, 16), half), :] = own_ref[...]
    out_ref[pl.ds(pl.multiple_of((1 - mine_ref[0]) * half, 16), half), :] = came_ref[...]


def part_kernel(mine_ref, own_ref, came_ref, first_ref, second_ref):
    start = 0
    for out_ref in (first_ref, second_ref):
        half = out_ref.shape[0] // 2
        for ref, place in ((own_ref, mine_ref[0]), (came_ref, 1 - mine_ref[0])):
            out_ref[pl.ds(pl.multiple_of(place * half, 16), half), :] = ref[
                start : start + half, :
            ]
        start += half


def early_place_kernel(
    flags_ref, first_ref, first_came_ref, second_ref, second_came_ref, down_ref, up_ref
):
    width = down_ref.shape[1]
    units = down_ref.shape[0] // 2
    cut = width // 2
    for first, second, first_half, second_half in (
        (first_ref, second_ref, flags_ref[0], flags_ref[1]),
        (first_came_ref, second_came_ref, 1 - flags_ref[0], 1 - flags_ref[1]),
    ):
        down_ref[pl.ds(pl.multiple_of(first_half * units, units), units), :] = first[
            :units, :
        ].astype(F32)
        columns = pl.ds(pl.multiple_of(first_half * units, LANES), units)
        up_ref[:cut, columns] = first[units:, :].astype(F32)
        columns = pl.ds(pl.multiple_of(second_half * units, LANES), units)
        up_ref[cut:, columns] = second[...].astype(F32)


def late_place_kernel(
    half_ref, part_ref, query_ref, key_ref, value_ref, out_ref, *buffers_and_semaphore
):
    *buffers, semaphore = buffers_and_semaphore
    query_buffer, key_buffer, value_buffer, out_buffer = buffers
    width = part_ref.shape[1]
    head_width = query_ref.shape[1]
    half = width // 2
    count = head_width // 2
    place = pl.ds(pl.multiple_of(half_ref[0] * half, LANES), half)
    copies = [
        pltpu.make_async_copy(buffer, target, semaphore.at[number])
        for number, (buffer, target) in enumerate(
            (
                (query_buffer, query_ref.at[place, :]),
                (key_buffer, key_ref.at[place, :]),
                (value_buffer, value_ref.at[place, :]),
                (out_buffer, out_ref.at[:, place]),
            )
        )
    ]
    query_buffer[...] = part_ref[:half, :head_width].astype(F32)
    copies[0].start()
    key_buffer[...] = part_ref[:half, head_width:].astype(F32)
    copies[1].start()
    for part in range(2):
        columns = slice(part * head_width, (part + 1) * head_width)
        value_buffer[part * count : (part + 1) * count, :] = part_ref[
            half : half + count, columns
        ].astype(F32)
    copies[2].start()
    for part in range(2):
        columns = slice(part * half, (part + 1) * half)
        out_buffer[part * count : (part + 1) * count, :] = part_ref[
            half + count :, columns
        ].astype(F32)
    copies[3].start()
    for copy in copies:
        copy.wait()


def place_late(links, half, part, outputs, head_width, after=()):
    width = part.shape[1]
    shapes = [(width, head_width)] * 3 + [(head_width, width)]
    buffers = [(width // 2, head_width)] * 3 + [(head_width, width // 2)]
    distant = pl.BlockSpec(memory_space=pltpu.HBM)
    near = pl.BlockSpec(memory_space=pltpu.VMEM)
    outputs = [] if outputs is None else list(outputs)

    def kernel(half_ref, part_ref, *refs):
        late_place_kernel(half_ref, part_ref, *refs[len(outputs) + len(after) :])

    return pl.pallas_call(
        kernel,
        in_specs=[pl.BlockSpec(memory_space=pltpu.SMEM), near]
        + [distant] * len(outputs)
        + [pl.BlockSpec(memory_space=pl.ANY)] * len(after),
        out_specs=[distant] * 4,
        out_shape=[jax.ShapeDtypeStruct(shape, F32) for shape in shapes],
        input_output_aliases={2 + number: number for number in range(len(outputs))},
        scratch_shapes=[pltpu.VMEM(shape, F32) for shape in buffers]
        + [pltpu.SemaphoreType.DMA((4,))],
        compiler_params=pltpu.CompilerParams(vmem_limit_bytes=16 * 1024 * 1024),
        name="late_place",
    )(half, part, *outputs, *after)


def small_kernel(
    rows,
    terms_ref,
    loss_ref,
    mel_ref,
    vocab_ref,
    down_ref,
    gain_two_ref,
    shift_two_ref,
    gain_one_ref,
    shift_one_ref,
    speech_ref,
    up_ref,
    table_ref,
):
    width = down_ref.shape[0]
    loss_ref[...] = terms_ref[0:1, 0:1] * (1.0 / rows)
    mel_ref[...] = terms_ref[0, LANES : LANES + mel_ref.shape[0]]
    vocab_ref[...] = terms_ref[0, 2 * LANES : 2 * LANES + vocab_ref.shape[0]]
    row = 1
    for ref in (down_ref, gain_two_ref, shift_two_ref, gain_one_ref, shift_one_ref, speech_ref):
        ref[...] = terms_ref[row, :]
        row += 1
    for columns in blocks_of(up_ref.shape[0], width):
        up_ref[columns] = terms_ref[row, :]
        row += 1
    table_ref[...] = terms_ref[row : row + table_ref.shape[0], : table_ref.shape[1]]


def shared_place_kernel(
    flags_ref,
    own_ref,
    own_other_ref,
    came_ref,
    came_other_ref,
    speech_ref,
    table_ref,
    mel_ref,
    vocab_ref,
    post_ref,
    hot_ref,
):
    core = flags_ref[2]
    post_rows = LANES // 2
    feat_rows = speech_ref.shape[0] // 4
    hot_rows = LANES // 4
    for ref, place, half in (
        (own_ref, core, flags_ref[1]),
        (came_ref, core, 1 - flags_ref[1]),
        (own_other_ref, 1 - core, flags_ref[1]),
        (came_other_ref, 1 - core, 1 - flags_ref[1]),
    ):
        spot = pl.multiple_of(place * LANES + half * post_rows, 16)
        post_ref[pl.ds(spot, post_rows), :] = ref[:post_rows, :].astype(F32)
        start = post_rows
        spot = pl.multiple_of((place * 2 + half) * feat_rows, 16)
        speech_ref[pl.ds(spot, feat_rows), :] = ref[start : start + feat_rows, :].astype(F32)
        start += feat_rows
        spot = pl.multiple_of((place * 2 + half) * hot_rows, 16)
        hot_ref[pl.ds(spot, hot_rows), :] = ref[start : start + hot_rows, :].astype(F32)
    table_ref[...] = hot_ref[: table_ref.shape[0], :]
    mel_ref[...] = post_ref[: mel_ref.shape[0], :]
    vocab_ref[...] = post_ref[LANES : LANES + vocab_ref.shape[0], :]


def swap_cores(array):
    return lax.ppermute(array, "mp", [(0, 1), (1, 0)])


ORDERS = (((0, 1, 2, 3), (1, 2, 0, 3)), ((2, 0, 1, 3), (2, 0, 1, 3)))
STEPS = 4


class Links:
    def __init__(self, devices, cores, index, core):
        self.devices, self.cores, self.index, self.core = devices, cores, index, core
        self.bits = devices.bit_length() - 1
        self.token = None
        self.pending = []

    def exchange(self, array, directions):
        pairs = [
            (
                place * self.cores + core,
                (place ^ (1 << directions[core])) * self.cores + core,
            )
            for place in range(self.devices)
            for core in range(self.cores)
        ]
        return lax.ppermute(array, ("dp", "mp"), pairs)

    def mine(self, directions):
        direction = jnp.where(self.core == 0, directions[0], directions[1])
        return ((self.index >> direction) & 1).astype(jnp.int32)

    def run(self, kernel, name, flags, operands, outputs, scratch=(), mebibytes=16, after=()):
        results, self.token = run_kernel(
            kernel,
            name,
            0.05,
            flags,
            operands,
            outputs,
            scratch,
            mebibytes,
            after if self.token is None else (self.token, *after),
        )
        return results

    def later(self, kernel, flags, operands, outputs, take):
        self.pending.append((kernel, flags, operands, outputs, take))

    def flush(self, name, after=()):
        pieces, self.pending = self.pending, []
        flags = [flag for piece in pieces for flag in piece[1]] or [jnp.int32(0)]
        operands = [each for piece in pieces for each in piece[2]]
        outputs = [each for piece in pieces for each in piece[3]]

        def kernel(flags_ref, *refs):
            ins, outs = list(refs[: len(operands)]), list(refs[len(operands) :])
            count = 0
            for body, piece_flags, piece_ins, piece_outs, _ in pieces:
                body(
                    *([[flags_ref[count + place] for place in range(len(piece_flags))]] if piece_flags else []),
                    *[ins.pop(0) for _ in piece_ins],
                    *[outs.pop(0) for _ in piece_outs],
                )
                count += len(piece_flags)

        results = self.run(kernel, name, jnp.stack(flags), operands, outputs, after=after)
        for piece in pieces:
            count = len(piece[3])
            piece[4](results[:count])
            results = results[count:]


def step_directions(slot, step):
    return tuple(order[step] for order in ORDERS[slot])


def shape_of(operand):
    return (operand[1] if isinstance(operand, tuple) else operand).shape


class Wave:
    def __init__(self, links, name, sent, kept, terms=None):
        self.links = links
        self.name = name
        self.terms = terms
        self.sent = list(sent)
        self.kept = list(kept)
        self.came = [None, None]

    def scatter(self, step):
        for slot in range(2):
            self.came[slot] = self.links.exchange(self.sent[slot], step_directions(slot, step))

    def piece(self, kernel, directions, operands, outputs, small, take):
        if small:
            operands = operands + [self.terms]
            outputs = outputs + [((SMALL_ROWS, outputs[0][0][1]), F32)]

        def take_all(results):
            if small:
                *results, self.terms = results
            take(results)

        self.links.later(
            functools.partial(kernel, small),
            [] if directions is None else [self.links.mine(directions)],
            operands,
            outputs,
            take_all,
        )

    def add(self, step, distant=False):
        for slot in range(2):
            small = slot == 1 and self.terms is not None
            rows, width = shape_of(self.kept[slot])
            half, extra = rows // 2, 2 * SMALL_ROWS if small else 0

            def take(results, slot=slot):
                self.sent[slot], self.kept[slot] = results

            self.piece(
                add_kernel,
                step_directions(slot, step + 1),
                [self.kept[slot], far(self.came[slot]) if distant else self.came[slot]],
                [
                    ((half + extra, width), BF16),
                    ((half, width), BF16, "far") if step == 0 and distant else ((half, width), BF16),
                ],
                small,
                take,
            )

    def join(self):
        halves = [shape_of(kept)[0] // 2 for kept in self.kept]
        width = shape_of(self.kept[0])[1]
        small = self.terms is not None

        def take(results):
            self.sent_joint, *self.kept = results

        self.piece(
            join_kernel,
            step_directions(0, STEPS - 1),
            [self.kept[0], self.came[0], self.kept[1], self.came[1]],
            [((sum(halves) + (2 * SMALL_ROWS if small else 0), width), BF16)]
            + [((half, width), BF16) for half in halves],
            small,
            take,
        )

    def scatter_joint(self):
        self.came_joint = self.links.exchange(self.sent_joint, step_directions(0, STEPS - 1))

    def finish(self):
        self.counts = [shape_of(kept)[0] for kept in self.kept]
        width = shape_of(self.kept[0])[1]

        def take(results):
            (self.joint,) = results

        self.piece(
            finish_kernel,
            None,
            [*self.kept, self.came_joint],
            [((sum(self.counts), width), BF16)],
            self.terms is not None,
            take,
        )

    def sum_others(self):
        for direction in range(STEPS, self.links.bits):
            both = (direction, direction)
            came = self.links.exchange(self.joint, both)
            self.joint = (self.joint.astype(F32) + came.astype(F32)).astype(BF16)
            if self.terms is not None:
                self.terms = self.terms + self.links.exchange(self.terms, both)

    def gather_joint(self):
        self.came_joint = self.links.exchange(self.joint, step_directions(0, STEPS - 1))

    def part(self):
        width = self.joint.shape[1]

        def take(results):
            self.shares = list(results)

        self.links.later(
            part_kernel,
            [self.links.mine(step_directions(0, STEPS - 1))],
            [self.joint, self.came_joint],
            [((2 * count, width), BF16) for count in self.counts],
            take,
        )

    def join_whole(self):
        self.counts = [shape_of(kept)[0] for kept in self.kept]
        width = shape_of(self.kept[0])[1]
        small = self.terms is not None

        def take(results):
            (self.joint,) = results

        self.piece(
            whole_join_kernel,
            None,
            [self.kept[0], self.came[0], self.kept[1], self.came[1]],
            [((sum(self.counts) + (2 * SMALL_ROWS if small else 0), width), BF16)],
            small,
            take,
        )

    def exchange_whole(self):
        self.came_joint = self.links.exchange(self.joint, step_directions(0, STEPS - 1))

    def finish_whole(self):
        width = self.joint.shape[1]

        def take(results):
            self.shares = list(results)

        self.piece(
            whole_finish_kernel,
            None,
            [self.joint, self.came_joint],
            [((count, width), BF16) for count in self.counts],
            self.terms is not None,
            take,
        )

    def sum_others_whole(self):
        for direction in range(STEPS, self.links.bits):
            both = (direction, direction)
            self.shares = [
                (share.astype(F32) + self.links.exchange(share, both).astype(F32)).astype(BF16)
                for share in self.shares
            ]

    def gather(self, step):
        self.came = [
            self.links.exchange(rows, step_directions(slot, step))
            for slot, rows in enumerate(self.shares)
        ]

    def place(self, step):
        for slot in range(2):

            def take(results, slot=slot):
                (self.shares[slot],) = results

            rows, width = shape_of(self.shares[slot])
            self.links.later(
                place_kernel,
                [self.links.mine(step_directions(slot, step))],
                [self.shares[slot], self.came[slot]],
                [((2 * rows, width), BF16)],
                take,
            )


def per_device(
    features,
    token_ids,
    mel_target,
    token_target,
    segments,
    row_device,
    offset_bucket,
    speech_weight,
    speech_bias,
    token_table,
    first_gain,
    first_shift,
    query_weight,
    key_weight,
    value_weight,
    bias_table,
    out_weight,
    second_gain,
    second_shift,
    up_weight,
    up_bias,
    down_weight,
    down_bias,
    mel_weight,
    mel_bias,
    vocab_weight,
    vocab_bias,
):
    devices = lax.axis_size("dp")
    device_index = lax.axis_index("dp")
    core = lax.axis_index("mp")
    cores = lax.axis_size("mp")
    rows_speech, part_len, feat_width = features.shape
    rows_total, length = segments.shape
    model_width = speech_weight.shape[1]
    vocab_size = token_table.shape[0]
    mel_width = mel_weight.shape[1]
    local_heads = bias_table.shape[1]
    buckets = bias_table.shape[0]
    head_width = query_weight.shape[1]
    head_size = head_width // local_heads
    units = up_weight.shape[1]
    is_speech = device_index % 2 == 0
    my_row = device_index // 2 + jnp.where(is_speech, 0, rows_speech)
    links = Links(devices, cores, device_index, core)
    flags = jnp.stack(
        [
            core,
            is_speech.astype(jnp.int32),
            1 - links.mine(step_directions(0, 0)),
            1 - links.mine(step_directions(1, 0)),
        ]
    ).astype(jnp.int32)

    plain_width = feat_width + mel_width
    core_width = -(-(plain_width + 2) // (LANES * cores)) * LANES
    ids = jnp.stack([token_ids, token_target], axis=2).astype(BF16)
    (packed,), _ = run_kernel(
        pack_kernel,
        "pack_rows",
        1,
        flags,
        [far(features), far(mel_target), ids],
        [((rows_total, part_len, core_width), BF16)],
    )
    arrived = lax.all_to_all(packed, "dp", split_axis=0, concat_axis=0, tiled=True)
    arrived = arrived.reshape(length, core_width)

    my_segments = lax.dynamic_slice_in_dim(segments, my_row, 1)
    segment_column = my_segments.reshape(length, 1)
    bucket_line = jnp.pad(offset_bucket, (0, 1), constant_values=-1).reshape(1, 2 * length)
    full_rows = lambda array: jnp.pad(array, ((0, LANES - array.shape[0]), (0, 0)))
    post_bias = jnp.concatenate(
        [jnp.pad(mel_bias, (0, LANES - mel_width)), jnp.pad(vocab_bias, (0, LANES - vocab_size))]
    )
    vectors = jnp.stack(
        [
            jnp.pad(each, (0, units - each.size))
            for each in (
                speech_bias,
                first_gain,
                first_shift,
                second_gain,
                second_shift,
                up_bias,
                down_bias,
                post_bias,
            )
        ]
    )
    token_rows, mel_rows, vocab_rows = (
        full_rows(array) for array in (token_table, mel_weight.T, vocab_weight.T)
    )
    (window,), window_token = run_kernel(
        window_kernel,
        "bias_window",
        3,
        flags,
        [bucket_line, bias_table.T],
        [((local_heads, LANES, 2 * length), F32, "far")],
        after=(far(vectors), far(token_rows)),
    )
    arrived, window_token = lax.optimization_barrier((arrived, window_token))

    model_low = ((length, model_width), BF16)
    head_low = ((length, head_width), BF16)
    (
        embedded,
        attended,
        embedded_far,
        normed_one,
        queries,
        key_rows,
        value_rows,
        heads_flat,
        inputs,
        extra,
    ), _ = run_kernel(
        functools.partial(attend_kernel, head_size, plain_width),
        "embed_and_attend",
        8,
        flags,
        [
            arrived,
            swap_cores(arrived),
            far(speech_weight),
            far(token_rows),
            far(vectors),
            far(query_weight),
            far(key_weight),
            far(value_weight),
            far(out_weight),
            far(window),
            segment_column,
            my_segments,
        ],
        [
            model_low,
            model_low,
            (*model_low, "far"),
            (*model_low, "far"),
            (*head_low, "far"),
            (*head_low, "far"),
            (*head_low, "far"),
            (*head_low, "far"),
            ((length, feat_width + LANES), BF16, "far"),
            ((length, LANES), BF16),
        ],
        [pltpu.VMEM((length, length), F32)],
        mebibytes=26,
        after=(window_token,),
    )
    (mixed, slope, branch, mixed_far, normed_two, active), _ = run_kernel(
        forward_kernel,
        "feed_forward",
        5,
        flags,
        [
            embedded,
            attended,
            swap_cores(attended),
            far(vectors),
            up_weight,
            down_weight,
        ],
        [
            ((length, model_width), F32),
            ((length, units), F32),
            model_low,
            ((length, model_width), F32, "far"),
            model_low,
            ((length, units), BF16),
        ],
        mebibytes=28,
    )
    early_shapes = [
        ((units // 2 + model_width // 2, model_width), BF16, "far"),
        ((model_width // 2, model_width), BF16, "far"),
    ]
    (
        *early_parts,
        grad_normed_two,
        grad_final_far,
        final_low,
        grad_post,
        loss_sums,
    ), links.token = run_kernel(
        functools.partial(loss_kernel, mel_width, vocab_size),
        "loss_and_feed_back",
        0.05,
        flags,
        [
            mixed,
            branch,
            swap_cores(branch),
            far(vectors),
            mel_rows,
            vocab_rows,
            extra,
            slope,
            up_weight,
            down_weight,
            active,
            normed_two,
        ],
        early_shapes * 2
        + [
            model_low,
            (*model_low, "far"),
            (*model_low, "far"),
            ((length, 2 * LANES), BF16, "far"),
            ((8, units), F32, "far"),
        ],
        [
            pltpu.VMEM((2 * LANES, model_width), BF16),
            pltpu.VMEM((length, model_width), BF16),
            pltpu.VMEM((length, units), BF16),
        ],
        mebibytes=34,
    )

    early = Wave(links, "early", early_parts[:2], [far(kept) for kept in early_parts[2:]])
    early.scatter(0)
    other_normed_two = swap_cores(grad_normed_two)
    part = ((model_width // 2 + head_width, model_width), BF16)
    post_part = ((LANES // 2, model_width), BF16)
    (
        grad_normed_one,
        late_sent,
        late_kept,
        grad_mixed,
        post_sent,
        post_kept,
        grad_offsets,
        back_sums,
    ) = links.run(
        functools.partial(back_kernel, head_size),
        "attend_back",
        flags,
        [
            grad_normed_two,
            other_normed_two,
            far(mixed_far),
            far(grad_final_far),
            far(vectors),
            far(out_weight),
            far(queries),
            far(key_rows),
            far(value_rows),
            far(window),
            segment_column,
            my_segments,
            far(query_weight),
            far(key_weight),
            far(value_weight),
            far(normed_one),
            far(heads_flat),
            far(grad_post),
            far(final_low),
        ],
        [
            model_low,
            (*part, "far"),
            (*part, "far"),
            ((length, model_width), F32, "far"),
            (*post_part, "far"),
            (*post_part, "far"),
            ((local_heads, 2 * length), F32, "far"),
            ((8, model_width), F32, "far"),
        ],
        [
            pltpu.VMEM((length, model_width), BF16),
            pltpu.VMEM((length, head_width), BF16),
            pltpu.VMEM((length, 3 * head_width), BF16),
            pltpu.VMEM((length, length), F32),
            pltpu.VMEM((length, length), BF16),
            pltpu.VMEM((length, length), BF16),
            pltpu.VMEM((LANES, 2 * length), F32),
            pltpu.VMEM((LANES, model_width), F32),
        ],
        mebibytes=32,
    )
    other_normed_one = swap_cores(grad_normed_one)
    early.add(0, True)
    links.flush("phase_a")
    early.kept = [far(kept) for kept in early.kept]
    early.scatter(1)
    late_rows = LANES + feat_width // 4
    late_second_sent, late_second_kept, feature_back, terms = links.run(
        input_kernel,
        "input_back",
        flags,
        [
            grad_normed_one,
            other_normed_one,
            far(embedded_far),
            far(grad_mixed),
            far(vectors),
            far(speech_weight),
            far(inputs),
            far(post_sent),
            far(post_kept),
            far(loss_sums),
            far(back_sums),
            far(grad_offsets),
            far(bucket_line),
        ],
        [
            ((late_rows + 2 * SMALL_ROWS, model_width), BF16, "far"),
            ((late_rows, model_width), BF16),
            ((length, feat_width // cores), BF16, "far"),
            ((SMALL_ROWS, model_width), F32),
        ],
        [
            pltpu.VMEM((length, model_width), BF16),
            pltpu.VMEM((LANES, model_width), F32),
        ],
        mebibytes=18,
    )
    late = Wave(
        links, "late", [late_sent, late_second_sent], [far(late_kept), late_second_kept], terms
    )
    feature_half = lax.all_to_all(
        feature_back.reshape(devices, part_len, feat_width // cores),
        "dp",
        split_axis=0,
        concat_axis=0,
        tiled=True,
    )
    early.add(1, True)
    links.flush("phase_b")
    early.scatter(2)
    early.join_whole()
    links.flush("phase_c", (feature_half,))
    early.exchange_whole()
    *late.sent, early.joint = lax.optimization_barrier((*late.sent, early.joint))
    late.scatter(0)
    late.add(0)
    links.flush("phase_d")
    late.scatter(1)
    feature_half = feature_half.reshape(rows_speech, 2, part_len, feat_width // cores)[:, 0]
    other_feature = swap_cores(feature_half)
    feature_grad = jnp.concatenate(
        [
            jnp.where(core == 0, feature_half, other_feature),
            jnp.where(core == 0, other_feature, feature_half),
        ],
        axis=2,
    )
    early.finish_whole()
    late.add(1)
    links.flush("phase_e", (feature_grad,))
    early.sum_others_whole()
    early.gather(2)
    late.scatter(2)
    early.place(2)
    late.join()
    links.flush("phase_f")
    early.gather(1)
    late.scatter_joint()
    early.place(1)
    late.finish()
    links.flush("phase_g")
    late.sum_others()
    early.gather(0)
    late.gather_joint()
    late.part()
    line_out = ((model_width,), F32)
    small = []
    links.later(
        functools.partial(small_kernel, rows_total),
        [],
        [late.terms],
        [((1, 1), F32), ((mel_width,), F32), ((vocab_size,), F32)]
        + [line_out] * 6
        + [((units,), F32), ((local_heads, buckets), F32)],
        small.extend,
    )
    links.flush("phase_h")
    late.gather(2)
    late.place(2)
    links.flush("phase_h2", [early.came[1]])
    late.gather(1)
    late.place(1)
    links.flush("phase_i", early.came)
    late.gather(0)

    place_flags = jnp.stack(
        [links.mine(step_directions(0, 0)), links.mine(step_directions(1, 0)), core]
    ).astype(jnp.int32)
    grad_down, grad_up = links.run(
        early_place_kernel,
        "early_place",
        place_flags,
        [early.shares[0], far(early.came[0]), early.shares[1], far(early.came[1])],
        [((units, model_width), F32), ((model_width, units), F32)],
        mebibytes=20,
    )
    early_end = links.token
    grad_query, grad_key, grad_value, grad_out = place_late(
        links, place_flags[:1], late.shares[0], None, head_width, after=(early_end,)
    )
    shared_own, shared_came, _ = lax.optimization_barrier(
        (late.shares[1], late.came[1], early_end)
    )
    shared_own_other, shared_came_other = swap_cores(shared_own), swap_cores(shared_came)
    grad_speech_weight, grad_token_table, grad_mel_weight, grad_vocab_weight = links.run(
        shared_place_kernel,
        "shared_place",
        place_flags,
        [shared_own, shared_own_other, shared_came, shared_came_other],
        [
            ((feat_width, model_width), F32),
            ((vocab_size, model_width), F32),
            ((mel_width, model_width), F32),
            ((vocab_size, model_width), F32),
        ],
        [pltpu.VMEM((2 * LANES, model_width), F32), pltpu.VMEM((LANES, model_width), F32)],
        after=(far(grad_query),),
    )
    grad_query, grad_key, grad_value, grad_out = place_late(
        links,
        1 - place_flags[:1],
        late.came[0],
        (grad_query, grad_key, grad_value, grad_out),
        head_width,
    )
    grad_mel_weight, grad_vocab_weight = grad_mel_weight.T, grad_vocab_weight.T
    (
        loss_total,
        grad_mel_bias,
        grad_vocab_bias,
        grad_down_bias,
        grad_second_gain,
        grad_second_shift,
        grad_first_gain,
        grad_first_shift,
        grad_speech_bias,
        grad_up_bias,
        grad_table,
    ) = small
    return (
        loss_total.reshape(()),
        feature_grad,
        grad_speech_weight,
        grad_speech_bias,
        grad_token_table,
        grad_first_gain,
        grad_first_shift,
        grad_query,
        grad_key,
        grad_value,
        grad_table.T,
        grad_out,
        grad_second_gain,
        grad_second_shift,
        grad_up,
        grad_up_bias,
        grad_down,
        grad_down_bias,
        grad_mel_weight,
        grad_mel_bias,
        grad_vocab_weight,
        grad_vocab_bias,
    )


def solution(mesh):
    placed = (
        P(None, "dp", None),
        P(None, "dp"),
        P(None, "dp", None),
        P(None, "dp"),
        P(),
        P(),
        P(),
        P(),
        P(),
        P(),
        P(),
        P(),
        P(None, "mp"),
        P(None, "mp"),
        P(None, "mp"),
        P(None, "mp"),
        P("mp", None),
        P(),
        P(),
        P(None, "mp"),
        P("mp"),
        P("mp", None),
        P(),
        P(),
        P(),
        P(),
        P(),
    )
    return jax.shard_map(
        per_device,
        mesh=mesh,
        in_specs=placed,
        out_specs=(
            P(),
            P(None, "dp", None),
            P(),
            P(),
            P(),
            P(),
            P(),
            P(None, "mp"),
            P(None, "mp"),
            P(None, "mp"),
            P(None, "mp"),
            P("mp", None),
            P(),
            P(),
            P(None, "mp"),
            P("mp"),
            P("mp", None),
            P(),
            P(),
            P(),
            P(),
            P(),
        ),
        check_vma=False,
    )
```

```python
import functools

import jax
import jax.numpy as jnp
from jax import lax
from jax.experimental import pallas as pl
from jax.experimental.pallas import tpu as pltpu
from jax.sharding import PartitionSpec as P

EPSILON = 1e-05
NEGATIVE = -1e30
HIGHEST = lax.Precision.HIGHEST
BF16 = jnp.bfloat16
F32 = jnp.float32
LANES = 128
SMALL_ROWS = 16


def contract_rows(left_side, right_side):
    return lax.dot_general(
        left_side, right_side, (((0,), (0,)), ((), ())), preferred_element_type=F32
    )


def times_transposed(left_side, right_side):
    return lax.dot_general(
        left_side, right_side, (((1,), (1,)), ((), ())), preferred_element_type=F32
    )


def matmul(left_side, right_side):
    return jnp.dot(left_side, right_side, preferred_element_type=F32)


def normalize(row_data):
    center = row_data - jnp.mean(row_data, axis=-1, keepdims=True)
    inverse = lax.rsqrt(jnp.mean(center * center, axis=-1, keepdims=True) + EPSILON)
    return center * inverse, inverse


def norm_back(grad_out, normal, inverse, norm_gain):
    scaled = grad_out * norm_gain
    return inverse * (
        scaled
        - jnp.mean(scaled, axis=-1, keepdims=True)
        - normal * jnp.mean(scaled * normal, axis=-1, keepdims=True)
    )


def column_sum(array):
    return jnp.sum(array, axis=0, keepdims=True)


def cost(microseconds):
    return pl.CostEstimate(
        flops=0, bytes_accessed=int(microseconds * 3.5e6), transcendentals=0
    )


class Fetched:
    def __init__(self, source, target, semaphore):
        self.copy = pltpu.make_async_copy(source, target, semaphore)
        self.target = target
        self.begun = False
        self.waited = False
        self.shape = target.shape

    def begin(self):
        if not self.begun:
            self.copy.start()
            self.begun = True

    def ready(self):
        self.begin()
        if not self.waited:
            self.copy.wait()
            self.waited = True
        return self.target

    def __getitem__(self, places):
        return self.ready()[places]


class Stored:
    def __init__(self, target, source, semaphore):
        self.copy = pltpu.make_async_copy(source, target, semaphore)
        self.source = source
        self.started = False
        self.shape = source.shape

    def __getitem__(self, places):
        return self.source[places]

    def __setitem__(self, places, value):
        self.source[places] = value

    def flush(self):
        if not self.started:
            self.copy.start()
            self.started = True


def run_kernel(
    kernel, name, microseconds, flags, operands, outputs, scratch=(), mebibytes=16, after=()
):
    in_place = pl.BlockSpec(memory_space=pltpu.VMEM)
    distant = pl.BlockSpec(memory_space=pltpu.HBM)
    after = [
        pltpu.with_memory_space_constraint(array[1], pltpu.HBM)
        if isinstance(array, tuple)
        else array
        for array in after
    ]
    far = [isinstance(operand, tuple) for operand in operands]
    arrays = [
        pltpu.with_memory_space_constraint(operand[1], pltpu.HBM) if is_far else operand
        for operand, is_far in zip(operands, far)
    ]
    out_far = [len(output) == 3 and output[2] == "far" for output in outputs]
    copied = {output[2]: place for place, output in enumerate(outputs) if len(output) == 3}
    fetched = [
        pltpu.VMEM(array.shape, array.dtype)
        for place, (array, is_far) in enumerate(zip(arrays, far))
        if is_far and place not in copied
    ]
    stored = [
        pltpu.VMEM(output[0], output[1]) for output, is_far in zip(outputs, out_far) if is_far
    ]
    moves = sum(far) + sum(out_far)
    semaphores = [pltpu.SemaphoreType.DMA((moves,))] if moves else []

    def with_moves(*refs):
        refs = list(refs)
        semaphore = refs.pop() if moves else None
        buffers = refs[len(refs) - len(fetched) - len(stored) :]
        refs = refs[: len(refs) - len(fetched) - len(stored)]
        first_out = 1 + len(arrays) + len(after)
        count = 0
        came = []
        for place, is_far in enumerate(far):
            if is_far:
                target = refs[first_out + copied[place]] if place in copied else buffers.pop(0)
                refs[place + 1] = Fetched(refs[place + 1], target, semaphore.at[count])
                if operands[place][0] == "far":
                    refs[place + 1].begin()
                came.append(refs[place + 1])
                count += 1
        kept = []
        for place, is_far in enumerate(out_far):
            if is_far:
                refs[first_out + place] = Stored(
                    refs[first_out + place], buffers.pop(0), semaphore.at[count]
                )
                kept.append(refs[first_out + place])
                count += 1
        token_ref = refs[first_out + len(outputs)]
        token_ref[...] = jnp.zeros_like(token_ref)
        kernel(
            *refs[: 1 + len(arrays)],
            *refs[first_out : first_out + len(outputs)],
            *refs[first_out + len(outputs) + 1 :],
        )
        for ref in kept:
            ref.flush()
        for ref in came:
            ref.ready()
        for ref in kept:
            ref.copy.wait()

    *results, token = pl.pallas_call(
        with_moves,
        in_specs=[pl.BlockSpec(memory_space=pltpu.SMEM)]
        + [distant if is_far else in_place for is_far in far]
        + [pl.BlockSpec(memory_space=pl.ANY)] * len(after),
        out_specs=[distant if is_far else in_place for is_far in out_far] + [in_place],
        out_shape=[
            pltpu.HBM(output[0], output[1])
            if is_far
            else jax.ShapeDtypeStruct(output[0], output[1])
            for output, is_far in zip(outputs, out_far)
        ]
        + [jax.ShapeDtypeStruct((8, LANES), F32)],
        scratch_shapes=list(scratch) + fetched + stored + semaphores,
        compiler_params=pltpu.CompilerParams(vmem_limit_bytes=mebibytes * 1024 * 1024),
        cost_estimate=cost(microseconds),
        name=name,
    )(flags, *arrays, *after)
    return results, token


def far(array):
    return ("far", array)


def later(array):
    return ("later", array)


def begin(*refs):
    for ref in refs:
        ref.begin()


def blocks_of(length, size):
    return [slice(start, start + size) for start in range(0, length, size)]


def times_hot(left_side, hot, dims):
    total = 0.0
    for _ in range(3):
        term = left_side.astype(BF16)
        total += lax.dot_general(term, hot, (dims, ((), ())), preferred_element_type=F32)
        left_side = left_side - term.astype(F32)
    return total


def window_kernel(flags_ref, bucket_ref, table_ref, window_ref):
    heads, buckets = table_ref.shape
    width = bucket_ref.shape[1]
    places = lax.broadcasted_iota(jnp.int32, (buckets, width), 0)
    hot = jnp.where(places == bucket_ref[...], 1.0, 0.0).astype(BF16)
    offsets = times_hot(table_ref[...], hot, ((1,), (0,)))
    for head in range(heads):
        spread = jnp.broadcast_to(offsets[head : head + 1, :], (LANES, width))
        window_ref[head] = pltpu.roll(spread, width - LANES + 1, 1, stride=1, stride_axis=0)


def pack_kernel(flags_ref, features_ref, target_ref, ids_ref, sent_ref):
    core_width = sent_ref.shape[2]
    rest = features_ref.shape[2] - core_width
    mel_width = target_ref.shape[2]
    sent_ref[...] = jnp.zeros_like(sent_ref)
    features, target = features_ref.ready(), target_ref.ready()

    @pl.when(flags_ref[0] == 0)
    def _():
        for row in range(features_ref.shape[0]):
            sent_ref[2 * row] = features[row, :, :core_width]

    @pl.when(flags_ref[0] != 0)
    def _():
        for row in range(features_ref.shape[0]):
            sent_ref[2 * row, :, :rest] = features[row, :, core_width:]
            sent_ref[2 * row, :, rest : rest + mel_width] = target[row]
            start = rest + mel_width
            sent_ref[2 * row + 1, :, start : start + 2] = ids_ref[row]


def key_probs(keys, queries, window_ref, head, mask_ref):
    length = keys.shape[0]
    blocks = length // LANES
    bias = jnp.concatenate(
        [
            window_ref[head, :, LANES * (blocks - 1 - b) : LANES * (blocks - 1 - b) + length]
            for b in range(blocks)
        ],
        axis=0,
    )
    scores = times_transposed(keys, queries) + bias + mask_ref[...]
    powers = jnp.exp(scores - jnp.max(scores, axis=0, keepdims=True))
    return powers * (1.0 / column_sum(powers))


SPEECH_BIAS, FIRST_GAIN, FIRST_SHIFT, SECOND_GAIN, SECOND_SHIFT, UP_BIAS, DOWN_BIAS, POST_BIAS = range(8)


def vector(ref, row, width):
    return ref[row : row + 1, :width]


def attend_kernel(
    head_size,
    plain_width,
    flags_ref,
    own_ref,
    other_ref,
    speech_weight_ref,
    token_table_ref,
    vectors_ref,
    query_weight_ref,
    key_weight_ref,
    value_weight_ref,
    out_weight_ref,
    window_ref,
    column_ref,
    row_ref,
    embedded_ref,
    attended_ref,
    embedded_far_ref,
    normed_ref,
    queries_ref,
    keys_ref,
    values_ref,
    heads_ref,
    inputs_ref,
    extra_ref,
    mask_ref,
):
    length, half_width = own_ref.shape
    width = embedded_ref.shape[1]
    feat_width = inputs_ref.shape[1] - LANES
    first = flags_ref[0] == 0
    speech = flags_ref[1].astype(F32)
    scaling = jnp.asarray(head_size ** (-0.5), BF16)
    for rows in blocks_of(length, LANES):
        own, other = own_ref[rows, :], other_ref[rows, :]
        low = jnp.where(first, own, other)
        high = jnp.where(first, other, own)
        inputs_ref[rows, :half_width] = low
        inputs_ref[rows, half_width:feat_width] = high[:, : feat_width - half_width]
        extra = high[:, feat_width - half_width : feat_width - half_width + LANES]
        extra_ref[rows, :] = extra
        ids = extra[:, plain_width - feat_width : plain_width - feat_width + 1].astype(F32)
        places = lax.broadcasted_iota(jnp.int32, (LANES, LANES), 1).astype(F32)
        hot = jnp.where(ids == places, 1.0 - speech, 0.0)
        inputs_ref[rows, feat_width:] = hot.astype(BF16)
    inputs_ref.flush()
    speech_weight, token_table = speech_weight_ref.ready(), token_table_ref.ready()
    vectors = vectors_ref.ready()
    for rows in blocks_of(length, 2 * LANES):
        embedded = (
            matmul(inputs_ref[rows, :feat_width], speech_weight[...])
            + matmul(inputs_ref[rows, feat_width:], token_table[...])
            + vector(vectors, SPEECH_BIAS, width) * speech
        ).astype(BF16)
        embedded_ref[rows, :] = embedded
        embedded_far_ref[rows, :] = embedded
        normal, _ = normalize(embedded.astype(F32))
        normed_ref[rows, :] = (
            normal * vector(vectors, FIRST_GAIN, width) + vector(vectors, FIRST_SHIFT, width)
        ).astype(BF16)
    embedded_far_ref.flush()
    normed_ref.flush()
    query_weight, key_weight = query_weight_ref.ready(), key_weight_ref.ready()
    value_weight = value_weight_ref.ready()
    for rows in blocks_of(length, 2 * LANES):
        normed = normed_ref[rows, :]
        queries_ref[rows, :] = matmul(normed, query_weight[...]).astype(BF16) * scaling
        keys_ref[rows, :] = matmul(normed, key_weight[...]).astype(BF16)
        values_ref[rows, :] = matmul(normed, value_weight[...]).astype(BF16)
    queries_ref.flush()
    keys_ref.flush()
    values_ref.flush()
    mask_ref[...] = jnp.where(column_ref[...] == row_ref[...], 0.0, NEGATIVE)
    window = window_ref.ready()
    for head, columns in enumerate(blocks_of(queries_ref.shape[1], head_size)):
        probs = key_probs(
            keys_ref[:, columns], queries_ref[:, columns], window, head, mask_ref
        ).astype(BF16)
        heads_ref[:, columns] = contract_rows(probs, values_ref[:, columns]).astype(BF16)
    heads_ref.flush()
    out_weight = out_weight_ref.ready()
    for rows in blocks_of(length, 2 * LANES):
        attended_ref[rows, :] = matmul(heads_ref[rows, :], out_weight[...]).astype(BF16)


def forward_kernel(
    flags_ref,
    embedded_ref,
    own_ref,
    other_ref,
    vectors_ref,
    up_weight_ref,
    down_weight_ref,
    mixed_ref,
    slope_ref,
    branch_ref,
    mixed_far_ref,
    normed_ref,
    active_ref,
):
    length, width = embedded_ref.shape
    units = active_ref.shape[1]
    vectors = vectors_ref.ready()
    for rows in blocks_of(length, 2 * LANES):
        mixed = embedded_ref[rows, :].astype(F32) + (
            own_ref[rows, :].astype(F32) + other_ref[rows, :].astype(F32)
        )
        mixed_ref[rows, :] = mixed
        mixed_far_ref[rows, :] = mixed
        normal, _ = normalize(mixed)
        normed_ref[rows, :] = (
            normal * vector(vectors, SECOND_GAIN, width) + vector(vectors, SECOND_SHIFT, width)
        ).astype(BF16)
    mixed_far_ref.flush()
    for rows in blocks_of(length, 2 * LANES):
        hidden = matmul(normed_ref[rows, :], up_weight_ref[...]) + vector(vectors, UP_BIAS, units)
        square = hidden * hidden
        inner = 0.7978845608028654 * hidden * (1.0 + 0.044715 * square)
        curve = jnp.tanh(inner)
        half = 0.5 * (1.0 + curve)
        active = (hidden * half).astype(BF16)
        active_ref[rows, :] = active
        slope_ref[rows, :] = half + 0.5 * hidden * (1.0 - curve * curve) * (
            0.7978845608028654 * (1.0 + 0.134145 * square)
        )
        branch_ref[rows, :] = matmul(active, down_weight_ref[...]).astype(BF16)


def loss_kernel(
    mel_width,
    vocab_size,
    flags_ref,
    mixed_ref,
    own_ref,
    other_ref,
    vectors_ref,
    mel_weight_ref,
    vocab_weight_ref,
    extra_ref,
    slope_ref,
    up_weight_ref,
    down_weight_ref,
    active_ref,
    normed_ref,
    first_ref,
    second_ref,
    first_kept_ref,
    second_kept_ref,
    grad_normed_ref,
    grad_final_far_ref,
    final_ref,
    grad_post_ref,
    sums_ref,
    post_weight_ref,
    grad_final_ref,
    grad_hidden_ref,
):
    length, width = mixed_ref.shape
    units = slope_ref.shape[1]
    speech = flags_ref[1].astype(F32)
    mel_scale = speech * (1.0 / (mel_width * length))
    text_scale = (1.0 - speech) * (1.0 / length)
    vectors = vectors_ref.ready()
    post_weight_ref[:LANES, :] = mel_weight_ref[...]
    post_weight_ref[LANES:, :] = vocab_weight_ref[...]
    totals = None
    for rows in blocks_of(length, 2 * LANES):
        final = mixed_ref[rows, :] + (
            own_ref[rows, :].astype(F32) + other_ref[rows, :].astype(F32)
        )
        final = (final + vector(vectors, DOWN_BIAS, width)).astype(BF16)
        final_ref[rows, :] = final
        results = times_transposed(final, post_weight_ref[...])
        results += vector(vectors, POST_BIAS, 2 * LANES)
        extra = extra_ref[rows, :].astype(F32)
        places = lax.broadcasted_iota(jnp.int32, extra.shape, 1)
        error = jnp.where(places < mel_width, results[:, :LANES] - extra, 0.0)
        smooth = jnp.sqrt(error * error + 1.0)
        grad_mel = error / smooth * mel_scale
        logits = jnp.where(places < vocab_size, results[:, LANES:], NEGATIVE)
        shifted = logits - jnp.max(logits, axis=-1, keepdims=True)
        powers = jnp.exp(shifted)
        power_sum = jnp.sum(powers, axis=-1, keepdims=True)
        label = extra[:, mel_width + 1 : mel_width + 2] == places.astype(F32)
        picked = jnp.sum(jnp.where(label, shifted, 0.0), axis=-1, keepdims=True)
        text_loss = column_sum(jnp.log(power_sum) - picked) * text_scale
        mel_loss = column_sum((smooth - 1.0) * mel_scale)
        loss = mel_loss + jnp.where(places[:1] == 0, text_loss, 0.0)
        grad_text = (powers / power_sum - jnp.where(label, 1.0, 0.0)) * text_scale
        grad_post = jnp.concatenate([grad_mel, grad_text], axis=1).astype(BF16)
        grad_post_ref[rows, :] = grad_post
        grad_final = matmul(grad_post, post_weight_ref[...]).astype(BF16)
        grad_final_ref[rows, :] = grad_final
        grad_final_far_ref[rows, :] = grad_final
        grad_active = times_transposed(grad_final, down_weight_ref[...])
        grad_hidden = (slope_ref[rows, :] * grad_active).astype(BF16)
        grad_hidden_ref[rows, :] = grad_hidden
        grad_normed_ref[rows, :] = times_transposed(grad_hidden, up_weight_ref[...]).astype(BF16)
        sums = (
            loss,
            column_sum(grad_post.astype(F32)),
            column_sum(grad_final.astype(F32)),
            column_sum(grad_hidden.astype(F32)),
        )
        totals = sums if totals is None else [a + b for a, b in zip(totals, sums)]
    final_ref.flush()
    grad_post_ref.flush()
    grad_final_far_ref.flush()
    sums_ref[...] = jnp.zeros(sums_ref.shape, F32)
    sums_ref[0:1, :LANES] = jnp.broadcast_to(
        jnp.sum(totals[0], axis=1, keepdims=True), (1, LANES)
    )
    sums_ref[0:1, LANES : 3 * LANES] = totals[1]
    sums_ref[1:2, :width] = totals[2]
    sums_ref[2:3, :] = totals[3]
    sums_ref.flush()
    count, block, cut = units // 2, units // 2, width // 2
    for first_half, second_half, first, second in (
        (flags_ref[2], flags_ref[3], first_ref, second_ref),
        (1 - flags_ref[2], 1 - flags_ref[3], first_kept_ref, second_kept_ref),
    ):
        second[...] = contract_rows(
            normed_ref[:, cut:], wide(grad_hidden_ref, second_half * block, block)
        ).astype(BF16)
        second.flush()
        first[:count, :] = contract_rows(
            wide(active_ref, first_half * count, count), grad_final_ref[...]
        ).astype(BF16)
        first[count:, :] = contract_rows(
            normed_ref[:, :cut], wide(grad_hidden_ref, first_half * block, block)
        ).astype(BF16)
        first.flush()


def wide(ref, start, size):
    return ref[:, pl.ds(pl.multiple_of(start, LANES), size)]


def back_kernel(
    head_size,
    flags_ref,
    own_ref,
    other_ref,
    mixed_ref,
    grad_final_ref,
    vectors_ref,
    out_weight_ref,
    queries_ref,
    keys_ref,
    values_ref,
    window_ref,
    column_ref,
    row_ref,
    query_weight_ref,
    key_weight_ref,
    value_weight_ref,
    normed_ref,
    heads_ref,
    grad_post_ref,
    final_ref,
    grad_normed_ref,
    sent_ref,
    kept_ref,
    grad_mixed_ref,
    post_sent_ref,
    post_kept_ref,
    grad_offsets_ref,
    sums_ref,
    grad_low_ref,
    grad_heads_ref,
    grad_projected_ref,
    mask_ref,
    probs_ref,
    scores_ref,
    window_sum_ref,
    post_ref,
):
    length, head_width = queries_ref.shape
    width = grad_low_ref.shape[1]
    blocks = length // LANES
    mixed, grad_final, vectors = mixed_ref.ready(), grad_final_ref.ready(), vectors_ref.ready()
    out_weight = out_weight_ref.ready()
    gain_sum, shift_sum = 0.0, 0.0
    for rows in blocks_of(length, 2 * LANES):
        grad_normed = own_ref[rows, :].astype(F32) + other_ref[rows, :].astype(F32)
        normal, inverse = normalize(mixed[rows, :])
        gain_sum += column_sum(grad_normed * normal)
        shift_sum += column_sum(grad_normed)
        grad_mixed = grad_final[rows, :].astype(F32) + norm_back(
            grad_normed, normal, inverse, vector(vectors, SECOND_GAIN, width)
        )
        grad_mixed_ref[rows, :] = grad_mixed
        grad_low = grad_mixed.astype(BF16)
        grad_low_ref[rows, :] = grad_low
        grad_heads_ref[rows, :] = times_transposed(grad_low, out_weight[...]).astype(BF16)
    grad_mixed_ref.flush()
    sums_ref[...] = jnp.zeros(sums_ref.shape, F32)
    sums_ref[0:1, :] = gain_sum
    sums_ref[1:2, :] = shift_sum
    sums_ref.flush()
    mask_ref[...] = jnp.where(column_ref[...] == row_ref[...], 0.0, NEGATIVE)
    queries_ref, keys_ref, values_ref = queries_ref.ready(), keys_ref.ready(), values_ref.ready()
    window = window_ref.ready()
    scaling = head_size ** (-0.5)
    for head, columns in enumerate(blocks_of(head_width, head_size)):
        keys, queries = keys_ref[:, columns], queries_ref[:, columns]
        grads = grad_heads_ref[:, columns]
        probs = key_probs(keys, queries, window, head, mask_ref)
        weighted = probs * times_transposed(values_ref[:, columns], grads)
        grad_scores = weighted - probs * column_sum(weighted)
        probs_ref[...] = probs.astype(BF16)
        scores_ref[...] = grad_scores.astype(BF16)
        window_sum_ref[...] = jnp.zeros_like(window_sum_ref)
        for block in range(blocks):
            start = LANES * (blocks - 1 - block)
            window_sum_ref[:, start : start + length] += grad_scores[
                LANES * block : LANES * (block + 1)
            ]
        start = head * head_size
        for kind, value in enumerate(
            (
                contract_rows(scores_ref[...], keys) * scaling,
                matmul(scores_ref[...], queries),
                matmul(probs_ref[...], grads),
            )
        ):
            grad_projected_ref[
                :, kind * head_width + start : kind * head_width + start + head_size
            ] = value.astype(BF16)
        diagonal = window_sum_ref[...]
        half = LANES // 2
        while half >= 1:
            diagonal = pltpu.roll(diagonal[:half], half, 1) + diagonal[half:]
            half //= 2
        grad_offsets_ref[head : head + 1, :] = diagonal
    grad_offsets_ref.flush()
    for rows in blocks_of(length, 2 * LANES):
        total = 0.0
        for kind, weight_ref in enumerate((query_weight_ref, key_weight_ref, value_weight_ref)):
            total += times_transposed(
                grad_projected_ref[rows, kind * head_width : (kind + 1) * head_width],
                weight_ref.ready()[...],
            )
        grad_normed_ref[rows, :] = total.astype(BF16)
    normed, heads = normed_ref.ready(), heads_ref.ready()
    grad_post, final = grad_post_ref.ready(), final_ref.ready()
    half = width // 2
    count = head_width // 2
    post_rows = LANES // 2
    post_ref[...] = contract_rows(wide(grad_post, flags_ref[0] * LANES, LANES), final[...])
    for first_ref, post_half_ref, first, second in (
        (sent_ref, post_sent_ref, flags_ref[2], flags_ref[3]),
        (kept_ref, post_kept_ref, 1 - flags_ref[2], 1 - flags_ref[3]),
    ):
        post_half_ref[...] = post_ref[
            pl.ds(pl.multiple_of(second * post_rows, post_rows), post_rows), :
        ].astype(BF16)
        post_half_ref.flush()
        grad_project = contract_rows(
            wide(normed, first * half, half), grad_projected_ref[...]
        ).astype(BF16)
        first_ref[:half, :] = grad_project[:, : 2 * head_width]
        first_ref[half : half + count, :head_width] = grad_project[:count, 2 * head_width :]
        first_ref[half : half + count, head_width:] = grad_project[count:, 2 * head_width :]
        grad_out = contract_rows(heads[...], wide(grad_low_ref, first * half, half))
        first_ref[half + count :, :half] = grad_out[:count].astype(BF16)
        first_ref[half + count :, half:] = grad_out[count:].astype(BF16)
        first_ref.flush()


def input_kernel(
    flags_ref,
    own_ref,
    other_ref,
    embedded_ref,
    grad_mixed_ref,
    vectors_ref,
    speech_weight_ref,
    inputs_ref,
    post_sent_ref,
    post_kept_ref,
    loss_sums_ref,
    back_sums_ref,
    grad_offsets_ref,
    bucket_ref,
    sent_ref,
    kept_ref,
    feature_back_ref,
    terms_ref,
    grad_embedded_ref,
    hot_ref,
):
    length, width = own_ref.shape
    embedded, grad_mixed = embedded_ref.ready(), grad_mixed_ref.ready()
    vectors, speech_weight = vectors_ref.ready(), speech_weight_ref.ready()
    feat_width = speech_weight.shape[0]
    core_width = feat_width // 2
    speech = flags_ref[1].astype(F32)
    core = flags_ref[0]
    gain_sum, shift_sum, bias_sum = 0.0, 0.0, 0.0
    core_weight = speech_weight[pl.ds(pl.multiple_of(core * core_width, core_width), core_width), :]
    for rows in blocks_of(length, 2 * LANES):
        grad_normed = own_ref[rows, :].astype(F32) + other_ref[rows, :].astype(F32)
        normal, inverse = normalize(embedded[rows, :].astype(F32))
        gain_sum += column_sum(grad_normed * normal)
        shift_sum += column_sum(grad_normed)
        grad_embedded = (
            grad_mixed[rows, :]
            + norm_back(grad_normed, normal, inverse, vector(vectors, FIRST_GAIN, width))
        ).astype(BF16)
        grad_embedded_ref[rows, :] = grad_embedded
        bias_sum += column_sum(grad_embedded.astype(F32))
        feature_back_ref[rows, :] = times_transposed(grad_embedded, core_weight).astype(BF16)
    inputs = inputs_ref.ready()
    hot_ref[...] = contract_rows(inputs[:, feat_width:], grad_embedded_ref[...])
    post_rows = LANES // 2
    feat_rows = core_width // 2
    hot_rows = LANES // 4
    small_rows = 2 * SMALL_ROWS
    for which_ref, post_ref, half, base in (
        (sent_ref, post_sent_ref, flags_ref[3], small_rows),
        (kept_ref, post_kept_ref, 1 - flags_ref[3], 0),
    ):
        which_ref[base : base + post_rows, :] = post_ref[...]
        start = base + post_rows
        which_ref[start : start + feat_rows, :] = contract_rows(
            wide(inputs, core * core_width + half * feat_rows, feat_rows), grad_embedded_ref[...]
        ).astype(BF16)
        start += feat_rows
        which_ref[start : start + hot_rows, :] = hot_ref[
            pl.ds(pl.multiple_of(core * 2 * hot_rows + half * hot_rows, hot_rows), hot_rows), :
        ].astype(BF16)
        which_ref[start + hot_rows :, :] = jnp.zeros((hot_rows, width), BF16)
    loss_sums, back_sums = loss_sums_ref.ready(), back_sums_ref.ready()
    bias_rows = loss_sums.shape[1] // width
    rows = [loss_sums[0:1, :width], loss_sums[1:2, :width], back_sums[0:1, :], back_sums[1:2, :]]
    rows += [gain_sum, shift_sum, bias_sum * speech]
    rows += [loss_sums[2:3, part * width : (part + 1) * width] for part in range(bias_rows)]
    terms_ref[...] = jnp.zeros_like(terms_ref)
    for place, row in enumerate(rows):
        terms_ref[place : place + 1, :] = row
    start = len(rows)
    heads, offset_count = grad_offsets_ref.shape
    places = lax.broadcasted_iota(jnp.int32, (width // 2, offset_count), 0)
    hot = jnp.where(places == bucket_ref[...], 1.0, 0.0).astype(BF16)
    terms_ref[start : start + heads, : width // 2] = times_hot(
        grad_offsets_ref[...], hot, ((1,), (1,))
    )
    terms = terms_ref[...]
    high = terms.astype(BF16)
    rest = (terms - high.astype(F32)).astype(BF16)
    terms_ref[...] = high.astype(F32) + rest.astype(F32)
    sent_ref[:SMALL_ROWS, :] = high
    sent_ref[SMALL_ROWS:small_rows, :] = rest


def rows_at(ref, start, count):
    return ref[pl.ds(pl.multiple_of(start, 16), count), :]


def add_low(left_side, right_side):
    return (left_side.astype(F32) + right_side.astype(F32)).astype(BF16)


def add_small(terms_ref, came_ref):
    return terms_ref[...] + (
        came_ref[:SMALL_ROWS, :].astype(F32)
        + came_ref[SMALL_ROWS : 2 * SMALL_ROWS, :].astype(F32)
    )


def send_small(small, sent_ref, terms_ref):
    high = small.astype(BF16)
    rest = (small - high.astype(F32)).astype(BF16)
    sent_ref[:SMALL_ROWS, :] = high
    sent_ref[SMALL_ROWS : 2 * SMALL_ROWS, :] = rest
    terms_ref[...] = high.astype(F32) + rest.astype(F32)


def add_kernel(with_small, mine_ref, kept_ref, came_ref, *refs):
    half = kept_ref.shape[0] // 2
    base = 0
    if with_small:
        base = 2 * SMALL_ROWS
        terms_ref, sent_ref, next_ref, new_terms_ref = refs
        send_small(add_small(terms_ref, came_ref), sent_ref, new_terms_ref)
    else:
        sent_ref, next_ref = refs
    mine = mine_ref[0]
    start = (1 - mine) * half
    sent_ref[base:, :] = add_low(
        rows_at(kept_ref, start, half), rows_at(came_ref, base + start, half)
    )
    start = mine * half
    next_ref[...] = add_low(
        rows_at(kept_ref, start, half), rows_at(came_ref, base + start, half)
    )


def join_kernel(with_small, mine_ref, kept_ref, came_ref, kept_two_ref, came_two_ref, *refs):
    start = base = 0
    if with_small:
        start = base = 2 * SMALL_ROWS
        terms_ref, sent_ref, next_ref, next_two_ref, new_terms_ref = refs
        send_small(add_small(terms_ref, came_two_ref), sent_ref, new_terms_ref)
    else:
        sent_ref, next_ref, next_two_ref = refs
    for kept, came, extra, out_ref in (
        (kept_ref, came_ref, 0, next_ref),
        (kept_two_ref, came_two_ref, base, next_two_ref),
    ):
        half = out_ref.shape[0]
        place = (1 - mine_ref[0]) * half
        sent_ref[start : start + half, :] = add_low(
            rows_at(kept, place, half), rows_at(came, extra + place, half)
        )
        start += half
        place = mine_ref[0] * half
        out_ref[...] = add_low(rows_at(kept, place, half), rows_at(came, extra + place, half))


def finish_kernel(with_small, kept_ref, kept_two_ref, came_ref, *refs):
    start = 0
    if with_small:
        start = 2 * SMALL_ROWS
        terms_ref, total_ref, small_ref = refs
        small_ref[...] = add_small(terms_ref, came_ref)
    else:
        (total_ref,) = refs
    out = 0
    for kept in (kept_ref, kept_two_ref):
        count = kept.shape[0]
        total_ref[out : out + count, :] = add_low(kept[...], came_ref[start : start + count, :])
        start += count
        out += count


def whole_join_kernel(with_small, kept_ref, came_ref, kept_two_ref, came_two_ref, *refs):
    start = base = 0
    if with_small:
        start = base = 2 * SMALL_ROWS
        terms_ref, joint_ref, new_terms_ref = refs
        send_small(add_small(terms_ref, came_two_ref), joint_ref, new_terms_ref)
    else:
        (joint_ref,) = refs
    count = kept_ref.shape[0]
    joint_ref[start : start + count, :] = add_low(kept_ref[...], came_ref[...])
    joint_ref[start + count :, :] = add_low(kept_two_ref[...], came_two_ref[base:, :])


def whole_finish_kernel(with_small, joint_ref, came_ref, *refs):
    start = 0
    if with_small:
        start = 2 * SMALL_ROWS
        terms_ref, *outs, small_ref = refs
        small_ref[...] = add_small(terms_ref, came_ref)
    else:
        outs = refs
    for out_ref in outs:
        rows = slice(start, start + out_ref.shape[0])
        out_ref[...] = add_low(joint_ref[rows, :], came_ref[rows, :])
        start += out_ref.shape[0]


def place_kernel(mine_ref, own_ref, came_ref, out_ref):
    half = own_ref.shape[0]
    out_ref[pl.ds(pl.multiple_of(mine_ref[0] * half, 16), half), :] = own_ref[...]
    out_ref[pl.ds(pl.multiple_of((1 - mine_ref[0]) * half, 16), half), :] = came_ref[...]


def part_kernel(mine_ref, own_ref, came_ref, first_ref, second_ref):
    start = 0
    for out_ref in (first_ref, second_ref):
        half = out_ref.shape[0] // 2
        for ref, place in ((own_ref, mine_ref[0]), (came_ref, 1 - mine_ref[0])):
            out_ref[pl.ds(pl.multiple_of(place * half, 16), half), :] = ref[
                start : start + half, :
            ]
        start += half


def early_place_kernel(
    flags_ref, first_ref, first_came_ref, second_ref, second_came_ref, down_ref, up_ref
):
    width = down_ref.shape[1]
    units = down_ref.shape[0] // 2
    cut = width // 2
    for first, second, first_half, second_half in (
        (first_ref, second_ref, flags_ref[0], flags_ref[1]),
        (first_came_ref, second_came_ref, 1 - flags_ref[0], 1 - flags_ref[1]),
    ):
        down_ref[pl.ds(pl.multiple_of(first_half * units, units), units), :] = first[
            :units, :
        ].astype(F32)
        columns = pl.ds(pl.multiple_of(first_half * units, LANES), units)
        up_ref[:cut, columns] = first[units:, :].astype(F32)
        columns = pl.ds(pl.multiple_of(second_half * units, LANES), units)
        up_ref[cut:, columns] = second[...].astype(F32)


def late_place_kernel(
    half_ref, part_ref, query_ref, key_ref, value_ref, out_ref, *buffers_and_semaphore
):
    *buffers, semaphore = buffers_and_semaphore
    query_buffer, key_buffer, value_buffer, out_buffer = buffers
    width = part_ref.shape[1]
    head_width = query_ref.shape[1]
    half = width // 2
    count = head_width // 2
    place = pl.ds(pl.multiple_of(half_ref[0] * half, LANES), half)
    copies = [
        pltpu.make_async_copy(buffer, target, semaphore.at[number])
        for number, (buffer, target) in enumerate(
            (
                (query_buffer, query_ref.at[place, :]),
                (key_buffer, key_ref.at[place, :]),
                (value_buffer, value_ref.at[place, :]),
                (out_buffer, out_ref.at[:, place]),
            )
        )
    ]
    query_buffer[...] = part_ref[:half, :head_width].astype(F32)
    copies[0].start()
    key_buffer[...] = part_ref[:half, head_width:].astype(F32)
    copies[1].start()
    for part in range(2):
        columns = slice(part * head_width, (part + 1) * head_width)
        value_buffer[part * count : (part + 1) * count, :] = part_ref[
            half : half + count, columns
        ].astype(F32)
    copies[2].start()
    for part in range(2):
        columns = slice(part * half, (part + 1) * half)
        out_buffer[part * count : (part + 1) * count, :] = part_ref[
            half + count :, columns
        ].astype(F32)
    copies[3].start()
    for copy in copies:
        copy.wait()


def place_late(links, half, part, outputs, head_width, after=()):
    width = part.shape[1]
    shapes = [(width, head_width)] * 3 + [(head_width, width)]
    buffers = [(width // 2, head_width)] * 3 + [(head_width, width // 2)]
    distant = pl.BlockSpec(memory_space=pltpu.HBM)
    near = pl.BlockSpec(memory_space=pltpu.VMEM)
    outputs = [] if outputs is None else list(outputs)

    def kernel(half_ref, part_ref, *refs):
        late_place_kernel(half_ref, part_ref, *refs[len(outputs) + len(after) :])

    return pl.pallas_call(
        kernel,
        in_specs=[pl.BlockSpec(memory_space=pltpu.SMEM), near]
        + [distant] * len(outputs)
        + [pl.BlockSpec(memory_space=pl.ANY)] * len(after),
        out_specs=[distant] * 4,
        out_shape=[jax.ShapeDtypeStruct(shape, F32) for shape in shapes],
        input_output_aliases={2 + number: number for number in range(len(outputs))},
        scratch_shapes=[pltpu.VMEM(shape, F32) for shape in buffers]
        + [pltpu.SemaphoreType.DMA((4,))],
        compiler_params=pltpu.CompilerParams(vmem_limit_bytes=16 * 1024 * 1024),
        name="late_place",
    )(half, part, *outputs, *after)


def small_kernel(
    rows,
    terms_ref,
    loss_ref,
    mel_ref,
    vocab_ref,
    down_ref,
    gain_two_ref,
    shift_two_ref,
    gain_one_ref,
    shift_one_ref,
    speech_ref,
    up_ref,
    table_ref,
):
    width = down_ref.shape[0]
    loss_ref[...] = terms_ref[0:1, 0:1] * (1.0 / rows)
    mel_ref[...] = terms_ref[0, LANES : LANES + mel_ref.shape[0]]
    vocab_ref[...] = terms_ref[0, 2 * LANES : 2 * LANES + vocab_ref.shape[0]]
    row = 1
    for ref in (down_ref, gain_two_ref, shift_two_ref, gain_one_ref, shift_one_ref, speech_ref):
        ref[...] = terms_ref[row, :]
        row += 1
    for columns in blocks_of(up_ref.shape[0], width):
        up_ref[columns] = terms_ref[row, :]
        row += 1
    table_ref[...] = terms_ref[row : row + table_ref.shape[0], : table_ref.shape[1]]


def shared_place_kernel(
    flags_ref,
    own_ref,
    own_other_ref,
    came_ref,
    came_other_ref,
    speech_ref,
    table_ref,
    mel_ref,
    vocab_ref,
    post_ref,
    hot_ref,
):
    core = flags_ref[2]
    post_rows = LANES // 2
    feat_rows = speech_ref.shape[0] // 4
    hot_rows = LANES // 4
    for ref, place, half in (
        (own_ref, core, flags_ref[1]),
        (came_ref, core, 1 - flags_ref[1]),
        (own_other_ref, 1 - core, flags_ref[1]),
        (came_other_ref, 1 - core, 1 - flags_ref[1]),
    ):
        spot = pl.multiple_of(place * LANES + half * post_rows, 16)
        post_ref[pl.ds(spot, post_rows), :] = ref[:post_rows, :].astype(F32)
        start = post_rows
        spot = pl.multiple_of((place * 2 + half) * feat_rows, 16)
        speech_ref[pl.ds(spot, feat_rows), :] = ref[start : start + feat_rows, :].astype(F32)
        start += feat_rows
        spot = pl.multiple_of((place * 2 + half) * hot_rows, 16)
        hot_ref[pl.ds(spot, hot_rows), :] = ref[start : start + hot_rows, :].astype(F32)
    table_ref[...] = hot_ref[: table_ref.shape[0], :]
    mel_ref[...] = post_ref[: mel_ref.shape[0], :]
    vocab_ref[...] = post_ref[LANES : LANES + vocab_ref.shape[0], :]


def swap_cores(array):
    return lax.ppermute(array, "mp", [(0, 1), (1, 0)])


ORDERS = (((0, 1, 2, 3), (1, 2, 0, 3)), ((2, 0, 1, 3), (2, 0, 1, 3)))
STEPS = 4


class Links:
    def __init__(self, devices, cores, index, core):
        self.devices, self.cores, self.index, self.core = devices, cores, index, core
        self.bits = devices.bit_length() - 1
        self.token = None
        self.pending = []

    def exchange(self, array, directions):
        pairs = [
            (
                place * self.cores + core,
                (place ^ (1 << directions[core])) * self.cores + core,
            )
            for place in range(self.devices)
            for core in range(self.cores)
        ]
        return lax.ppermute(array, ("dp", "mp"), pairs)

    def mine(self, directions):
        direction = jnp.where(self.core == 0, directions[0], directions[1])
        return ((self.index >> direction) & 1).astype(jnp.int32)

    def run(self, kernel, name, flags, operands, outputs, scratch=(), mebibytes=16, after=()):
        results, self.token = run_kernel(
            kernel,
            name,
            0.05,
            flags,
            operands,
            outputs,
            scratch,
            mebibytes,
            after if self.token is None else (self.token, *after),
        )
        return results

    def later(self, kernel, flags, operands, outputs, take):
        self.pending.append((kernel, flags, operands, outputs, take))

    def flush(self, name, after=()):
        pieces, self.pending = self.pending, []
        flags = [flag for piece in pieces for flag in piece[1]] or [jnp.int32(0)]
        operands = [each for piece in pieces for each in piece[2]]
        outputs = [each for piece in pieces for each in piece[3]]

        def kernel(flags_ref, *refs):
            ins, outs = list(refs[: len(operands)]), list(refs[len(operands) :])
            count = 0
            for body, piece_flags, piece_ins, piece_outs, _ in pieces:
                body(
                    *([[flags_ref[count + place] for place in range(len(piece_flags))]] if piece_flags else []),
                    *[ins.pop(0) for _ in piece_ins],
                    *[outs.pop(0) for _ in piece_outs],
                )
                count += len(piece_flags)

        results = self.run(kernel, name, jnp.stack(flags), operands, outputs, after=after)
        for piece in pieces:
            count = len(piece[3])
            piece[4](results[:count])
            results = results[count:]


def step_directions(slot, step):
    return tuple(order[step] for order in ORDERS[slot])


def shape_of(operand):
    return (operand[1] if isinstance(operand, tuple) else operand).shape


class Wave:
    def __init__(self, links, name, sent, kept, terms=None):
        self.links = links
        self.name = name
        self.terms = terms
        self.sent = list(sent)
        self.kept = list(kept)
        self.came = [None, None]

    def scatter(self, step):
        for slot in range(2):
            self.came[slot] = self.links.exchange(self.sent[slot], step_directions(slot, step))

    def piece(self, kernel, directions, operands, outputs, small, take):
        if small:
            operands = operands + [self.terms]
            outputs = outputs + [((SMALL_ROWS, outputs[0][0][1]), F32)]

        def take_all(results):
            if small:
                *results, self.terms = results
            take(results)

        self.links.later(
            functools.partial(kernel, small),
            [] if directions is None else [self.links.mine(directions)],
            operands,
            outputs,
            take_all,
        )

    def add(self, step, distant=False):
        for slot in range(2):
            small = slot == 1 and self.terms is not None
            rows, width = shape_of(self.kept[slot])
            half, extra = rows // 2, 2 * SMALL_ROWS if small else 0

            def take(results, slot=slot):
                self.sent[slot], self.kept[slot] = results

            self.piece(
                add_kernel,
                step_directions(slot, step + 1),
                [self.kept[slot], far(self.came[slot]) if distant else self.came[slot]],
                [
                    ((half + extra, width), BF16),
                    ((half, width), BF16, "far") if step == 0 and distant else ((half, width), BF16),
                ],
                small,
                take,
            )

    def join(self):
        halves = [shape_of(kept)[0] // 2 for kept in self.kept]
        width = shape_of(self.kept[0])[1]
        small = self.terms is not None

        def take(results):
            self.sent_joint, *self.kept = results

        self.piece(
            join_kernel,
            step_directions(0, STEPS - 1),
            [self.kept[0], self.came[0], self.kept[1], self.came[1]],
            [((sum(halves) + (2 * SMALL_ROWS if small else 0), width), BF16)]
            + [((half, width), BF16) for half in halves],
            small,
            take,
        )

    def scatter_joint(self):
        self.came_joint = self.links.exchange(self.sent_joint, step_directions(0, STEPS - 1))

    def finish(self):
        self.counts = [shape_of(kept)[0] for kept in self.kept]
        width = shape_of(self.kept[0])[1]

        def take(results):
            (self.joint,) = results

        self.piece(
            finish_kernel,
            None,
            [*self.kept, self.came_joint],
            [((sum(self.counts), width), BF16)],
            self.terms is not None,
            take,
        )

    def sum_others(self):
        for direction in range(STEPS, self.links.bits):
            both = (direction, direction)
            came = self.links.exchange(self.joint, both)
            self.joint = (self.joint.astype(F32) + came.astype(F32)).astype(BF16)
            if self.terms is not None:
                self.terms = self.terms + self.links.exchange(self.terms, both)

    def gather_joint(self):
        self.came_joint = self.links.exchange(self.joint, step_directions(0, STEPS - 1))

    def part(self):
        width = self.joint.shape[1]

        def take(results):
            self.shares = list(results)

        self.links.later(
            part_kernel,
            [self.links.mine(step_directions(0, STEPS - 1))],
            [self.joint, self.came_joint],
            [((2 * count, width), BF16) for count in self.counts],
            take,
        )

    def join_whole(self):
        self.counts = [shape_of(kept)[0] for kept in self.kept]
        width = shape_of(self.kept[0])[1]
        small = self.terms is not None

        def take(results):
            (self.joint,) = results

        self.piece(
            whole_join_kernel,
            None,
            [self.kept[0], self.came[0], self.kept[1], self.came[1]],
            [((sum(self.counts) + (2 * SMALL_ROWS if small else 0), width), BF16)],
            small,
            take,
        )

    def exchange_whole(self):
        self.came_joint = self.links.exchange(self.joint, step_directions(0, STEPS - 1))

    def finish_whole(self):
        width = self.joint.shape[1]

        def take(results):
            self.shares = list(results)

        self.piece(
            whole_finish_kernel,
            None,
            [self.joint, self.came_joint],
            [((count, width), BF16) for count in self.counts],
            self.terms is not None,
            take,
        )

    def sum_others_whole(self):
        for direction in range(STEPS, self.links.bits):
            both = (direction, direction)
            self.shares = [
                (share.astype(F32) + self.links.exchange(share, both).astype(F32)).astype(BF16)
                for share in self.shares
            ]

    def gather(self, step):
        self.came = [
            self.links.exchange(rows, step_directions(slot, step))
            for slot, rows in enumerate(self.shares)
        ]

    def place(self, step):
        for slot in range(2):

            def take(results, slot=slot):
                (self.shares[slot],) = results

            rows, width = shape_of(self.shares[slot])
            self.links.later(
                place_kernel,
                [self.links.mine(step_directions(slot, step))],
                [self.shares[slot], self.came[slot]],
                [((2 * rows, width), BF16)],
                take,
            )


def per_device(
    features,
    token_ids,
    mel_target,
    token_target,
    segments,
    row_device,
    offset_bucket,
    speech_weight,
    speech_bias,
    token_table,
    first_gain,
    first_shift,
    query_weight,
    key_weight,
    value_weight,
    bias_table,
    out_weight,
    second_gain,
    second_shift,
    up_weight,
    up_bias,
    down_weight,
    down_bias,
    mel_weight,
    mel_bias,
    vocab_weight,
    vocab_bias,
):
    devices = lax.axis_size("dp")
    device_index = lax.axis_index("dp")
    core = lax.axis_index("mp")
    cores = lax.axis_size("mp")
    rows_speech, part_len, feat_width = features.shape
    rows_total, length = segments.shape
    model_width = speech_weight.shape[1]
    vocab_size = token_table.shape[0]
    mel_width = mel_weight.shape[1]
    local_heads = bias_table.shape[1]
    buckets = bias_table.shape[0]
    head_width = query_weight.shape[1]
    head_size = head_width // local_heads
    units = up_weight.shape[1]
    is_speech = device_index % 2 == 0
    my_row = device_index // 2 + jnp.where(is_speech, 0, rows_speech)
    links = Links(devices, cores, device_index, core)
    flags = jnp.stack(
        [
            core,
            is_speech.astype(jnp.int32),
            1 - links.mine(step_directions(0, 0)),
            1 - links.mine(step_directions(1, 0)),
        ]
    ).astype(jnp.int32)

    plain_width = feat_width + mel_width
    core_width = -(-(plain_width + 2) // (LANES * cores)) * LANES
    ids = jnp.stack([token_ids, token_target], axis=2).astype(BF16)
    (packed,), _ = run_kernel(
        pack_kernel,
        "pack_rows",
        1,
        flags,
        [far(features), far(mel_target), ids],
        [((rows_total, part_len, core_width), BF16)],
    )
    arrived = lax.all_to_all(packed, "dp", split_axis=0, concat_axis=0, tiled=True)
    arrived = arrived.reshape(length, core_width)

    my_segments = lax.dynamic_slice_in_dim(segments, my_row, 1)
    segment_column = my_segments.reshape(length, 1)
    bucket_line = jnp.pad(offset_bucket, (0, 1), constant_values=-1).reshape(1, 2 * length)
    full_rows = lambda array: jnp.pad(array, ((0, LANES - array.shape[0]), (0, 0)))
    post_bias = jnp.concatenate(
        [jnp.pad(mel_bias, (0, LANES - mel_width)), jnp.pad(vocab_bias, (0, LANES - vocab_size))]
    )
    vectors = jnp.stack(
        [
            jnp.pad(each, (0, units - each.size))
            for each in (
                speech_bias,
                first_gain,
                first_shift,
                second_gain,
                second_shift,
                up_bias,
                down_bias,
                post_bias,
            )
        ]
    )
    token_rows, mel_rows, vocab_rows = (
        full_rows(array) for array in (token_table, mel_weight.T, vocab_weight.T)
    )
    (window,), window_token = run_kernel(
        window_kernel,
        "bias_window",
        3,
        flags,
        [bucket_line, bias_table.T],
        [((local_heads, LANES, 2 * length), F32, "far")],
        after=(far(vectors), far(token_rows)),
    )
    arrived, window_token = lax.optimization_barrier((arrived, window_token))

    model_low = ((length, model_width), BF16)
    head_low = ((length, head_width), BF16)
    (
        embedded,
        attended,
        embedded_far,
        normed_one,
        queries,
        key_rows,
        value_rows,
        heads_flat,
        inputs,
        extra,
    ), _ = run_kernel(
        functools.partial(attend_kernel, head_size, plain_width),
        "embed_and_attend",
        8,
        flags,
        [
            arrived,
            swap_cores(arrived),
            far(speech_weight),
            far(token_rows),
            far(vectors),
            far(query_weight),
            far(key_weight),
            far(value_weight),
            far(out_weight),
            far(window),
            segment_column,
            my_segments,
        ],
        [
            model_low,
            model_low,
            (*model_low, "far"),
            (*model_low, "far"),
            (*head_low, "far"),
            (*head_low, "far"),
            (*head_low, "far"),
            (*head_low, "far"),
            ((length, feat_width + LANES), BF16, "far"),
            ((length, LANES), BF16),
        ],
        [pltpu.VMEM((length, length), F32)],
        mebibytes=26,
        after=(window_token,),
    )
    (mixed, slope, branch, mixed_far, normed_two, active), _ = run_kernel(
        forward_kernel,
        "feed_forward",
        5,
        flags,
        [
            embedded,
            attended,
            swap_cores(attended),
            far(vectors),
            up_weight,
            down_weight,
        ],
        [
            ((length, model_width), F32),
            ((length, units), F32),
            model_low,
            ((length, model_width), F32, "far"),
            model_low,
            ((length, units), BF16),
        ],
        mebibytes=28,
    )
    early_shapes = [
        ((units // 2 + model_width // 2, model_width), BF16, "far"),
        ((model_width // 2, model_width), BF16, "far"),
    ]
    (
        *early_parts,
        grad_normed_two,
        grad_final_far,
        final_low,
        grad_post,
        loss_sums,
    ), links.token = run_kernel(
        functools.partial(loss_kernel, mel_width, vocab_size),
        "loss_and_feed_back",
        0.05,
        flags,
        [
            mixed,
            branch,
            swap_cores(branch),
            far(vectors),
            mel_rows,
            vocab_rows,
            extra,
            slope,
            up_weight,
            down_weight,
            active,
            normed_two,
        ],
        early_shapes * 2
        + [
            model_low,
            (*model_low, "far"),
            (*model_low, "far"),
            ((length, 2 * LANES), BF16, "far"),
            ((8, units), F32, "far"),
        ],
        [
            pltpu.VMEM((2 * LANES, model_width), BF16),
            pltpu.VMEM((length, model_width), BF16),
            pltpu.VMEM((length, units), BF16),
        ],
        mebibytes=34,
    )

    early = Wave(links, "early", early_parts[:2], [far(kept) for kept in early_parts[2:]])
    early.scatter(0)
    other_normed_two = swap_cores(grad_normed_two)
    part = ((model_width // 2 + head_width, model_width), BF16)
    post_part = ((LANES // 2, model_width), BF16)
    (
        grad_normed_one,
        late_sent,
        late_kept,
        grad_mixed,
        post_sent,
        post_kept,
        grad_offsets,
        back_sums,
    ) = links.run(
        functools.partial(back_kernel, head_size),
        "attend_back",
        flags,
        [
            grad_normed_two,
            other_normed_two,
            far(mixed_far),
            far(grad_final_far),
            far(vectors),
            far(out_weight),
            far(queries),
            far(key_rows),
            far(value_rows),
            far(window),
            segment_column,
            my_segments,
            far(query_weight),
            far(key_weight),
            far(value_weight),
            far(normed_one),
            far(heads_flat),
            far(grad_post),
            far(final_low),
        ],
        [
            model_low,
            (*part, "far"),
            (*part, "far"),
            ((length, model_width), F32, "far"),
            (*post_part, "far"),
            (*post_part, "far"),
            ((local_heads, 2 * length), F32, "far"),
            ((8, model_width), F32, "far"),
        ],
        [
            pltpu.VMEM((length, model_width), BF16),
            pltpu.VMEM((length, head_width), BF16),
            pltpu.VMEM((length, 3 * head_width), BF16),
            pltpu.VMEM((length, length), F32),
            pltpu.VMEM((length, length), BF16),
            pltpu.VMEM((length, length), BF16),
            pltpu.VMEM((LANES, 2 * length), F32),
            pltpu.VMEM((LANES, model_width), F32),
        ],
        mebibytes=32,
    )
    other_normed_one = swap_cores(grad_normed_one)
    early.add(0, True)
    links.flush("phase_a")
    early.kept = [far(kept) for kept in early.kept]
    early.scatter(1)
    late_rows = LANES + feat_width // 4
    late_second_sent, late_second_kept, feature_back, terms = links.run(
        input_kernel,
        "input_back",
        flags,
        [
            grad_normed_one,
            other_normed_one,
            far(embedded_far),
            far(grad_mixed),
            far(vectors),
            far(speech_weight),
            far(inputs),
            far(post_sent),
            far(post_kept),
            far(loss_sums),
            far(back_sums),
            far(grad_offsets),
            far(bucket_line),
        ],
        [
            ((late_rows + 2 * SMALL_ROWS, model_width), BF16, "far"),
            ((late_rows, model_width), BF16),
            ((length, feat_width // cores), BF16, "far"),
            ((SMALL_ROWS, model_width), F32),
        ],
        [
            pltpu.VMEM((length, model_width), BF16),
            pltpu.VMEM((LANES, model_width), F32),
        ],
        mebibytes=18,
    )
    late = Wave(
        links, "late", [late_sent, late_second_sent], [far(late_kept), late_second_kept], terms
    )
    feature_half = lax.all_to_all(
        feature_back.reshape(devices, part_len, feat_width // cores),
        "dp",
        split_axis=0,
        concat_axis=0,
        tiled=True,
    )
    early.add(1, True)
    links.flush("phase_b")
    early.scatter(2)
    early.join_whole()
    links.flush("phase_c", (feature_half,))
    early.exchange_whole()
    *late.sent, early.joint = lax.optimization_barrier((*late.sent, early.joint))
    late.scatter(0)
    late.add(0)
    links.flush("phase_d")
    late.scatter(1)
    feature_half = feature_half.reshape(rows_speech, 2, part_len, feat_width // cores)[:, 0]
    other_feature = swap_cores(feature_half)
    feature_grad = jnp.concatenate(
        [
            jnp.where(core == 0, feature_half, other_feature),
            jnp.where(core == 0, other_feature, feature_half),
        ],
        axis=2,
    )
    early.finish_whole()
    late.add(1)
    links.flush("phase_e", (feature_grad,))
    early.sum_others_whole()
    early.gather(2)
    late.scatter(2)
    early.place(2)
    late.join()
    links.flush("phase_f")
    early.gather(1)
    late.scatter_joint()
    early.place(1)
    late.finish()
    links.flush("phase_g")
    late.sum_others()
    early.gather(0)
    late.gather_joint()
    late.part()
    line_out = ((model_width,), F32)
    small = []
    links.later(
        functools.partial(small_kernel, rows_total),
        [],
        [late.terms],
        [((1, 1), F32), ((mel_width,), F32), ((vocab_size,), F32)]
        + [line_out] * 6
        + [((units,), F32), ((local_heads, buckets), F32)],
        small.extend,
    )
    links.flush("phase_h")
    late.gather(2)
    late.place(2)
    links.flush("phase_h2", [early.came[1]])
    late.gather(1)
    late.place(1)
    links.flush("phase_i", early.came)
    late.gather(0)

    place_flags = jnp.stack(
        [links.mine(step_directions(0, 0)), links.mine(step_directions(1, 0)), core]
    ).astype(jnp.int32)
    grad_down, grad_up = links.run(
        early_place_kernel,
        "early_place",
        place_flags,
        [early.shares[0], early.came[0], early.shares[1], far(early.came[1])],
        [((units, model_width), F32), ((model_width, units), F32)],
        mebibytes=20,
    )
    early_end = links.token
    grad_query, grad_key, grad_value, grad_out = place_late(
        links, place_flags[:1], late.shares[0], None, head_width, after=(early_end,)
    )
    shared_own, shared_came, _ = lax.optimization_barrier(
        (late.shares[1], late.came[1], early_end)
    )
    shared_own_other, shared_came_other = swap_cores(shared_own), swap_cores(shared_came)
    grad_speech_weight, grad_token_table, grad_mel_weight, grad_vocab_weight = links.run(
        shared_place_kernel,
        "shared_place",
        place_flags,
        [shared_own, shared_own_other, shared_came, shared_came_other],
        [
            ((feat_width, model_width), F32),
            ((vocab_size, model_width), F32),
            ((mel_width, model_width), F32),
            ((vocab_size, model_width), F32),
        ],
        [pltpu.VMEM((2 * LANES, model_width), F32), pltpu.VMEM((LANES, model_width), F32)],
        after=(far(grad_query),),
    )
    grad_query, grad_key, grad_value, grad_out = place_late(
        links,
        1 - place_flags[:1],
        late.came[0],
        (grad_query, grad_key, grad_value, grad_out),
        head_width,
    )
    grad_mel_weight, grad_vocab_weight = grad_mel_weight.T, grad_vocab_weight.T
    (
        loss_total,
        grad_mel_bias,
        grad_vocab_bias,
        grad_down_bias,
        grad_second_gain,
        grad_second_shift,
        grad_first_gain,
        grad_first_shift,
        grad_speech_bias,
        grad_up_bias,
        grad_table,
    ) = small
    return (
        loss_total.reshape(()),
        feature_grad,
        grad_speech_weight,
        grad_speech_bias,
        grad_token_table,
        grad_first_gain,
        grad_first_shift,
        grad_query,
        grad_key,
        grad_value,
        grad_table.T,
        grad_out,
        grad_second_gain,
        grad_second_shift,
        grad_up,
        grad_up_bias,
        grad_down,
        grad_down_bias,
        grad_mel_weight,
        grad_mel_bias,
        grad_vocab_weight,
        grad_vocab_bias,
    )


def solution(mesh):
    placed = (
        P(None, "dp", None),
        P(None, "dp"),
        P(None, "dp", None),
        P(None, "dp"),
        P(),
        P(),
        P(),
        P(),
        P(),
        P(),
        P(),
        P(),
        P(None, "mp"),
        P(None, "mp"),
        P(None, "mp"),
        P(None, "mp"),
        P("mp", None),
        P(),
        P(),
        P(None, "mp"),
        P("mp"),
        P("mp", None),
        P(),
        P(),
        P(),
        P(),
        P(),
    )
    return jax.shard_map(
        per_device,
        mesh=mesh,
        in_specs=placed,
        out_specs=(
            P(),
            P(None, "dp", None),
            P(),
            P(),
            P(),
            P(),
            P(),
            P(None, "mp"),
            P(None, "mp"),
            P(None, "mp"),
            P(None, "mp"),
            P("mp", None),
            P(),
            P(),
            P(None, "mp"),
            P("mp"),
            P("mp", None),
            P(),
            P(),
            P(),
            P(),
            P(),
        ),
        check_vma=False,
    )
```
